32 devices in a mesh: dp: 2 (over x), fsdp: 16 (over z, y, core).
Axes of the slice: x: 2, y: 2, z: 4, core: 2. Of those that a mesh axis runs over, the one named last changes fastest.
Arguments:
- tokens: bfloat16 [16384, 1024], P(('dp', 'fsdp')), may hold values from -6 to 6
- cotangent: bfloat16 [16384, 1024], P(('dp', 'fsdp')), may hold values from -6 to 6
- group_ids: int32 [8], replicated, may hold values from 0 to 7
- loss_weights: int32 [8], replicated, may hold values from 1 to 4
- gain_one: bfloat16 [1024], P(('dp', 'fsdp')), may hold values from 0.5 to 1.5
- w_query: bfloat16 [1024, 1024], P(('dp', 'fsdp')), may hold values from -0.1875 to 0.1875
- w_key: bfloat16 [1024, 512], P(('dp', 'fsdp')), may hold values from -0.1875 to 0.1875
- w_value: bfloat16 [1024, 512], P(('dp', 'fsdp')), may hold values from -0.1875 to 0.1875
- w_gate: bfloat16 [1024, 16], P(('dp', 'fsdp')), may hold values from -0.1875 to 0.1875
- gate_bias: float32 [16], replicated, may hold values from -12 to 0, as said below
- w_out: bfloat16 [1024, 1024], P(('dp', 'fsdp')), may hold values from -0.1875 to 0.1875
- gain_two: bfloat16 [1024], P(('dp', 'fsdp')), may hold values from 0.5 to 1.5
- w_gate_ff: bfloat16 [1024, 2816], P(('dp', 'fsdp')), may hold values from -0.1875 to 0.1875
- w_up: bfloat16 [1024, 2816], P(('dp', 'fsdp')), may hold values from -0.1875 to 0.1875
- w_down: bfloat16 [2816, 1024], P(None, ('dp', 'fsdp')), may hold values from -0.109375 to 0.109375
Outputs:
- output: bfloat16 [16384, 1024], P(('dp', 'fsdp'))
- grad_input: bfloat16 [16384, 1024], P(('dp', 'fsdp'))
- grad_gain_one: float32 [1024], P(('dp', 'fsdp'))
- grad_w_query: float32 [1024, 1024], P(('dp', 'fsdp'))
- grad_w_key: float32 [1024, 512], P(('dp', 'fsdp'))
- grad_w_value: float32 [1024, 512], P(('dp', 'fsdp'))
- grad_w_gate: float32 [1024, 16], P(('dp', 'fsdp'))
- grad_gate_bias: float32 [16], replicated
- grad_w_out: float32 [1024, 1024], P(('dp', 'fsdp'))
- grad_gain_two: float32 [1024], P(('dp', 'fsdp'))
- grad_w_gate_ff: float32 [1024, 2816], P(('dp', 'fsdp'))
- grad_w_up: float32 [1024, 2816], P(('dp', 'fsdp'))
- grad_w_down: float32 [2816, 1024], P(None, ('dp', 'fsdp'))
The draws below stay inside these ranges and needn't reach their ends.
Inputs may be any that keep to these rules, and one draw needn't show every extreme that they name: `gate_bias`: per-head offset of the decay gate's input.
All inputs are finite; a program needn't handle non-finite values.
Results may differ from the reference program's by a relative error of at most 0.035.
Values may be sent and summed in bfloat16 or wider, within the bound.
No kernel may reach another device: no remote copies, remote signals or barrier semaphores. Data moves between devices by JAX's collectives and lax.ppermute only.
A program may use at most 384 MiB of HBM per device.

```python
import math
import jax
import jax.numpy as jnp
import numpy as np
from jax import lax

D = 1024
HEADS = 16
HEAD = 64
KVH = 2
LATENT = 256
FF = 2816
TOK_DEV = 512
GROUPS = 8
SEQ_LEN = 2048
SEQS = 8
TOKENS = 16384


def draw_gate_bias(key, part):
    key = jax.random.fold_in(key, 7)
    first_key = jax.random.fold_in(key, 0)
    spread = jax.random.uniform(first_key, (HEADS,), jnp.float32)
    slowest = jnp.log(0.5 / SEQ_LEN)
    fastest = jnp.log(1.0 / 30.0)
    log_rate = slowest + spread * (fastest - slowest)
    return jnp.log(jnp.expm1(16.0 * jnp.exp(log_rate))) - 0.5


def with_ends(entries, stream_key, least, high):
    longest = entries.shape.index(max(entries.shape))
    spots = []
    for shift in (0, 1):
        where = [jax.random.randint(jax.random.fold_in(stream_key, axis), (), 0, length) for axis, length in enumerate(entries.shape)]
        where[longest] = (where[longest] + shift) % entries.shape[longest]
        spots.append(tuple(where))
    return entries.at[spots[0]].set(least).at[spots[1]].set(high)


def level_of(own_key, shape, shards, least, largest):
    def one(position, shards_of):
        steps = jax.random.uniform(jax.random.fold_in(jax.random.fold_in(own_key, 6), position), (shards_of,), jnp.float32, least / len(shards), largest / len(shards))
        return jnp.repeat(jnp.exp(steps), shape[position] // shards_of).reshape((-1,) + (1,) * (len(shape) - position - 1))

    gain = one(*shards[0])
    for cut in shards[1:]:
        gain = gain * one(*cut)
    return gain


def cumulative_ranks(number_of, skew):
    portions = [(1 << 20) // math.isqrt(grade ** skew) + 1 for grade in range(1, number_of + 1)]
    scale = 1 + sum(portions) // (1 << 30)
    return np.cumsum(np.array([max(1, weight // scale) for weight in portions]))


def skewed_ids(own_key, extent, number_of, slope):
    listing = cumulative_ranks(number_of, slope)
    ticket = jax.random.randint(jax.random.fold_in(own_key, 1), extent, 0, int(listing[number_of - 1]))
    rank = jnp.searchsorted(jnp.asarray(listing, jnp.int32), ticket, side="right")
    return jax.random.permutation(jax.random.fold_in(own_key, 2), number_of)[rank].astype(jnp.int32)


def bell_draw(key, extent, scale, most, shards=(), kind=jnp.bfloat16):
    level = level_of(key, extent, shards, -0.22, 0.18) if shards else 1.0
    values = jax.random.normal(key, extent, jnp.float32) * scale * level
    return jnp.minimum(jnp.maximum(values, -most), most).astype(kind)


def setup_inputs(seed: int = 0) -> dict:
    splits = jax.random.split(jax.random.key(seed), 16)
    tokens = bell_draw(splits[0], (TOKENS, D), 1.0, 6.0, ((0, 32),))
    cotangent = bell_draw(splits[1], (TOKENS, D), 1.0, 6.0, ((0, 32),))
    group_ids = with_ends(skewed_ids(splits[2], (SEQS,), GROUPS, 2), jax.random.fold_in(splits[2], 3), 0, GROUPS - 1).astype(jnp.int32)
    loss_weights = with_ends(jax.random.randint(splits[3], (GROUPS,), 1, 5), jax.random.fold_in(splits[3], 1), 1, 4).astype(jnp.int32)
    gain_one = jnp.clip(1.0 + 0.1 * jax.random.normal(splits[4], (D,), jnp.float32), 0.5, 1.5).astype(jnp.bfloat16)
    w_query = bell_draw(splits[5], (D, HEADS * HEAD), D ** -0.5, 0.1875, ((0, 32),))
    w_key = bell_draw(splits[6], (D, KVH * LATENT), D ** -0.5, 0.1875, ((0, 32),))
    w_value = bell_draw(splits[7], (D, KVH * LATENT), D ** -0.5, 0.1875, ((0, 32),))
    w_gate = bell_draw(splits[8], (D, HEADS), D ** -0.5, 0.1875, ((0, 32),))
    gate_bias = draw_gate_bias(jax.random.fold_in(splits[15], 71), 0)
    w_out = bell_draw(splits[10], (HEADS * HEAD, D), (HEADS * HEAD) ** -0.5, 0.1875, ((0, 32),))
    gain_two = jnp.clip(1.0 + 0.1 * jax.random.normal(splits[11], (D,), jnp.float32), 0.5, 1.5).astype(jnp.bfloat16)
    w_gate_ff = bell_draw(splits[12], (D, FF), D ** -0.5, 0.1875, ((0, 32),))
    w_up = bell_draw(splits[13], (D, FF), D ** -0.5, 0.1875, ((0, 32),))
    w_down = bell_draw(splits[14], (FF, D), FF ** -0.5, 0.109375, ((1, 32),))
    return {"tokens": tokens, "cotangent": cotangent, "group_ids": group_ids, "loss_weights": loss_weights, "gain_one": gain_one, "w_query": w_query, "w_key": w_key, "w_value": w_value, "w_gate": w_gate, "gate_bias": gate_bias, "w_out": w_out, "gain_two": gain_two, "w_gate_ff": w_gate_ff, "w_up": w_up, "w_down": w_down}


epsilon = 1e-05
head_floor = 0.25
ROPE_BASE = 10000.0
GATE_TEMP = 16.0
HIGHEST = lax.Precision.HIGHEST

@jax.custom_vjp
def low(v):
    return lax.optimization_barrier(v.astype(jnp.bfloat16)).astype(jnp.float32)

@jax.custom_vjp
def low_back(v):
    return v

def low_keep(v):
    return (low(v), None)

def low_pass(kept, grad):
    return (grad,)

def back_keep(v):
    return (v, None)

def back_low(kept, grad):
    return (low(grad),)
low.defvjp(low_keep, low_pass)
low_back.defvjp(back_keep, back_low)

def inverse_rms(values, added=epsilon):
    return lax.rsqrt(lax.optimization_barrier(jnp.mean(values * values, axis=-1, keepdims=True)) + added)

def rotate(values, positions):
    half_width = values.shape[-1] // 2
    frequency = ROPE_BASE ** (-jnp.arange(half_width, dtype=jnp.float32) / half_width)
    angles = positions.astype(jnp.float32)[:, None] * frequency[None, :]
    cosine = jnp.cos(angles)[:, None, :]
    sine_part = jnp.sin(angles)[:, None, :]
    leading = values[..., :half_width]
    trailing = values[..., half_width:]
    return jnp.concatenate([leading * cosine - trailing * sine_part, trailing * cosine + leading * sine_part], axis=-1)

def broaden(latent):
    rows_count = latent.shape[0]
    width = latent.shape[2]
    per_group = latent.shape[1] // KVH
    repeats = HEADS // latent.shape[1]
    shaped = latent.reshape(rows_count, KVH, 1, per_group, width)
    return jnp.broadcast_to(shaped, (rows_count, KVH, repeats, per_group, width)).reshape(rows_count, HEADS, width)

def decay_table(cumulative):
    step_count = cumulative.shape[0]
    row_order = jnp.arange(step_count)
    causal = (row_order[:, None] >= row_order[None, :])[None, :, :]
    differences = cumulative.T[:, :, None] - cumulative.T[:, None, :]
    return jnp.where(causal, jnp.exp(jnp.where(causal, differences, 0.0)), 0.0)

def mix_block(carry_state, block_inputs):
    queries, key_heads, value_heads, log_decay = block_inputs
    cumulative = jnp.cumsum(log_decay, axis=0)
    decay_rows = decay_table(cumulative)
    scores = low_back(jnp.einsum('thd,shd->hts', queries, key_heads, precision=HIGHEST))
    weighted = low(scores * decay_rows)
    local_part = jnp.einsum('hts,she->the', weighted, value_heads, precision=HIGHEST)
    growth = jnp.exp(cumulative)
    carried_part = growth[:, :, None] * jnp.einsum('thd,hde->the', queries, carry_state, precision=HIGHEST)
    last_cum = cumulative[-1]
    tail_decay = jnp.exp(last_cum[None, :] - cumulative)
    update = jnp.einsum('shd,she->hde', key_heads * tail_decay[:, :, None], value_heads, precision=HIGHEST)
    new_state = jnp.exp(last_cum)[:, None, None] * carry_state + update
    return (new_state, local_part + carried_part)

def layer(inputs, gain_one, w_query, w_key, w_value, w_gate, gate_bias, w_out, gain_two, w_gate_ff, w_up, w_down):
    length = inputs.shape[0]
    positions = jnp.arange(length)
    slot_count = KVH * (LATENT // HEAD)
    normed_one = low(inputs * inverse_rms(inputs) * gain_one)
    query_pre = low_back(jnp.dot(normed_one, w_query, precision=HIGHEST))
    key_pre = low_back(jnp.dot(normed_one, w_key, precision=HIGHEST))
    value_pre = low_back(jnp.dot(normed_one, w_value, precision=HIGHEST))
    gate_pre = low_back(jnp.dot(normed_one, w_gate, precision=HIGHEST))
    queries = low(rotate(query_pre.reshape(length, HEADS, HEAD), positions) * float(HEAD) ** (-0.5))
    key_heads = broaden(low(rotate(key_pre.reshape(length, slot_count, HEAD), positions)))
    value_heads = broaden(low(value_pre).reshape(length, slot_count, HEAD))
    log_decay = -jax.nn.softplus(gate_pre + gate_bias[None, :]) / GATE_TEMP
    block_count = length // TOK_DEV

    def split_rows(whole_array):
        return whole_array.reshape((block_count, TOK_DEV) + whole_array.shape[1:])
    initial = jnp.zeros((HEADS, HEAD, HEAD), jnp.float32)
    final_state, mixed_out = lax.scan(jax.checkpoint(mix_block), initial, (split_rows(queries), split_rows(key_heads), split_rows(value_heads), split_rows(log_decay)))
    mixed_out = low_back(mixed_out.reshape(length, HEADS, HEAD))
    head_normed = low(mixed_out * inverse_rms(mixed_out, head_floor))
    attention = low_back(jnp.dot(head_normed.reshape(length, HEADS * HEAD), w_out, precision=HIGHEST))
    middle = inputs + attention
    normed_two = low(middle * inverse_rms(middle) * gain_two)
    gate_ff = low_back(jnp.dot(normed_two, w_gate_ff, precision=HIGHEST))
    up_ff = low_back(jnp.dot(normed_two, w_up, precision=HIGHEST))
    hidden = low(jax.nn.silu(gate_ff) * up_ff)
    return middle + low_back(jnp.dot(hidden, w_down, precision=HIGHEST))

def sequence_weights(group_ids, loss_weights):
    group_count = loss_weights.shape[0]
    member = (group_ids[:, None] == jnp.arange(group_count, dtype=jnp.int32)[None, :]).astype(jnp.float32)
    counts = lax.optimization_barrier(jnp.sum(member, axis=0))
    raw_weight = lax.optimization_barrier(jnp.sum(member * loss_weights.astype(jnp.float32)[None, :], axis=1)) / lax.optimization_barrier(jnp.sum(member * counts[None, :], axis=1))
    return raw_weight * (group_ids.shape[0] / jnp.sum(raw_weight))

def reference(tokens, cotangent, group_ids, loss_weights, gain_one, w_query, w_key, w_value, w_gate, gate_bias, w_out, gain_two, w_gate_ff, w_up, w_down):
    params = tuple((weight.astype(jnp.float32) for weight in (gain_one, w_query, w_key, w_value, w_gate, gate_bias, w_out, gain_two, w_gate_ff, w_up, w_down)))
    seq_scale = sequence_weights(group_ids, loss_weights)
    seq_count = group_ids.shape[0]
    inputs = tokens.astype(jnp.float32).reshape(seq_count, SEQ_LEN, D)
    cot_rows = cotangent.astype(jnp.float32).reshape(seq_count, SEQ_LEN, D) * seq_scale[:, None, None]

    def one_sequence(running, sequence_item):
        rows_in, rows_cot = sequence_item
        result, pullback = jax.vjp(layer, rows_in, *params)
        gradients = pullback(rows_cot)
        running = tuple((total_part + gradient for total_part, gradient in zip(running, gradients[1:])))
        return (running, (result.astype(jnp.bfloat16), gradients[0].astype(jnp.bfloat16)))
    zeros_init = tuple((jnp.zeros_like(parameter) for parameter in params))
    totals, (outputs, grad_rows) = lax.scan(one_sequence, zeros_init, (inputs, cot_rows))
    return (outputs.reshape(seq_count * SEQ_LEN, D), grad_rows.reshape(seq_count * SEQ_LEN, D), totals[0], totals[1], totals[2], totals[3], totals[4], totals[5], totals[6], totals[7], totals[8], totals[9], totals[10])
```

```python
import jax
import jax.numpy as jnp
from jax import lax
from jax.sharding import Mesh, PartitionSpec as P

HEADS = 16
HEAD = 64
KVH = 2
LATENT = 256
SPAN = 4

epsilon = 1e-05
head_floor = 0.25
ROPE_BASE = 10000.0
GATE_TEMP = 16.0
HIGHEST = lax.Precision.HIGHEST

CHIPS = ("dp", "hi", "mid")
ALL = ("dp", "hi", "mid", "core")
F32 = jnp.float32
BF16 = jnp.bfloat16


def swap(v, axis):
    return lax.ppermute(v, axis, [(0, 1), (1, 0)])


def place(bit, mine, theirs):
    return jnp.where(
        bit == 0, jnp.concatenate([mine, theirs], 0), jnp.concatenate([theirs, mine], 0)
    )


def square_gather(part):
    half = part.shape[0] // 2
    over_dp, over_mid = swap(part, "dp"), swap(part, "mid")
    first = swap(over_dp[:half], "mid")
    second = swap(over_mid[half:], "dp")
    diagonal = jnp.concatenate([first, second], 0)
    dp, mid = lax.axis_index("dp"), lax.axis_index("mid")
    near = place(mid, part[None], over_mid[None])
    far = place(mid, over_dp[None], diagonal[None])
    return place(dp, near[None], far[None])


def hi_gather(part, by_permutes):
    if not by_permutes:
        return lax.all_gather(part, "hi")
    hi = lax.axis_index("hi")
    other = lax.ppermute(part, "hi", [(i, i ^ 2) for i in range(4)])
    pair = place(hi // 2, part[None], other[None])
    opposite = lax.ppermute(pair, "hi", [(i, i ^ 1) for i in range(4)])
    both = jnp.where(
        hi % 2 == 0, jnp.stack([pair, opposite], 1), jnp.stack([opposite, pair], 1)
    )
    return both.reshape((4,) + part.shape)


def gather(part, how):
    rows, width = part.shape
    if how == "whole" or lax.axis_size("dp") != 2 or lax.axis_size("hi") != 4:
        return lax.all_gather(part, CHIPS, axis=0, tiled=True)
    stacked = hi_gather(part, how == "permutes")
    square = square_gather(stacked)
    return square.transpose(0, 2, 1, 3, 4).reshape(-1, width)


def square_scatter(parts):
    dp, mid = lax.axis_index("dp"), lax.axis_index("mid")
    half = parts.shape[2] // 2

    def at(a, b):
        piece = lax.dynamic_index_in_dim(parts, a, 0, keepdims=False)
        return lax.dynamic_index_in_dim(piece, b, 0, keepdims=False)

    own, over_dp = at(dp, mid), at(1 - dp, mid)
    over_mid, diagonal = at(dp, 1 - mid), at(1 - dp, 1 - mid)
    to_mid = swap(diagonal[:half], "dp")
    to_dp = swap(diagonal[half:], "mid")
    send_mid = jnp.concatenate([over_mid[:half] + to_mid, over_mid[half:]], 0)
    send_dp = jnp.concatenate([over_dp[:half], over_dp[half:] + to_dp], 0)
    return own.astype(F32) + swap(send_dp, "dp").astype(F32) + swap(send_mid, "mid").astype(F32)


def scatter(whole, how):
    rows, width = whole.shape
    chips = lax.axis_size(CHIPS)
    if how == "whole" or lax.axis_size("dp") != 2 or lax.axis_size("hi") != 4:
        return lax.psum_scatter(whole.astype(BF16), CHIPS, scatter_dimension=0, tiled=True)
    parts = whole.astype(BF16).reshape(2, 4, 2, rows // chips, width).transpose(0, 2, 1, 3, 4)
    stacked = square_scatter(parts)
    if how == "permutes":
        hi = lax.axis_index("hi")
        stacked = stacked.reshape(2, 2, rows // chips, width)
        mine = lax.dynamic_index_in_dim(stacked, hi % 2, 1, keepdims=False)
        theirs = lax.dynamic_index_in_dim(stacked, 1 - hi % 2, 1, keepdims=False)
        pair = mine + lax.ppermute(
            theirs.astype(BF16), "hi", [(i, i ^ 1) for i in range(4)]
        ).astype(F32)
        mine = lax.dynamic_index_in_dim(pair, hi // 2, 0, keepdims=False)
        theirs = lax.dynamic_index_in_dim(pair, 1 - hi // 2, 0, keepdims=False)
        return mine + lax.ppermute(
            theirs.astype(BF16), "hi", [(i, i ^ 2) for i in range(4)]
        ).astype(F32)
    return lax.psum_scatter(stacked.astype(BF16), "hi", scatter_dimension=0, tiled=False)


def to_owner(rows, core):
    count = rows.shape[0] // 2
    rows = rows.astype(BF16).reshape(2, count, rows.shape[1])
    mine = lax.dynamic_index_in_dim(rows, core, 0, keepdims=False)
    theirs = lax.dynamic_index_in_dim(rows, 1 - core, 0, keepdims=False)
    return mine, swap(theirs, "core")


def beside(core, mine, theirs):
    return jnp.where(
        core == 0, jnp.concatenate([mine, theirs], 1), jnp.concatenate([theirs, mine], 1)
    ).astype(F32)


def inverse_rms(values, added=epsilon):
    return lax.rsqrt(jnp.mean(values * values, axis=-1, keepdims=True) + added)


def norm_back(grad_unit, unit_rows, scale_rows):
    return scale_rows * (
        grad_unit - unit_rows * jnp.mean(grad_unit * unit_rows, axis=-1, keepdims=True)
    )


def rope_tables(positions):
    half_width = HEAD // 2
    frequency = ROPE_BASE ** (-jnp.arange(half_width, dtype=F32) / half_width)
    angles = positions.astype(F32)[..., None] * frequency
    return jnp.cos(angles)[..., None, :], jnp.sin(angles)[..., None, :]


def rotate(values, cosine, sine_part):
    half_width = values.shape[-1] // 2
    leading = values[..., :half_width]
    trailing = values[..., half_width:]
    return jnp.concatenate(
        [leading * cosine - trailing * sine_part, trailing * cosine + leading * sine_part], axis=-1
    )


def matmul(left, right):
    return jnp.dot(left, right, preferred_element_type=F32)


def contract_rows(left, right):
    return jnp.einsum("ta,tb->ab", left, right, preferred_element_type=F32)


def against(left, right):
    return jnp.einsum("tb,ab->ta", left, right, preferred_element_type=F32)


def sequence_weights(group_ids, loss_weights):
    group_count = loss_weights.shape[0]
    member = (group_ids[:, None] == jnp.arange(group_count, dtype=jnp.int32)[None, :]).astype(F32)
    counts = jnp.sum(member, axis=0)
    raw_weight = jnp.sum(member * loss_weights.astype(F32)[None, :], axis=1) / jnp.sum(
        member * counts[None, :], axis=1
    )
    return raw_weight * (group_ids.shape[0] / jnp.sum(raw_weight))


def broaden(latent):
    return jnp.concatenate([latent, latent], axis=-2)


def narrow(gradient):
    slots = gradient.shape[-2] // 2
    return gradient[..., :slots, :] + gradient[..., slots:, :]


def decay_table(cumulative):
    count = cumulative.shape[1]
    order = jnp.arange(count)
    causal = order[:, None] >= order[None, :]
    rows = cumulative.transpose(0, 2, 1)
    differences = rows[:, :, :, None] - rows[:, :, None, :]
    return jnp.where(causal, jnp.exp(jnp.where(causal, differences, 0.0)), 0.0)


AG = dict(front="permutes", out="permutes", ff="hi", down="hi")
RS = dict(front="permutes", out="hi", gate="hi", up="hi", down="hi")


def shards(
    tokens,
    cotangent,
    group_ids,
    loss_weights,
    gain_one,
    w_query,
    w_key,
    w_value,
    w_gate,
    gate_bias,
    w_out,
    gain_two,
    w_gate_ff,
    w_up,
    w_down,
):
    count, width = tokens.shape
    local = HEADS // 2
    slots = KVH * (LATENT // HEAD) // 2
    core, mid = lax.axis_index("core"), lax.axis_index("mid")
    sequence = (lax.axis_index(("dp", "hi", "mid", "core"))) // SPAN

    def halves(w):
        half = w.shape[1] // 2
        return w[:, :half], w[:, half:]

    wq, wk, wv = halves(w_query), halves(w_key), halves(w_value)
    wo, wg, wu, wd = halves(w_out), halves(w_gate_ff), halves(w_up), halves(w_down.T)
    wa = halves(w_gate)
    pad = 128 - local - 2

    def packed(i):
        front = [wq[i], wk[i], wv[i], wa[i], gain_one[:, None], gain_two[:, None]]
        front.append(jnp.zeros((gain_one.shape[0], pad), BF16))
        return jnp.concatenate(front + [wo[i], wg[i], wu[i], wd[i]], axis=1)

    first, second = packed(0), packed(1)
    kept = jnp.where(core == 0, first, second)
    sent = jnp.where(core == 0, second, first)
    chip = place(core, kept, swap(sent, "core"))
    n_front = (w_query.shape[1] + w_key.shape[1] + w_value.shape[1]) // 2 + 128
    n_out = w_out.shape[1] // 2
    n_ff = w_up.shape[1] // 2
    other_tokens = swap(tokens, "core")
    other_cotangent = swap(cotangent, "core")
    ends = [n_front, n_front + n_out, n_front + n_out + 2 * n_ff]
    w_front = gather(chip[:, : ends[0]], AG["front"])
    w_out_half = gather(chip[:, ends[0] : ends[1]], AG["out"])
    w_ff = gather(chip[:, ends[1] : ends[2]], AG["ff"])
    w_down_t = gather(chip[:, ends[2] :], AG["down"])
    w_gate_ff, w_up = w_ff[:, :n_ff], w_ff[:, n_ff:]
    w_out_other = swap(w_out_half, "core")
    w_out = jnp.where(
        core == 0,
        jnp.concatenate([w_out_half, w_out_other], 1),
        jnp.concatenate([w_out_other, w_out_half], 1),
    )

    gains = w_front[:, n_front - 128 + local : n_front - 128 + local + 2].T.astype(F32)
    gain_one, gain_two = gains[0], gains[1]
    inputs = jnp.stack([tokens, other_tokens]).astype(F32)
    scale_one = inverse_rms(inputs)
    unit_one = inputs * scale_one
    normed_one = (unit_one * gain_one).astype(BF16).reshape(2 * count, width)
    pre = matmul(normed_one, w_front).reshape(2, count, n_front)
    n_q, n_k = local * HEAD, slots * HEAD
    block = 2 * mid + (core ^ jnp.arange(2))
    positions = block[:, None] * count + jnp.arange(count)[None, :]
    cosine, sine_part = rope_tables(positions)
    queries = (
        rotate(pre[..., :n_q].reshape(2, count, local, HEAD), cosine, sine_part)
        * float(HEAD) ** (-0.5)
    ).astype(BF16)
    keys = rotate(
        pre[..., n_q : n_q + n_k].reshape(2, count, slots, HEAD), cosine, sine_part
    ).astype(BF16)
    values = pre[..., n_q + n_k : n_q + 2 * n_k].reshape(2, count, slots, HEAD).astype(BF16)
    own_bias = lax.dynamic_slice_in_dim(gate_bias, core * local, local)
    gate_in = pre[..., n_q + 2 * n_k : n_q + 2 * n_k + local] + own_bias
    key_heads, value_heads = broaden(keys), broaden(values)
    log_decay = -jax.nn.softplus(gate_in) / GATE_TEMP
    cumulative = jnp.cumsum(log_decay, axis=1)
    decay_rows = decay_table(cumulative)
    scores = jnp.einsum("bthd,bshd->bhts", queries, key_heads, preferred_element_type=F32)
    weighted = (scores * decay_rows).astype(BF16)
    local_part = jnp.einsum("bhts,bshe->bthe", weighted, value_heads, preferred_element_type=F32)
    last_cum = cumulative[:, -1]
    total_decay = jnp.exp(last_cum)
    tail_decay = jnp.exp(last_cum[:, None, :] - cumulative)
    key_scaled = key_heads.astype(F32) * tail_decay[..., None]
    update = jnp.einsum("bshd,bshe->bhde", key_scaled, value_heads.astype(F32), precision=HIGHEST)

    def in_order(v):
        return jnp.where(core == 0, v, v[::-1])

    decay_seq = in_order(total_decay)[:, :, None, None]
    update_seq = in_order(update)
    leaving = decay_seq[1] * update_seq[0] + update_seq[1]
    state_0 = lax.ppermute(leaving.astype(BF16), "mid", [(0, 1)]).astype(F32)
    state_1 = decay_seq[0] * state_0 + update_seq[0]
    state_in = in_order(jnp.stack([state_0, state_1]))
    queries_float = queries.astype(F32)
    growth = jnp.exp(cumulative)
    carried_part = growth[..., None] * jnp.einsum(
        "bthd,bhde->bthe", queries_float, state_in, precision=HIGHEST
    )
    mixed_out = local_part + carried_part
    head_scale = inverse_rms(mixed_out, head_floor)
    head_normed = mixed_out * head_scale
    normed_pair = head_normed.astype(BF16).reshape(2, count, local * HEAD)
    normed_theirs = swap(normed_pair[1], "core")
    normed_flat = jnp.where(
        core == 0,
        jnp.concatenate([normed_pair[0], normed_theirs], 1),
        jnp.concatenate([normed_theirs, normed_pair[0]], 1),
    )
    attention = matmul(normed_flat, w_out)
    middle = inputs[0] + attention
    scale_two = inverse_rms(middle)
    unit_two = middle * scale_two
    normed_two_own = (unit_two * gain_two).astype(BF16)
    normed_two = jnp.concatenate([normed_two_own, swap(normed_two_own, "core")], 0)
    gate_ff = matmul(normed_two, w_gate_ff)
    up_ff = matmul(normed_two, w_up)
    sigmoid_gate = jax.nn.sigmoid(gate_ff)
    silu_gate = gate_ff * sigmoid_gate
    hidden = (silu_gate * up_ff).astype(BF16)
    seq_weights = sequence_weights(group_ids, loss_weights)
    own_weight = jnp.sum(jnp.where(jnp.arange(group_ids.shape[0]) == sequence, seq_weights, 0.0))
    grad_out = cotangent.astype(F32) * own_weight
    grad_branch = jnp.concatenate(
        [grad_out.astype(BF16), (other_cotangent.astype(F32) * own_weight).astype(BF16)], 0
    )
    d_down = scatter(contract_rows(grad_branch, hidden), RS["down"])
    grad_hidden = matmul(grad_branch, w_down_t)
    grad_gate = (
        grad_hidden * up_ff * (sigmoid_gate * (1.0 + gate_ff * (1.0 - sigmoid_gate)))
    ).astype(BF16)
    grad_up = (grad_hidden * silu_gate).astype(BF16)
    d_gate_ff = scatter(contract_rows(normed_two, grad_gate), RS["gate"])
    d_up = scatter(contract_rows(normed_two, grad_up), RS["up"])
    part = against(grad_gate, w_gate_ff) + against(grad_up, w_up)
    grad_normed_two = part[:count] + swap(part[count:].astype(BF16), "core").astype(F32)
    d_gain_two = jnp.sum(grad_normed_two * unit_two, axis=0)
    grad_middle = grad_out + norm_back(grad_normed_two * gain_two, unit_two, scale_two)
    grad_attention = grad_middle.astype(BF16)
    out_part = against(hidden, w_down_t)
    output = middle + (out_part[:count] + swap(out_part[count:].astype(BF16), "core").astype(F32))

    d_out_part = contract_rows(normed_flat, grad_attention)
    d_out_halves = d_out_part[:, :n_out], d_out_part[:, n_out:]
    d_out_kept = jnp.where(core == 0, d_out_halves[0], d_out_halves[1])
    d_out_sent = jnp.where(core == 0, d_out_halves[1], d_out_halves[0]).astype(BF16)
    d_out = scatter(d_out_kept + swap(d_out_sent, "core").astype(F32), RS["out"])
    grad_normed = against(grad_attention, w_out)
    grad_halves = grad_normed[:, : local * HEAD], grad_normed[:, local * HEAD :]
    grad_kept = jnp.where(core == 0, grad_halves[0], grad_halves[1])
    grad_sent = jnp.where(core == 0, grad_halves[1], grad_halves[0]).astype(BF16)
    grad_normed = jnp.stack([grad_kept, swap(grad_sent, "core").astype(F32)])
    grad_normed = grad_normed.reshape(2, count, local, HEAD)
    grad_mixed = norm_back(grad_normed, head_normed, head_scale).astype(BF16)
    grad_mixed_f = grad_mixed.astype(F32)
    through = jnp.einsum(
        "bthd,bthe->bhde", queries_float * growth[..., None], grad_mixed_f, precision=HIGHEST
    )
    through_seq = in_order(through)
    entering = through_seq[0] + decay_seq[0] * through_seq[1]
    later_1 = lax.ppermute(entering.astype(BF16), "mid", [(1, 0)]).astype(F32)
    later_0 = through_seq[1] + decay_seq[1] * later_1
    later_state = in_order(jnp.stack([later_0, later_1]))
    grad_weighted = jnp.einsum(
        "bthe,bshe->bhts", grad_mixed, value_heads, preferred_element_type=F32
    )
    d_values = jnp.einsum("bhts,bthe->bshe", weighted, grad_mixed, preferred_element_type=F32)
    grad_scores = (grad_weighted * decay_rows).astype(BF16)
    d_queries = jnp.einsum("bhts,bshd->bthd", grad_scores, key_heads, preferred_element_type=F32)
    d_keys = jnp.einsum("bhts,bthd->bshd", grad_scores, queries, preferred_element_type=F32)
    spread = grad_weighted * scores * decay_rows
    grad_cum = (jnp.sum(spread, axis=3) - jnp.sum(spread, axis=2)).transpose(0, 2, 1)
    d_queries = d_queries + growth[..., None] * jnp.einsum(
        "bthe,bhde->bthd", grad_mixed_f, state_in, precision=HIGHEST
    )
    grad_cum = grad_cum + jnp.sum(grad_mixed_f * carried_part, axis=3)
    grad_total = jnp.sum(later_state * state_in, axis=(2, 3))
    key_side = jnp.einsum(
        "bshe,bhde->bshd", value_heads.astype(F32), later_state, precision=HIGHEST
    )
    d_keys = d_keys + key_side * tail_decay[..., None]
    d_values = d_values + jnp.einsum(
        "bshd,bhde->bshe", key_scaled, later_state, precision=HIGHEST
    )
    grad_tail = jnp.sum(key_side * key_heads.astype(F32), axis=3) * tail_decay
    grad_cum = grad_cum - grad_tail
    last_row = (jnp.arange(count) == count - 1).astype(F32)[None, :, None]
    grad_cum = grad_cum + last_row * (
        jnp.sum(grad_tail, axis=1) + grad_total * total_decay
    )[:, None, :]
    grad_log = jnp.flip(jnp.cumsum(jnp.flip(grad_cum, 1), axis=1), 1)
    grad_gate_pre_f = -grad_log * jax.nn.sigmoid(gate_in) / GATE_TEMP
    d_bias = jnp.sum(grad_gate_pre_f, axis=(0, 1))
    grad_gate_pre = grad_gate_pre_f.astype(BF16)
    grad_query_pre = (rotate(d_queries, cosine, -sine_part) * float(HEAD) ** (-0.5)).astype(BF16)
    grad_key_pre = rotate(narrow(d_keys), cosine, -sine_part).astype(BF16)
    grad_value_pre = narrow(d_values).astype(BF16)
    grad_front = jnp.concatenate(
        [
            grad_query_pre.reshape(2 * count, n_q),
            grad_key_pre.reshape(2 * count, n_k),
            grad_value_pre.reshape(2 * count, n_k),
            grad_gate_pre.reshape(2 * count, local),
            jnp.zeros((2 * count, 128 - local), BF16),
        ],
        axis=1,
    )
    d_front = contract_rows(normed_one, grad_front)
    part = against(grad_front, w_front)
    d_gain_one = jnp.sum(part * unit_one.reshape(2 * count, width), axis=0)
    d_front = jnp.concatenate(
        [
            d_front[:, : n_front - 128 + local],
            d_gain_one[:, None],
            d_gain_two[:, None],
            jnp.broadcast_to(d_bias[None, :], (width, local)),
            jnp.zeros((width, 128 - 2 * local - 2), F32),
        ],
        axis=1,
    )
    d_front = scatter(d_front, RS["front"])
    grad_normed_one = part[:count] + swap(part[count:].astype(BF16), "core").astype(F32)
    grad_input = grad_middle + norm_back(grad_normed_one * gain_one, unit_one[0], scale_one[0])

    summed = jnp.concatenate(
        [v.astype(BF16) for v in (d_front, d_out, d_gate_ff, d_up, d_down)], axis=1
    )
    mine, theirs = to_owner(summed, core)
    ends = [0, n_q, n_q + n_k, n_q + 2 * n_k]
    g_query = beside(core, mine[:, ends[0] : ends[1]], theirs[:, ends[0] : ends[1]])
    g_key = beside(core, mine[:, ends[1] : ends[2]], theirs[:, ends[1] : ends[2]])
    g_value = beside(core, mine[:, ends[2] : ends[3]], theirs[:, ends[2] : ends[3]])
    at = ends[3]
    g_gate = beside(core, mine[:, at : at + local], theirs[:, at : at + local])
    at = at + local
    g_gains = mine[:, at : at + 2].astype(F32) + theirs[:, at : at + 2].astype(F32)
    at = at + 2
    g_bias = beside(core, mine[:1, at : at + local], theirs[:1, at : at + local])[0]
    ends = [n_front, n_front + n_out, n_front + n_out + n_ff, n_front + n_out + 2 * n_ff]
    ends.append(ends[-1] + n_ff)
    big = [
        beside(core, mine[:, a:b], theirs[:, a:b]) for a, b in zip(ends[:-1], ends[1:])
    ]
    return (
        output.astype(BF16),
        grad_input.astype(BF16),
        g_gains[:, 0],
        g_query,
        g_key,
        g_value,
        g_gate,
        g_bias,
        big[0],
        g_gains[:, 1],
        big[1],
        big[2],
        big[3].T,
    )


def solution(mesh):
    devices = mesh.devices
    fine = Mesh(
        devices.reshape(devices.shape[0], devices.shape[1] // SPAN, SPAN // 2, 2), ALL
    )
    rows, columns, split = P(ALL, None), P(None, ALL), P(ALL)
    in_specs = (rows, rows, P(), P(), split) + (rows,) * 4 + (P(), rows, split, rows, rows, columns)
    out_specs = (rows, rows, split) + (rows,) * 4 + (P(), rows, split, rows, rows, columns)
    return jax.shard_map(shards, mesh=fine, in_specs=in_specs, out_specs=out_specs, check_vma=False)
```

```python
import functools

import jax
import jax.numpy as jnp
from jax import lax
from jax.experimental import pallas as pl
from jax.experimental.pallas import tpu as pltpu
from jax.sharding import Mesh, PartitionSpec as P

HEADS = 16
HEAD = 64
KVH = 2
LATENT = 256
SPAN = 4

epsilon = 1e-05
head_floor = 0.25
ROPE_BASE = 10000.0
GATE_TEMP = 16.0

CHIPS = ("dp", "hi", "mid")
ALL = ("dp", "hi", "mid", "core")
F32 = jnp.float32
BF16 = jnp.bfloat16


def swap(v, axis):
    return lax.ppermute(v, axis, [(0, 1), (1, 0)])


def place(bit, mine, theirs):
    return jnp.where(
        bit == 0, jnp.concatenate([mine, theirs], 0), jnp.concatenate([theirs, mine], 0)
    )


def small_slice():
    return lax.axis_size("dp") == 2 and lax.axis_size("hi") == 4


def gather(part):
    return lax.all_gather(part, CHIPS, axis=0, tiled=True)


def add3(a, b, c):
    return a.astype(F32) + b.astype(F32) + c.astype(F32)


def scatter(whole):
    return lax.psum_scatter(whole, CHIPS, scatter_dimension=0, tiled=True)


def beside(core, mine, theirs):
    return jnp.where(
        core == 0, jnp.concatenate([mine, theirs], 1), jnp.concatenate([theirs, mine], 1)
    ).astype(F32)


HALF = HEADS // 2
PAIRS = HALF // 2
WIDE = 2 * HEAD
N_Q = HALF * HEAD
N_K = N_Q // 2
N_FRONT = N_Q + 2 * N_K + WIDE
FLOPS = 0.55e9


def dot(left, right):
    return jnp.dot(left, right, preferred_element_type=F32)


def dot_t(left, right):
    return lax.dot_general(left, right, (((1,), (1,)), ((), ())), preferred_element_type=F32)


def t_dot(left, right):
    return lax.dot_general(left, right, (((0,), (0,)), ((), ())), preferred_element_type=F32)


def thirds(v):
    high = v.astype(BF16)
    rest = v - high.astype(F32)
    middle = rest.astype(BF16)
    return high, middle, (rest - middle.astype(F32)).astype(BF16)


def iota(shape, axis):
    return lax.broadcasted_iota(jnp.int32, shape, axis)


def spread_pair(per_head, p):
    lane = iota((1, WIDE), 1)
    return jnp.where(
        lane < HEAD, per_head[:, 2 * p : 2 * p + 1], per_head[:, 2 * p + 1 : 2 * p + 2]
    )


def head_sums(v):
    lane = iota((1, WIDE), 1)
    low = jnp.sum(jnp.where(lane < HEAD, v, 0.0), axis=1, keepdims=True)
    high = jnp.sum(jnp.where(lane < HEAD, 0.0, v), axis=1, keepdims=True)
    return jnp.where(lane < HEAD, low, high)


def turn(v, cosine, sine_part):
    lane = iota((1, WIDE), 1)
    other = jnp.where(
        lane % HEAD < HEAD // 2,
        pltpu.roll(v, WIDE - HEAD // 2, 1),
        pltpu.roll(v, HEAD // 2, 1),
    )
    return v * cosine + other * sine_part


def own_blocks():
    return (iota((WIDE, WIDE), 0) < HEAD) == (iota((WIDE, WIDE), 1) < HEAD)


def q_cols(p):
    return slice(WIDE * p, WIDE * (p + 1))


def k_cols(p):
    return slice(N_Q + WIDE * (p % 2), N_Q + WIDE * (p % 2 + 1))


def v_cols(p):
    return slice(N_Q + N_K + WIDE * (p % 2), N_Q + N_K + WIDE * (p % 2 + 1))


def without(kernel, start, count):
    return lambda *refs: kernel(*refs[:start], *refs[start + count :])


ANYWHERE = pl.BlockSpec(memory_space=pl.ANY)
SCALARS = pl.BlockSpec(memory_space=pltpu.SMEM)


def inverse_rms(values, added=epsilon):
    return lax.rsqrt(jnp.mean(values * values, axis=-1, keepdims=True) + added)


def norm_back(grad_unit, unit_rows, scale_rows):
    return scale_rows * (
        grad_unit - unit_rows * jnp.mean(grad_unit * unit_rows, axis=-1, keepdims=True)
    )


def row_of(where, i, b, rows):
    hi = where[2] ^ (0, 2, 1, 3)[i]
    index = ((where[1] ^ b[0]) * 4 + hi) * 2 + (where[3] ^ b[1])
    return pl.multiple_of(index * rows, rows)


def pack_kernel(core_ref, q_ref, k_ref, v_ref, a_ref, g1_ref, g2_ref, o_ref, f_ref, u_ref, d_ref, *outs):
    def put(out, at, v):
        out[:, at : at + v.shape[1]] = v
        return at + v.shape[1]

    rows = q_ref.shape[0]
    lane = iota((1, WIDE), 1)
    gates = a_ref[...].astype(F32)
    gains = [g1_ref[...].astype(F32), g2_ref[...].astype(F32)]
    for i in range(2):
        front, rest = outs[2 * i : 2 * i + 2]
        mine = core_ref[0] if i == 0 else 1 - core_ref[0]

        def half(ref):
            n = ref.shape[1] // 2
            return jnp.where(mine == 0, ref[:, :n], ref[:, n:])

        at = put(front, 0, half(q_ref))
        at = put(front, at, half(k_ref))
        at = put(front, at, half(v_ref))
        some = jnp.where(mine == 0, gates[:HALF], gates[HALF:])
        small = jnp.concatenate([some, *gains, jnp.zeros((WIDE - HALF - 2, rows), F32)], 0)
        at = put(front, at, small.T.astype(BF16))
        put(front, at, half(o_ref))
        at = put(rest, 0, half(f_ref))
        at = put(rest, at, half(u_ref))
        put(rest, at, half(d_ref))


def pack(core, *weights):
    rows = weights[0].shape[0]
    n_out, n_ff = weights[6].shape[1] // 2, weights[7].shape[1] // 2
    return pl.pallas_call(
        pack_kernel,
        in_specs=[pl.BlockSpec(memory_space=pltpu.SMEM)]
        + [pl.BlockSpec(memory_space=pltpu.VMEM)] * len(weights),
        out_specs=[pl.BlockSpec(memory_space=pltpu.VMEM)] * 4,
        out_shape=[
            jax.ShapeDtypeStruct((rows, n), BF16) for n in (N_FRONT + n_out, 3 * n_ff)
        ]
        * 2,
        name="pack",
    )(core.reshape(1).astype(jnp.int32), *weights)


def front_kernel(
    core_ref, own_ref, other_ref, bias_ref, cos_ref, sin_ref, *refs
):
    *pieces, w_ref, out_ref = refs[:-9]
    normed_ref, qkv_ref, c_ref, ct_ref, z_ref, gains_ref, u_ref, leave_ref, first_u = refs[-9:]
    step = pl.program_id(0)
    slot = step ^ core_ref[0]

    @pl.when(step == 0)
    def _():
        if len(pieces) == 1:
            w_ref[...] = pieces[0][:, :N_FRONT]
            out_ref[...] = pieces[0][:, N_FRONT:]
        else:
            own, over_dp, over_mid, first, second = pieces
            rows = own.shape[1]
            for i in range(4):
                far = first[i] if i < 2 else second[i - 2]
                for v, b in ((own[i], (0, 0)), (over_dp[i], (1, 0)), (over_mid[i], (0, 1)), (far, (1, 1))):
                    to = pl.ds(row_of(core_ref, i, b, rows), rows)
                    w_ref[to, :] = v[:, :N_FRONT]
                    out_ref[to, :] = v[:, N_FRONT:]

    x = jnp.where(slot == 0, own_ref[...], other_ref[...]).astype(F32)
    gains = w_ref[:, N_FRONT - WIDE :].astype(F32).T[HALF : HALF + 8]
    gains_ref[...] = gains
    scale = lax.rsqrt(jnp.mean(x * x, axis=-1, keepdims=True) + epsilon)
    normed = (x * scale * gains[:1]).astype(BF16)
    normed_ref[...] = normed
    pre = dot(normed, w_ref[...])
    cosine, sine_part = cos_ref[...], sin_ref[...]
    for p in range(PAIRS):
        turned = turn(pre[:, q_cols(p)], cosine, sine_part)
        qkv_ref[:, q_cols(p)] = (turned * float(HEAD) ** (-0.5)).astype(BF16)
    for p in range(PAIRS // 2):
        qkv_ref[:, k_cols(p)] = turn(pre[:, k_cols(p)], cosine, sine_part).astype(BF16)
        qkv_ref[:, v_cols(p)] = pre[:, v_cols(p)].astype(BF16)
    z = pre[:, N_FRONT - WIDE :] + bias_ref[...]
    z_ref[...] = z
    small = jnp.exp(-jnp.abs(z))
    log_part = jnp.where(
        small < 0.01, small * (1.0 - small * (0.5 - small * (1.0 / 3.0))), jnp.log(1.0 + small)
    )
    softplus = jnp.maximum(z, 0.0) + log_part
    log_decay = jnp.where(iota((1, WIDE), 1) < HALF, -softplus / GATE_TEMP, 0.0)
    count = x.shape[0]
    lower = (iota((count, count), 0) >= iota((count, count), 1)).astype(BF16)
    c = sum(dot(lower, third) for third in thirds(log_decay))
    c_ref[...] = c
    ct_ref[...] = c.T[:HALF]
    last = c[count - 1 :]
    tail = jnp.exp(last - c)
    mask = own_blocks()
    for p in range(PAIRS):
        scaled = (qkv_ref[:, k_cols(p)].astype(F32) * spread_pair(tail, p)).astype(BF16)
        update = jnp.where(mask, t_dot(scaled, qkv_ref[:, v_cols(p)]), 0.0)

        @pl.when(step == 0)
        def _():
            u_ref[p] = update
            first_u[p] = update

        @pl.when(step == 1)
        def _():
            grown = spread_pair(jnp.exp(last), p) * first_u[p] + update
            leave_ref[p] = grown.astype(BF16)


def tile_of(qkv_ref, c, ct, r, rows, p, h):
    lane = iota((1, WIDE), 1)
    mine = (lane < HEAD) if h == 0 else (lane >= HEAD)
    span = slice(rows * r, rows * (r + 1))
    upto = rows * (r + 1)
    query = jnp.where(mine, qkv_ref[span, q_cols(p)], 0)
    scores = dot_t(query, qkv_ref[:upto, k_cols(p)])
    head = 2 * p + h
    differences = c[span, head : head + 1] - ct[head : head + 1, :upto]
    causal = iota((rows, upto), 0) + rows * r >= iota((rows, upto), 1)
    decays = jnp.exp(jnp.where(causal, differences, -1e30))
    return mine, span, upto, scores, decays


def mix_kernel(
    core_ref, qkv_ref, c_ref, ct_ref, s0_ref, u_ref,
    mixed_ref, own_ref, sent_ref, s1_ref, state,
):
    step = pl.program_id(0)
    slot = step ^ core_ref[0]
    count = c_ref.shape[0]
    rows = count // 2
    lane = iota((1, WIDE), 1)
    c, ct = c_ref[...], ct_ref[...]

    @pl.when(step == 0)
    def _():
        state[...] = s0_ref[...].astype(F32)

    growth = jnp.exp(c)
    for p in range(PAIRS):
        held = state[p]
        carried = spread_pair(growth, p) * dot(qkv_ref[:, q_cols(p)], held.astype(BF16))
        for r in range(2):
            parts = []
            for h in range(2):
                mine, span, upto, scores, decays = tile_of(qkv_ref, c, ct, r, rows, p, h)
                weighted = (scores * decays).astype(BF16)
                parts.append(dot(weighted, qkv_ref[:upto, v_cols(p)]))
            mixed = jnp.where(lane < HEAD, parts[0], parts[1]) + carried[span]
            mixed_ref[span, q_cols(p)] = mixed
            scale = lax.rsqrt(head_sums(mixed * mixed) * (1.0 / HEAD) + head_floor)
            normed = (mixed * scale).astype(BF16)

            @pl.when(slot == 0)
            def _():
                own_ref[span, q_cols(p)] = normed

            @pl.when(slot == 1)
            def _():
                sent_ref[span, q_cols(p)] = normed

        @pl.when(step == 0)
        def _():
            grown = spread_pair(growth[count - 1 :], p) * held + u_ref[p]
            s1_ref[p] = grown
            state[p] = grown


def out_kernel(
    core_ref, own_ref, got_ref, half_ref, other_ref, x_ref, gains_ref, middle_ref, normed_ref
):
    core = core_ref[0]
    n = own_ref.shape[1]
    mine = pl.ds(pl.multiple_of(core * n, n), n)
    theirs = pl.ds(pl.multiple_of((1 - core) * n, n), n)
    own, got = own_ref[...], got_ref[...]
    a = dot(own, half_ref[mine, :]) + dot(got, half_ref[theirs, :])
    b = dot(own, other_ref[mine, :]) + dot(got, other_ref[theirs, :])
    attention = jnp.where(core == 0, jnp.concatenate([a, b], 1), jnp.concatenate([b, a], 1))
    middle = x_ref[...].astype(F32) + attention
    middle_ref[...] = middle
    normed_ref[...] = (middle * inverse_rms(middle) * gains_ref[1:2]).astype(BF16)


def permuted(v, back=False):
    n = v.shape[1] // 8
    order = [4 * (j % 2) + j // 2 for j in range(8)]
    if back:
        order = [2 * (j % 4) + j // 4 for j in range(8)]
    return jnp.concatenate([v[:, n * j : n * (j + 1)] for j in order], 1)


def ff_kernel(
    small, where_ref, weight_ref, own_ref, other_ref, cot_ref, cot_other_ref, gate_ref, up_ref,
    hidden_ref, slopes_ref, x_ref, branch_ref,
):
    first = pl.program_id(0) == 0
    x = jnp.where(first, own_ref[...], other_ref[...])
    x_ref[...] = x
    cot = jnp.where(first, cot_ref[...], cot_other_ref[...]).astype(F32)
    branch = (cot * weight_ref[0]).astype(BF16)
    branch_ref[...] = permuted(branch) if small else branch
    gate = dot(x, gate_ref[...])
    up = dot(x, up_ref[...])
    n = gate.shape[1]
    sigmoid = 1.0 / (1.0 + jnp.exp(-gate))
    silu = gate * sigmoid
    hidden_ref[...] = (silu * up).astype(BF16)
    slopes_ref[:, :n] = (up * (sigmoid * (1.0 + gate * (1.0 - sigmoid)))).astype(BF16)
    slopes_ref[:, n:] = silu.astype(BF16)


def ff_back_kernel(small, where_ref, g_ref, w_ref, slopes_ref, grad_ref):
    branch = permuted(g_ref[...], True) if small else g_ref[...]
    grad = dot(branch, w_ref[...])
    n = grad.shape[1]
    grad_ref[:, :n] = (grad * slopes_ref[:, :n].astype(F32)).astype(BF16)
    grad_ref[:, n:] = (grad * slopes_ref[:, n:].astype(F32)).astype(BF16)


def part_kernel(grad_ref, gate_ref, up_ref, part_ref):
    n = gate_ref.shape[1]
    part = dot_t(grad_ref[:, :n], gate_ref[...]) + dot_t(grad_ref[:, n:], up_ref[...])
    part_ref[...] = part.astype(part_ref.dtype)


def middle_kernel(
    core_ref, weight_ref, grad_ref, gate_ref, up_ref, got_ref, cot_ref, middle_ref, gains_ref,
    half_ref, other_ref, grad_middle_ref, attention_ref, gain_ref, own_ref, sent_ref,
):
    core = core_ref[0]
    n = gate_ref.shape[1]
    part = dot_t(grad_ref[:, :n], gate_ref[...]) + dot_t(grad_ref[:, n:], up_ref[...])
    part = part + got_ref[...].astype(F32)
    middle = middle_ref[...]
    scale = inverse_rms(middle)
    unit = middle * scale
    gain_ref[...] = jnp.broadcast_to(jnp.sum(part * unit, axis=0, keepdims=True), gain_ref.shape)
    grad_middle = cot_ref[...].astype(F32) * weight_ref[0]
    grad_middle = grad_middle + norm_back(part * gains_ref[1:2], unit, scale)
    grad_middle_ref[...] = grad_middle
    attention = grad_middle.astype(BF16)
    attention_ref[...] = attention
    n = half_ref.shape[1]
    low, high = attention[:, :n], attention[:, n:]
    kept, rest = jnp.where(core == 0, low, high), jnp.where(core == 0, high, low)
    for ref, at in ((own_ref, core), (sent_ref, 1 - core)):
        rows = pl.ds(pl.multiple_of(at * n, n), n)
        ref[...] = (dot_t(kept, half_ref[rows, :]) + dot_t(rest, other_ref[rows, :])).astype(BF16)


def out_back_kernel(core_ref, own_ref, got_ref, attention_ref, kept_ref, sent_ref):
    core = core_ref[0]
    n = own_ref.shape[1]
    low, high = attention_ref[:, :n], attention_ref[:, n:]
    kept, rest = jnp.where(core == 0, low, high), jnp.where(core == 0, high, low)
    for ref, at in ((own_ref, core), (got_ref, 1 - core)):
        rows = pl.ds(pl.multiple_of(at * n, n), n)
        heads = ref[...]
        kept_ref[rows, :] = t_dot(heads, kept).astype(BF16)
        sent_ref[rows, :] = t_dot(heads, rest).astype(BF16)


def head_back_kernel(
    core_ref, own_ref, got_ref, mixed_ref, q_ref, c_ref,
    gm_ref, p1_ref, enter_ref, first_p, decay,
):
    step = pl.program_id(0)
    slot = step ^ core_ref[0]
    count = c_ref.shape[0]
    growth = jnp.exp(c_ref[...])
    mask = own_blocks()
    for p in range(PAIRS):
        mixed = mixed_ref[:, q_cols(p)]
        grad = jnp.where(slot == 0, own_ref[:, q_cols(p)], got_ref[:, q_cols(p)]).astype(F32)
        scale = lax.rsqrt(head_sums(mixed * mixed) * (1.0 / HEAD) + head_floor)
        unit = mixed * scale
        back = scale * (grad - unit * (head_sums(grad * unit) * (1.0 / HEAD)))
        gm = back.astype(BF16)
        gm_ref[:, q_cols(p)] = gm
        grown = (q_ref[:, q_cols(p)].astype(F32) * spread_pair(growth, p)).astype(BF16)
        through = jnp.where(mask, t_dot(grown, gm), 0.0)

        @pl.when(step == 0)
        def _():
            first_p[p] = through
            decay[p] = jnp.broadcast_to(spread_pair(growth[count - 1 :], p), (8, WIDE))

        @pl.when(step == 1)
        def _():
            p1_ref[p] = through
            enter_ref[p] = (first_p[p] + decay[p][:1] * through).astype(BF16)


def back_kernel(
    core_ref, qkv_ref, c_ref, ct_ref, z_ref, gm_ref, s0_ref, s1_ref, e1_ref, p1_ref, cos_ref,
    sin_ref, front_ref, bias_ref, later, early,
):
    step = pl.program_id(0)
    count = c_ref.shape[0]
    rows = count // 2
    lane = iota((1, WIDE), 1)
    c, ct = c_ref[...], ct_ref[...]
    growth = jnp.exp(c)
    last = c[count - 1 :]
    tail = jnp.exp(last - c)
    last_row = iota((count, 1), 0) == count - 1
    per_head = jnp.zeros((count, WIDE), F32)
    key_sums, value_sums = [None, None], [None, None]
    cosine, sine_part = cos_ref[...], -sin_ref[...]

    @pl.when(step == 0)
    def _():
        later[...] = e1_ref[...].astype(F32)
        early[...] = s1_ref[...]

    @pl.when(step == 1)
    def _():
        early[...] = s0_ref[...].astype(F32)

    for p in range(PAIRS):
        held, ahead = early[p], later[p]
        query, key, value = qkv_ref[:, q_cols(p)], qkv_ref[:, k_cols(p)], qkv_ref[:, v_cols(p)]
        gm = gm_ref[:, q_cols(p)]
        query_t, gm_t = query.astype(F32).T.astype(BF16), gm.astype(F32).T.astype(BF16)
        d_query, d_key_t, d_value_t = [], [], []
        for h in range(2):
            by_rows, key_t, value_t = [], None, None
            for r in range(2):
                mine, span, upto, scores, decays = tile_of(qkv_ref, c, ct, r, rows, p, h)
                weighted = (scores * decays).astype(BF16)
                grad_weighted = dot_t(jnp.where(mine, gm[span], 0), value[:upto])
                grad_scores = (grad_weighted * decays).astype(BF16)
                by_rows.append(dot(grad_scores, key[:upto]))
                part = slice(HEAD * h, HEAD * (h + 1))
                one_key = dot(query_t[part, span], grad_scores)
                one_value = dot(gm_t[part, span], weighted)
                if r == 0:
                    key_t, value_t = one_key, one_value
                else:
                    key_t = jnp.concatenate([one_key[:, :rows] + key_t, one_key[:, rows:]], 1)
                    value_t = jnp.concatenate(
                        [one_value[:, :rows] + value_t, one_value[:, rows:]], 1
                    )
            d_query.append(jnp.concatenate(by_rows, 0))
            d_key_t.append(key_t)
            d_value_t.append(value_t)
        d_query = jnp.where(lane < HEAD, d_query[0], d_query[1])
        d_query = d_query + spread_pair(growth, p) * dot_t(gm, held.astype(BF16))
        ahead_low = ahead.astype(BF16)
        tails = spread_pair(tail, p)
        d_key_tail = tails * dot_t(value, ahead_low)
        d_key = jnp.concatenate(d_key_t, 0).T + d_key_tail
        d_value = jnp.concatenate(d_value_t, 0).T
        key_f = key.astype(F32)
        d_value = d_value + dot((key_f * tails).astype(BF16), ahead_low)
        total = spread_pair(jnp.exp(last), p)
        at_last = jnp.sum(key_f * d_key_tail, axis=0, keepdims=True)
        at_last = at_last + jnp.sum(ahead * held, axis=0, keepdims=True) * total
        grad_c = query.astype(F32) * d_query - key_f * d_key
        grad_c = grad_c + jnp.where(last_row, at_last, 0.0)
        to_head = iota((WIDE, WIDE), 1) == 2 * p + (iota((WIDE, WIDE), 0) >= HEAD)
        for third in thirds(grad_c):
            per_head = per_head + dot(third, to_head.astype(BF16))
        turned = turn(d_query, cosine, sine_part) * float(HEAD) ** (-0.5)
        front_ref[:, q_cols(p)] = turned.astype(BF16)
        if p < 2:
            key_sums[p], value_sums[p] = d_key, d_value
        else:
            key_sums[p - 2] = key_sums[p - 2] + d_key
            value_sums[p - 2] = value_sums[p - 2] + d_value

        @pl.when(step == 0)
        def _():
            later[p] = p1_ref[p] + total * ahead

    for p in range(2):
        front_ref[:, k_cols(p)] = turn(key_sums[p], cosine, sine_part).astype(BF16)
        front_ref[:, v_cols(p)] = value_sums[p].astype(BF16)
    upper = (iota((count, count), 0) <= iota((count, count), 1)).astype(BF16)
    grad_log = sum(dot(upper, third) for third in thirds(per_head))
    z = z_ref[...]
    grad_gate = jnp.where(lane < HALF, -grad_log / (GATE_TEMP * (1.0 + jnp.exp(-z))), 0.0)
    front_ref[:, N_FRONT - WIDE :] = grad_gate.astype(BF16)
    summed = jnp.broadcast_to(jnp.sum(grad_gate, axis=0, keepdims=True), (8, WIDE))

    @pl.when(step == 0)
    def _():
        bias_ref[...] = summed

    @pl.when(step == 1)
    def _():
        bias_ref[...] += summed


def front_back_kernel(
    core_ref, normed_ref, grad_ref, w_ref, own_ref, other_ref, gain_ref, bias_ref, kept_ref,
    got_ref, part_ref, sent_ref, *refs,
):
    *outs, d_ref = refs
    grad = grad_ref[...]
    d = t_dot(normed_ref[...], grad)
    part = dot_t(grad, w_ref[...])
    count = own_ref.shape[0]
    part_ref[...] = part[:count]
    sent_ref[...] = part[count:].astype(BF16)
    d_gain = jnp.zeros((1, part.shape[1]), F32)
    for ref, rows in ((own_ref, part[:count]), (other_ref, part[count:])):
        x = ref[...].astype(F32)
        unit = x * lax.rsqrt(jnp.mean(x * x, axis=-1, keepdims=True) + epsilon)
        d_gain = d_gain + jnp.sum(rows * unit, axis=0, keepdims=True)
    main = N_FRONT - WIDE
    d_ref[:, :main] = d[:, :main].astype(BF16)
    rest = jnp.concatenate(
        [jnp.zeros((HALF, d_gain.shape[1]), F32), d_gain, gain_ref[:1]]
        + [jnp.zeros((WIDE - HALF - 2, d_gain.shape[1]), F32)],
        0,
    ).T
    d_ref[:, main:N_FRONT] = (d[:, main:] + rest + pltpu.roll(bias_ref[...], HALF + 2, 1)[:1]).astype(BF16)
    d_ref[:, N_FRONT:] = (kept_ref[...].astype(F32) + got_ref[...].astype(F32)).astype(BF16)
    if len(outs) == 1:
        outs[0][...] = d_ref[...]
    else:
        own, over_dp, over_mid, first, second = outs
        rows = own.shape[1]
        for i in range(4):
            for ref, b in ((own, (0, 0)), (over_dp, (1, 0)), (over_mid, (0, 1))):
                ref[i] = d_ref[pl.ds(row_of(core_ref, i, b, rows), rows), :]
            far = first if i < 2 else second
            far[i % 2] = d_ref[pl.ds(row_of(core_ref, i, (1, 1), rows), rows), :]


def far_kernel(core_ref, far_ref, to_dp_ref, to_mid_ref):
    far = far_ref[...].reshape((-1,) + far_ref.shape[-1:])
    n = to_dp_ref.shape[0]
    to_dp_ref[...] = far[:n]
    to_mid_ref[...] = far[n:]


def sends_kernel(core_ref, dp_ref, mid_ref, to_mid_ref, to_dp_ref, over_dp_ref, over_mid_ref):
    width = dp_ref.shape[-1]
    over_dp, over_mid = dp_ref[...].reshape(-1, width), mid_ref[...].reshape(-1, width)
    to_mid, to_dp = to_mid_ref[...].reshape(-1, width), to_dp_ref[...].reshape(-1, width)
    n = to_dp.shape[0]
    over_dp_ref[:n] = over_dp[:n]
    over_dp_ref[n:] = (over_dp[n:].astype(F32) + to_dp.astype(F32)).astype(BF16)
    over_mid_ref[:n] = (over_mid[:n].astype(F32) + to_mid.astype(F32)).astype(BF16)
    over_mid_ref[n:] = over_mid[n:]


def own_kernel(core_ref, own_ref, dp_ref, mid_ref, sum_ref):
    own = own_ref[...].reshape(dp_ref.shape).astype(F32)
    sum_ref[...] = (own + dp_ref[...].astype(F32) + mid_ref[...].astype(F32)).astype(BF16)


def sum_kernel(core_ref, own_ref, dp_ref, mid_ref, kept_ref, sent_ref):
    n = kept_ref.shape[0]
    whole = own_ref[...].astype(F32) + dp_ref[...].astype(F32) + mid_ref[...].astype(F32)
    kept_ref[...] = whole[:n]
    sent_ref[...] = whole[n:].astype(BF16)


def down_kernel(core_ref, hidden_ref, w_ref, out_ref):
    out_ref[...] = dot_t(hidden_ref[...], w_ref[...]).astype(BF16)


def output_kernel(core_ref, hidden_ref, w_ref, middle_ref, got_ref, out_ref):
    out = middle_ref[...] + dot_t(hidden_ref[...], w_ref[...])
    out_ref[...] = (out + got_ref[...].astype(F32)).astype(BF16)


def input_kernel(core_ref, part_ref, got_ref, middle_ref, x_ref, gains_ref, out_ref):
    x = x_ref[...].astype(F32)
    scale = inverse_rms(x)
    grad = (part_ref[...] + got_ref[...].astype(F32)) * gains_ref[:1]
    out_ref[...] = (middle_ref[...] + norm_back(grad, x * scale, scale)).astype(BF16)


def last_kernel(core_ref, pair_ref, got_ref, mine_ref, sent_ref):
    whole = (pair_ref[...] + got_ref[...].astype(F32)).astype(BF16)
    n = mine_ref.shape[0]
    low, high = whole[:n], whole[n:]
    mine_ref[...] = jnp.where(core_ref[0] == 0, low, high)
    sent_ref[...] = jnp.where(core_ref[0] == 0, high, low)


def unpack_kernel(
    core_ref, mine_ref, got_ref, q_ref, k_ref, v_ref, a_ref, o_ref, gains_ref, bias_ref
):
    def both(ref, at):
        n = ref.shape[1] // 2
        a, b = mine_ref[:, at : at + n].astype(F32), got_ref[:, at : at + n].astype(F32)
        ref[:, :n] = jnp.where(core_ref[0] == 0, a, b)
        ref[:, n:] = jnp.where(core_ref[0] == 0, b, a)
        return at + n

    at = both(q_ref, 0)
    at = both(k_ref, at)
    at = both(v_ref, at)
    both(o_ref, N_FRONT)
    a = mine_ref[:, at:N_FRONT].astype(F32).T
    b = got_ref[:, at:N_FRONT].astype(F32).T
    low, high = jnp.where(core_ref[0] == 0, a, b), jnp.where(core_ref[0] == 0, b, a)
    a_ref[:HALF] = low[:HALF]
    a_ref[HALF:] = high[:HALF]
    gains_ref[...] = (a + b)[HALF : HALF + 8]
    bias_ref[:HALF] = low[HALF + 2 : 2 * HALF + 2]
    bias_ref[HALF:] = high[HALF + 2 : 2 * HALF + 2]


def call(kernel, ins, outs, name, microseconds, megabytes, steps=1, scratch=(), deps=(), reverse=False):
    order = (lambda i, s: (1 - i) ^ s[0]) if reverse else (lambda i, s: i ^ s[0])

    def spec(kind, shape):
        zeros = (0,) * (len(shape) - 1)
        if kind == "all":
            return pl.BlockSpec(shape, lambda i, s: (0,) + zeros)
        if kind == "scalar":
            return SCALARS
        if kind == "block":
            return pl.BlockSpec((shape[0] // 2,) + shape[1:], lambda i, s: (order(i, s),) + zeros)
        if kind == "rows":
            return pl.BlockSpec((shape[0] // steps,) + shape[1:], lambda i, s: (i,) + zeros)
        if kind == "entry":
            return pl.BlockSpec((None,) + shape[1:], lambda i, s: (order(i, s),) + zeros)
        if kind == "queries":
            return pl.BlockSpec((shape[0] // 2, N_Q), lambda i, s: (order(i, s), 0))
        if kind in ("own", "over_dp", "over_mid", "far"):
            a, b = int(kind in ("over_dp", "far")), int(kind in ("over_mid", "far"))
            block = (1, shape[1], 1) + shape[3:]
            return pl.BlockSpec(block, lambda i, s: (s[1] ^ a, 0, s[3] ^ b, 0, 0))
        block, index = kind
        return pl.BlockSpec(block, lambda i, s: index)

    where, *ins = ins
    moved = sum(v.size * v.dtype.itemsize for _, v in ins)
    return pl.pallas_call(
        without(kernel, 1 + len(ins), len(deps)),
        grid_spec=pltpu.PrefetchScalarGridSpec(
            num_scalar_prefetch=1,
            grid=(steps,),
            in_specs=[spec(kind, v.shape) for kind, v in ins] + [ANYWHERE] * len(deps),
            out_specs=[spec(kind, shape) for kind, shape, _ in outs],
            scratch_shapes=scratch,
        ),
        out_shape=[jax.ShapeDtypeStruct(shape, kind) for _, shape, kind in outs],
        compiler_params=pltpu.CompilerParams(
            dimension_semantics=("arbitrary",), vmem_limit_bytes=megabytes * 1024 * 1024
        ),
        cost_estimate=pl.CostEstimate(
            flops=int(microseconds * FLOPS), bytes_accessed=moved, transcendentals=0
        ),
        name=name,
    )(where, *[v for _, v in ins], *deps)


def piece(whole, a, b, low, count):
    sizes = (1, count, 1) + whole.shape[3:]
    return lax.dynamic_slice(whole, (a, low, b, 0, 0), sizes).reshape((count,) + whole.shape[3:])


def square_sends(over_dp, over_mid, to_mid, to_dp):
    half = to_mid.shape[0]
    send_mid = jnp.concatenate([over_mid[:half] + to_mid, over_mid[half:]], 0)
    send_dp = jnp.concatenate([over_dp[:half], over_dp[half:] + to_dp], 0)
    return send_dp, send_mid


def hi_swap(v, difference):
    return lax.ppermute(v, "hi", [(i, i ^ difference) for i in range(4)])


def sequence_weights(group_ids, loss_weights):
    group_count = loss_weights.shape[0]
    member = (group_ids[:, None] == jnp.arange(group_count, dtype=jnp.int32)[None, :]).astype(F32)
    counts = jnp.sum(member, axis=0)
    raw_weight = jnp.sum(member * loss_weights.astype(F32)[None, :], axis=1) / jnp.sum(
        member * counts[None, :], axis=1
    )
    return raw_weight * (group_ids.shape[0] / jnp.sum(raw_weight))


def shards(
    tokens,
    cotangent,
    group_ids,
    loss_weights,
    gain_one,
    w_query,
    w_key,
    w_value,
    w_gate,
    gate_bias,
    w_out,
    gain_two,
    w_gate_ff,
    w_up,
    w_down,
):
    count, width = tokens.shape
    both = 2 * count
    n_out, n_ff = w_out.shape[1] // 2, w_up.shape[1] // 2
    n_first = N_FRONT + n_out
    core, mid = lax.axis_index("core"), lax.axis_index("mid")
    dp, hi = lax.axis_index("dp"), lax.axis_index("hi")
    where = jnp.stack([core, dp, hi, mid]).astype(jnp.int32)
    small = small_slice()
    sequence = lax.axis_index(ALL) // SPAN
    square = (PAIRS, WIDE, WIDE)

    packed = pack(
        core, w_query, w_key, w_value, w_gate.T, gain_one[None], gain_two[None], w_out, w_gate_ff,
        w_up, w_down.T,
    )
    first = place(core, packed[0], swap(packed[2], "core"))
    rest = place(core, packed[1], swap(packed[3], "core"))
    w_rest = gather(rest)
    if small:
        pair = jnp.stack([first, hi_swap(first, 2)])
        own = jnp.concatenate([pair, hi_swap(pair, 1)], 0)
        over_dp, over_mid = swap(own, "dp"), swap(own, "mid")
        pieces = (own, over_dp, over_mid, swap(over_dp[:2], "mid"), swap(over_mid[2:], "dp"))
    else:
        pieces = (gather(first),)
    other_tokens, other_cotangent = swap(tokens, "core"), swap(cotangent, "core")
    gate_block, up_block, down_block = [((width, n_ff), (0, i)) for i in range(3)]

    block = 2 * mid + (core ^ jnp.arange(2))
    positions = (block[:, None] * count + jnp.arange(count)[None, :]).reshape(-1)
    frequency = ROPE_BASE ** (-jnp.arange(HEAD // 2, dtype=F32) / (HEAD // 2))
    angles = positions.astype(F32)[:, None] * frequency[None, :]
    cosine, sine_part = jnp.cos(angles), jnp.sin(angles)
    cosine = jnp.concatenate([cosine] * 4, 1)
    sine_part = jnp.concatenate([-sine_part, sine_part] * 2, 1)
    own_bias = lax.dynamic_slice_in_dim(gate_bias, core * HALF, HALF)
    own_bias = jnp.concatenate([own_bias, jnp.zeros((WIDE - HALF,), F32)])[None, :]
    w_front, w_half, normed_one, qkv, c, ct, z, gains, update, leaving = call(
        front_kernel,
        [where, ("all", tokens), ("all", other_tokens), ("all", own_bias)]
        + [("block", cosine), ("block", sine_part)]
        + [("all", v) for v in pieces],
        [("all", (width, N_FRONT), BF16), ("all", (width, n_out), BF16)]
        + [("block", (both, width), BF16), ("block", (both, 2 * N_Q), BF16)]
        + [("block", (both, WIDE), F32), ("entry", (2, HALF, count), F32)]
        + [("block", (both, WIDE), F32), ("all", (8, width), F32)]
        + [("all", square, F32), ("all", square, BF16)],
        "front",
        14,
        24,
        2,
        [pltpu.VMEM(square, F32)],
    )
    state_0 = lax.ppermute(leaving, "mid", [(0, 1)])
    w_other = swap(w_half, "core")
    mixed_out, normed_own, normed_sent, state_1 = call(
        mix_kernel,
        [where, ("block", qkv), ("block", c), ("entry", ct), ("all", state_0), ("all", update)],
        [("block", (both, N_Q), F32)]
        + [("all", (count, N_Q), BF16)] * 2
        + [("all", square, F32)],
        "mix",
        11,
        16,
        2,
        [pltpu.VMEM(square, F32)],
    )
    normed_got = swap(normed_sent, "core")
    middle, normed_two_own = call(
        out_kernel,
        [where]
        + [("all", v) for v in (normed_own, normed_got, w_half, w_other, tokens, gains)],
        [("all", (count, width), F32), ("all", (count, width), BF16)],
        "out",
        4,
        16,
    )
    normed_two_other = swap(normed_two_own, "core")
    seq_weights = sequence_weights(group_ids, loss_weights)
    own_weight = jnp.sum(jnp.where(jnp.arange(group_ids.shape[0]) == sequence, seq_weights, 0.0))
    own_weight = own_weight.reshape(1)
    hidden, slopes, normed_two, grad_branch = call(
        functools.partial(ff_kernel, small),
        [where, ("scalar", own_weight), ("all", normed_two_own), ("all", normed_two_other)]
        + [("all", cotangent), ("all", other_cotangent)]
        + [(gate_block, w_rest), (up_block, w_rest)],
        [("rows", (both, n_ff), BF16), ("rows", (both, 2 * n_ff), BF16)]
        + [("rows", (both, width), BF16)] * 2,
        "ff",
        15,
        44,
        2,
    )
    d_down = jnp.einsum(
        "ta,tb->ab", grad_branch, hidden, preferred_element_type=F32
    ).astype(BF16)
    if small:
        by_hi = d_down
        down_hi = d_down.reshape(4, -1, n_ff)
        down_hi = lax.psum_scatter(down_hi, "hi", scatter_dimension=0, tiled=False)
        down_hi = down_hi.reshape(2, 1, 2, -1, n_ff)
    else:
        by_hi = d_down
        down_sum = scatter(d_down)
    (grad_ff,) = call(
        functools.partial(ff_back_kernel, small),
        [where, ("rows", grad_branch), (down_block, w_rest), ("rows", slopes)],
        [("rows", (both, 2 * n_ff), BF16)],
        "ff_back",
        9,
        32,
        2,
        deps=(by_hi,),
    )
    d_ff = jnp.einsum(
        "ta,tb->ab", normed_two, grad_ff, preferred_element_type=F32
    ).astype(BF16)
    if small:
        d_ff = d_ff.reshape(2, 4, 2, -1, 2 * n_ff)
        ff_sends = [piece(d_ff, 1 - dp, 1 - mid, i, 2) for i in (0, 2)]
        ff_one = swap(ff_sends[0], "dp"), swap(ff_sends[1], "mid")
    else:
        ff_sends = [d_ff]
        ff_sum = scatter(d_ff)
    (part_sent,) = call(
        lambda _, *refs: part_kernel(*refs),
        [where, (((count, 2 * n_ff), (1, 0)), grad_ff), (gate_block, w_rest), (up_block, w_rest)],
        [("all", (count, width), BF16)],
        "part",
        8,
        24,
        deps=ff_sends,
    )
    part_got = swap(part_sent, "core")
    grad_middle, grad_attention, d_gain_two, grad_own, grad_sent = call(
        middle_kernel,
        [where, ("scalar", own_weight), (((count, 2 * n_ff), (0, 0)), grad_ff)]
        + [(gate_block, w_rest), (up_block, w_rest)]
        + [("all", v) for v in (part_got, cotangent, middle, gains, w_half, w_other)],
        [("all", (count, width), F32), ("all", (count, width), BF16), ("all", (8, width), F32)]
        + [("all", (count, N_Q), BF16)] * 2,
        "middle",
        12,
        36,
        deps=(part_sent,),
    )
    grad_got = swap(grad_sent, "core")
    d_out_kept, d_out_sent = call(
        out_back_kernel,
        [where] + [("all", v) for v in (normed_own, normed_got, grad_attention)],
        [("all", (width, n_out), BF16)] * 2,
        "out_back",
        2,
        16,
    )
    d_out_got = swap(d_out_sent, "core")
    grad_mixed, through, entering = call(
        head_back_kernel,
        [where, ("all", grad_own), ("all", grad_got), ("block", mixed_out), ("queries", qkv)]
        + [("block", c)],
        [("block", (both, N_Q), BF16), ("all", square, F32), ("all", square, BF16)],
        "head_back",
        8,
        16,
        2,
        [pltpu.VMEM(square, F32), pltpu.VMEM((PAIRS, 8, WIDE), F32)],
        deps=(d_out_sent,),
    )
    state_last = lax.ppermute(entering, "mid", [(1, 0)])
    down_rows = ((count, n_ff), (1, 0)), ((count, n_ff), (0, 0))
    (out_sent,) = call(
        down_kernel,
        [where, (down_rows[0], hidden), (down_block, w_rest)],
        [("all", (count, width), BF16)],
        "out_sent",
        5,
        16,
        deps=(entering,),
    )
    if small:
        ff_sends = call(
            sends_kernel,
            [where, ("over_dp", d_ff), ("over_mid", d_ff)] + [("all", v) for v in ff_one],
            [("all", (width // 4, 2 * n_ff), BF16)] * 2,
            "ff_sends",
            3,
            16,
            deps=(state_last, out_sent),
        )
        ff_got = swap(ff_sends[0], "dp"), swap(ff_sends[1], "mid")
    grad_front, d_bias = call(
        back_kernel,
        [where, ("block", qkv), ("block", c), ("entry", ct), ("block", z), ("block", grad_mixed)]
        + [("all", v) for v in (state_0, state_1, state_last, through)]
        + [("block", cosine), ("block", sine_part)],
        [("block", (both, N_FRONT), BF16), ("all", (8, WIDE), F32)],
        "back",
        20,
        24,
        2,
        [pltpu.VMEM(square, F32), pltpu.VMEM(square, F32)],
        deps=ff_sends,
        reverse=True,
    )
    (output,) = call(
        output_kernel,
        [where, (down_rows[1], hidden), (down_block, w_rest)]
        + [("all", v) for v in (middle, swap(out_sent, "core"))],
        [("all", (count, width), BF16)],
        "output",
        5.5,
        16,
        deps=(grad_front,),
    )
    if small:
        (ff_hi,) = call(
            own_kernel,
            [where, ("own", d_ff)] + [("all", v.reshape(4, -1, 2 * n_ff)) for v in ff_got],
            [("all", (4, width // 16, 2 * n_ff), BF16)],
            "ff_own",
            3,
            16,
            deps=(output,),
        )
        ff_sum = lax.psum_scatter(ff_hi, "hi", scatter_dimension=0, tiled=False)
        shapes = [(4, width // 16, n_first)] * 3 + [(2, width // 16, n_first)] * 2
        deps = (ff_hi,)
    else:
        shapes = [(width, n_first)]
        deps = (output,)
    part_kept, part_sent, *d_first = call(
        front_back_kernel,
        [where]
        + [("all", v) for v in (normed_one, grad_front, w_front, tokens, other_tokens)]
        + [("all", v) for v in (d_gain_two, d_bias, d_out_kept, d_out_got)],
        [("all", (count, width), F32), ("all", (count, width), BF16)]
        + [("all", shape, BF16) for shape in shapes],
        "front_back",
        12,
        32,
        scratch=[pltpu.VMEM((width, n_first), BF16)],
        deps=deps,
    )
    part_got = swap(part_sent, "core")

    def add_input(deps):
        return call(
            input_kernel,
            [where]
            + [("all", v) for v in (part_kept, part_got, grad_middle, tokens, gains)],
            [("all", (count, width), BF16)],
            "grad_input",
            4.5,
            16,
            deps=deps,
        )

    if small:
        own, over_dp, over_mid, far_0, far_1 = d_first
        one = swap(far_0, "dp"), swap(far_1, "mid")
        down_sends = call(
            far_kernel,
            [where, ("far", down_hi)],
            [("all", (width // 32, n_ff), BF16)] * 2,
            "down_far",
            1.5,
            16,
            deps=(far_0,),
        )
        down_one = swap(down_sends[0], "dp"), swap(down_sends[1], "mid")
        sends = square_sends(over_dp, over_mid, *one)
        down_sends = call(
            sends_kernel,
            [where, ("over_dp", down_hi), ("over_mid", down_hi)] + [("all", v) for v in down_one],
            [("all", (width // 16, n_ff), BF16)] * 2,
            "down_sends",
            2,
            16,
            deps=(sends[0],),
        )
        down_got = swap(down_sends[0], "dp"), swap(down_sends[1], "mid")
        (grad_input,) = add_input(sends[:1])
        kept, sent = call(
            sum_kernel,
            [where]
            + [("all", v) for v in (own, swap(sends[0], "dp"), swap(sends[1], "mid"))],
            [("all", (2,) + own.shape[1:], F32), ("all", (2,) + own.shape[1:], BF16)],
            "first_sum",
            2,
            16,
            deps=(grad_input, *down_sends),
        )
        pair = kept + hi_swap(sent, 1).astype(F32)
        last, last_got = pair[0], hi_swap(pair[1].astype(BF16), 2)
        (down_sum,) = call(
            own_kernel,
            [where, ("own", down_hi)] + [("all", v) for v in down_got],
            [("all", (width // 16, n_ff), BF16)],
            "down_own",
            1.5,
            16,
            deps=(kept,),
        )
    else:
        last = scatter(d_first[0]).astype(F32)
        last_got = jnp.zeros_like(last, BF16)
        (grad_input,) = add_input(())

    def owned(rows):
        n = rows.shape[0] // 2
        mine = lax.dynamic_slice_in_dim(rows, core * n, n)
        return mine, swap(lax.dynamic_slice_in_dim(rows, (1 - core) * n, n), "core")

    outs = []
    for v in (ff_sum[:, :n_ff], ff_sum[:, n_ff:], down_sum):
        mine, theirs = owned(v)
        outs.append((mine, theirs))
    n = last.shape[0] // 2
    mine, sent = call(
        last_kernel,
        [where, ("all", last), ("all", last_got)],
        [("all", (n, n_first), BF16)] * 2,
        "last",
        1.5,
        16,
        deps=tuple(theirs for _, theirs in outs),
    )
    theirs = swap(sent, "core")
    g_gate_ff, g_up, g_down = [beside(core, *v) for v in outs]
    g_query, g_key, g_value, g_gate, g_out, g_gains, g_bias = call(
        unpack_kernel,
        [where, ("all", mine), ("all", theirs)],
        [("all", (n, 2 * N_Q), F32)]
        + [("all", (n, 2 * N_K), F32)] * 2
        + [("all", (HEADS, n), F32), ("all", (n, 2 * n_out), F32)]
        + [("all", (8, n), F32), ("all", (HEADS, n), F32)],
        "unpack",
        1.5,
        16,
    )
    return (
        output,
        grad_input,
        g_gains[0],
        g_query,
        g_key,
        g_value,
        g_gate.T,
        g_bias[:, 0],
        g_out,
        g_gains[1],
        g_gate_ff,
        g_up,
        g_down.T,
    )


def solution(mesh):
    devices = mesh.devices
    fine = Mesh(
        devices.reshape(devices.shape[0], devices.shape[1] // SPAN, SPAN // 2, 2), ALL
    )
    rows, columns, split = P(ALL, None), P(None, ALL), P(ALL)
    in_specs = (rows, rows, P(), P(), split) + (rows,) * 4 + (P(), rows, split, rows, rows, columns)
    out_specs = (rows, rows, split) + (rows,) * 4 + (P(), rows, split, rows, rows, columns)
    return jax.shard_map(shards, mesh=fine, in_specs=in_specs, out_specs=out_specs, check_vma=False)
```

```python
import functools

import jax
import jax.numpy as jnp
from jax import lax
from jax.experimental import pallas as pl
from jax.experimental.pallas import tpu as pltpu
from jax.sharding import Mesh, PartitionSpec as P

HEADS = 16
HEAD = 64
KVH = 2
LATENT = 256
SPAN = 4

epsilon = 1e-05
head_floor = 0.25
ROPE_BASE = 10000.0
GATE_TEMP = 16.0

CHIPS = ("dp", "hi", "mid")
ALL = ("dp", "hi", "mid", "core")
F32 = jnp.float32
BF16 = jnp.bfloat16


def swap(v, axis):
    return lax.ppermute(v, axis, [(0, 1), (1, 0)])


def place(bit, mine, theirs):
    return jnp.where(
        bit == 0, jnp.concatenate([mine, theirs], 0), jnp.concatenate([theirs, mine], 0)
    )


def small_slice():
    return lax.axis_size("dp") == 2 and lax.axis_size("hi") == 4


def gather(part):
    return lax.all_gather(part, CHIPS, axis=0, tiled=True)


def add3(a, b, c):
    return a.astype(F32) + b.astype(F32) + c.astype(F32)


def scatter(whole):
    return lax.psum_scatter(whole, CHIPS, scatter_dimension=0, tiled=True)


def beside(core, mine, theirs):
    return jnp.where(
        core == 0, jnp.concatenate([mine, theirs], 1), jnp.concatenate([theirs, mine], 1)
    ).astype(F32)


HALF = HEADS // 2
PAIRS = HALF // 2
WIDE = 2 * HEAD
N_Q = HALF * HEAD
N_K = N_Q // 2
N_FRONT = N_Q + 2 * N_K + WIDE
FLOPS = 0.55e9


def dot(left, right):
    return jnp.dot(left, right, preferred_element_type=F32)


def dot_t(left, right):
    return lax.dot_general(left, right, (((1,), (1,)), ((), ())), preferred_element_type=F32)


def t_dot(left, right):
    return lax.dot_general(left, right, (((0,), (0,)), ((), ())), preferred_element_type=F32)


def thirds(v):
    high = v.astype(BF16)
    rest = v - high.astype(F32)
    middle = rest.astype(BF16)
    return high, middle, (rest - middle.astype(F32)).astype(BF16)


def iota(shape, axis):
    return lax.broadcasted_iota(jnp.int32, shape, axis)


def spread_pair(per_head, p):
    lane = iota((1, WIDE), 1)
    return jnp.where(
        lane < HEAD, per_head[:, 2 * p : 2 * p + 1], per_head[:, 2 * p + 1 : 2 * p + 2]
    )


def head_sums(v):
    lane = iota((1, WIDE), 1)
    low = jnp.sum(jnp.where(lane < HEAD, v, 0.0), axis=1, keepdims=True)
    high = jnp.sum(jnp.where(lane < HEAD, 0.0, v), axis=1, keepdims=True)
    return jnp.where(lane < HEAD, low, high)


def turn(v, cosine, sine_part):
    lane = iota((1, WIDE), 1)
    other = jnp.where(
        lane % HEAD < HEAD // 2,
        pltpu.roll(v, WIDE - HEAD // 2, 1),
        pltpu.roll(v, HEAD // 2, 1),
    )
    return v * cosine + other * sine_part


def own_blocks():
    return (iota((WIDE, WIDE), 0) < HEAD) == (iota((WIDE, WIDE), 1) < HEAD)


def q_cols(p):
    return slice(WIDE * p, WIDE * (p + 1))


def k_cols(p):
    return slice(N_Q + WIDE * (p % 2), N_Q + WIDE * (p % 2 + 1))


def v_cols(p):
    return slice(N_Q + N_K + WIDE * (p % 2), N_Q + N_K + WIDE * (p % 2 + 1))


def without(kernel, start, count):
    return lambda *refs: kernel(*refs[:start], *refs[start + count :])


ANYWHERE = pl.BlockSpec(memory_space=pl.ANY)
SCALARS = pl.BlockSpec(memory_space=pltpu.SMEM)


def inverse_rms(values, added=epsilon):
    return lax.rsqrt(jnp.mean(values * values, axis=-1, keepdims=True) + added)


def norm_back(grad_unit, unit_rows, scale_rows):
    return scale_rows * (
        grad_unit - unit_rows * jnp.mean(grad_unit * unit_rows, axis=-1, keepdims=True)
    )


def row_of(where, i, b, rows):
    hi = where[2] ^ (0, 2, 1, 3)[i]
    index = ((where[1] ^ b[0]) * 4 + hi) * 2 + (where[3] ^ b[1])
    return pl.multiple_of(index * rows, rows)


def pack_kernel(core_ref, q_ref, k_ref, v_ref, a_ref, g1_ref, g2_ref, o_ref, f_ref, u_ref, d_ref, *outs):
    def put(out, at, v):
        out[:, at : at + v.shape[1]] = v
        return at + v.shape[1]

    rows = q_ref.shape[0]
    lane = iota((1, WIDE), 1)
    gates = a_ref[...].astype(F32)
    gains = [g1_ref[...].astype(F32), g2_ref[...].astype(F32)]
    for i in range(2):
        front, rest = outs[2 * i : 2 * i + 2]
        mine = core_ref[0] if i == 0 else 1 - core_ref[0]

        def half(ref):
            n = ref.shape[1] // 2
            return jnp.where(mine == 0, ref[:, :n], ref[:, n:])

        at = put(front, 0, half(q_ref))
        at = put(front, at, half(k_ref))
        at = put(front, at, half(v_ref))
        some = jnp.where(mine == 0, gates[:HALF], gates[HALF:])
        small = jnp.concatenate([some, *gains, jnp.zeros((WIDE - HALF - 2, rows), F32)], 0)
        at = put(front, at, small.T.astype(BF16))
        put(front, at, half(o_ref))
        at = put(rest, 0, half(f_ref))
        at = put(rest, at, half(u_ref))
        put(rest, at, half(d_ref))


def pack(core, *weights):
    rows = weights[0].shape[0]
    n_out, n_ff = weights[6].shape[1] // 2, weights[7].shape[1] // 2
    return pl.pallas_call(
        pack_kernel,
        in_specs=[pl.BlockSpec(memory_space=pltpu.SMEM)]
        + [pl.BlockSpec(memory_space=pltpu.VMEM)] * len(weights),
        out_specs=[pl.BlockSpec(memory_space=pltpu.VMEM)] * 4,
        out_shape=[
            jax.ShapeDtypeStruct((rows, n), BF16) for n in (N_FRONT + n_out, 3 * n_ff)
        ]
        * 2,
        name="pack",
    )(core.reshape(1).astype(jnp.int32), *weights)


def front_kernel(
    core_ref, own_ref, other_ref, bias_ref, cos_ref, sin_ref, *refs
):
    *pieces, w_ref, out_ref = refs[:-9]
    normed_ref, qkv_ref, c_ref, ct_ref, z_ref, gains_ref, u_ref, leave_ref, first_u = refs[-9:]
    step = pl.program_id(0)
    slot = step ^ core_ref[0]

    @pl.when(step == 0)
    def _():
        if len(pieces) == 1:
            w_ref[...] = pieces[0][:, :N_FRONT]
            out_ref[...] = pieces[0][:, N_FRONT:]
        else:
            own, over_dp, over_mid, first, second = pieces
            rows = own.shape[1]
            for i in range(4):
                far = first[i] if i < 2 else second[i - 2]
                for v, b in ((own[i], (0, 0)), (over_dp[i], (1, 0)), (over_mid[i], (0, 1)), (far, (1, 1))):
                    to = pl.ds(row_of(core_ref, i, b, rows), rows)
                    w_ref[to, :] = v[:, :N_FRONT]
                    out_ref[to, :] = v[:, N_FRONT:]

    x = jnp.where(slot == 0, own_ref[...], other_ref[...]).astype(F32)
    gains = w_ref[:, N_FRONT - WIDE :].astype(F32).T[HALF : HALF + 8]
    gains_ref[...] = gains
    scale = lax.rsqrt(jnp.mean(x * x, axis=-1, keepdims=True) + epsilon)
    normed = (x * scale * gains[:1]).astype(BF16)
    normed_ref[...] = normed
    pre = dot(normed, w_ref[...])
    cosine, sine_part = cos_ref[...], sin_ref[...]
    for p in range(PAIRS):
        turned = turn(pre[:, q_cols(p)], cosine, sine_part)
        qkv_ref[:, q_cols(p)] = (turned * float(HEAD) ** (-0.5)).astype(BF16)
    for p in range(PAIRS // 2):
        qkv_ref[:, k_cols(p)] = turn(pre[:, k_cols(p)], cosine, sine_part).astype(BF16)
        qkv_ref[:, v_cols(p)] = pre[:, v_cols(p)].astype(BF16)
    z = pre[:, N_FRONT - WIDE :] + bias_ref[...]
    z_ref[...] = z
    small = jnp.exp(-jnp.abs(z))
    log_part = jnp.where(
        small < 0.01, small * (1.0 - small * (0.5 - small * (1.0 / 3.0))), jnp.log(1.0 + small)
    )
    softplus = jnp.maximum(z, 0.0) + log_part
    log_decay = jnp.where(iota((1, WIDE), 1) < HALF, -softplus / GATE_TEMP, 0.0)
    count = x.shape[0]
    lower = (iota((count, count), 0) >= iota((count, count), 1)).astype(BF16)
    c = sum(dot(lower, third) for third in thirds(log_decay))
    c_ref[...] = c
    ct_ref[...] = c.T[:HALF]
    last = c[count - 1 :]
    tail = jnp.exp(last - c)
    mask = own_blocks()
    for p in range(PAIRS):
        scaled = (qkv_ref[:, k_cols(p)].astype(F32) * spread_pair(tail, p)).astype(BF16)
        update = jnp.where(mask, t_dot(scaled, qkv_ref[:, v_cols(p)]), 0.0)

        @pl.when(step == 0)
        def _():
            u_ref[p] = update
            first_u[p] = update

        @pl.when(step == 1)
        def _():
            grown = spread_pair(jnp.exp(last), p) * first_u[p] + update
            leave_ref[p] = grown.astype(BF16)


def tile_of(qkv_ref, c, ct, r, rows, p, h):
    lane = iota((1, WIDE), 1)
    mine = (lane < HEAD) if h == 0 else (lane >= HEAD)
    span = slice(rows * r, rows * (r + 1))
    upto = rows * (r + 1)
    query = jnp.where(mine, qkv_ref[span, q_cols(p)], 0)
    scores = dot_t(query, qkv_ref[:upto, k_cols(p)])
    head = 2 * p + h
    differences = c[span, head : head + 1] - ct[head : head + 1, :upto]
    causal = iota((rows, upto), 0) + rows * r >= iota((rows, upto), 1)
    decays = jnp.exp(jnp.where(causal, differences, -1e30))
    return mine, span, upto, scores, decays


def mix_kernel(
    core_ref, qkv_ref, c_ref, ct_ref, s0_ref, u_ref,
    mixed_ref, own_ref, sent_ref, s1_ref, state,
):
    step = pl.program_id(0)
    slot = step ^ core_ref[0]
    count = c_ref.shape[0]
    rows = count // 2
    lane = iota((1, WIDE), 1)
    c, ct = c_ref[...], ct_ref[...]

    @pl.when(step == 0)
    def _():
        state[...] = s0_ref[...].astype(F32)

    growth = jnp.exp(c)
    for p in range(PAIRS):
        held = state[p]
        carried = spread_pair(growth, p) * dot(qkv_ref[:, q_cols(p)], held.astype(BF16))
        for r in range(2):
            parts = []
            for h in range(2):
                mine, span, upto, scores, decays = tile_of(qkv_ref, c, ct, r, rows, p, h)
                weighted = (scores * decays).astype(BF16)
                parts.append(dot(weighted, qkv_ref[:upto, v_cols(p)]))
            mixed = jnp.where(lane < HEAD, parts[0], parts[1]) + carried[span]
            mixed_ref[span, q_cols(p)] = mixed
            scale = lax.rsqrt(head_sums(mixed * mixed) * (1.0 / HEAD) + head_floor)
            normed = (mixed * scale).astype(BF16)

            @pl.when(slot == 0)
            def _():
                own_ref[span, q_cols(p)] = normed

            @pl.when(slot == 1)
            def _():
                sent_ref[span, q_cols(p)] = normed

        @pl.when(step == 0)
        def _():
            grown = spread_pair(growth[count - 1 :], p) * held + u_ref[p]
            s1_ref[p] = grown
            state[p] = grown


def out_kernel(
    core_ref, own_ref, got_ref, half_ref, other_ref, x_ref, gains_ref, middle_ref, normed_ref
):
    core = core_ref[0]
    n = own_ref.shape[1]
    mine = pl.ds(pl.multiple_of(core * n, n), n)
    theirs = pl.ds(pl.multiple_of((1 - core) * n, n), n)
    own, got = own_ref[...], got_ref[...]
    a = dot(own, half_ref[mine, :]) + dot(got, half_ref[theirs, :])
    b = dot(own, other_ref[mine, :]) + dot(got, other_ref[theirs, :])
    attention = jnp.where(core == 0, jnp.concatenate([a, b], 1), jnp.concatenate([b, a], 1))
    middle = x_ref[...].astype(F32) + attention
    middle_ref[...] = middle
    normed_ref[...] = (middle * inverse_rms(middle) * gains_ref[1:2]).astype(BF16)


def ff_kernel(
    small, where_ref, weight_ref, own_ref, other_ref, cot_ref, cot_other_ref, w_ref,
    hidden_out, down_out, d_ff_out, d_down_out, kept_ref, sent_ref, *refs,
):
    *far_outs, gate, up, down, hidden, grads, branch, d_ff, d_down, in_sems, out_sems = refs
    count = own_ref.shape[0]
    n = gate.shape[1]
    loads = [
        pltpu.make_async_copy(w_ref.at[:, pl.ds(n * i, n)], to, in_sems.at[i])
        for i, to in enumerate((gate, up, down))
    ]
    for load in loads:
        load.start()
    stores = []

    def store(piece, to):
        stores.append(pltpu.make_async_copy(piece, to, out_sems.at[len(stores)]))
        stores[-1].start()

    for i, ref in enumerate((cot_ref, cot_other_ref)):
        scaled = (ref[...].astype(F32) * weight_ref[0]).astype(BF16)
        branch[count * i : count * (i + 1), :] = scaled
    for load in loads:
        load.wait()
    block = 512
    for i, ref in enumerate((own_ref, other_ref)):

        @pl.loop(0, count // block)
        def _(j):
            from_ = pl.ds(pl.multiple_of(j * block, block), block)
            at = pl.ds(pl.multiple_of(count * i + j * block, block), block)
            x = ref[from_, :]
            g, u = dot(x, gate[...]), dot(x, up[...])
            grad = dot(branch[at, :], down[...])
            sigmoid = 1.0 / (1.0 + jnp.exp(-g))
            silu = g * sigmoid
            hidden[at, :] = (silu * u).astype(BF16)
            slope = sigmoid * (1.0 + g * (1.0 - sigmoid))
            grads[at, :n] = (grad * u * slope).astype(BF16)
            grads[at, n:] = (grad * silu).astype(BF16)

    store(hidden, hidden_out)
    store(down, down_out)

    def part(i):
        at = slice(count * i, count * (i + 1))
        return dot_t(grads[at, :n], gate[...]) + dot_t(grads[at, n:], up[...])

    width = own_ref.shape[1]

    @pl.loop(0, width // block)
    def _(j):
        at = pl.ds(pl.multiple_of(j * block, block), block)
        d = t_dot(own_ref[:, at], grads[:count, :]) + t_dot(other_ref[:, at], grads[count:, :])
        d_ff[at, :] = d.astype(BF16)

    store(d_ff, d_ff_out)
    if small:
        rows = width // 16
        for i in range(4):
            index = ((1 - where_ref[1]) * 4 + i) * 2 + 1 - where_ref[3]
            from_ = pl.ds(pl.multiple_of(index * rows, rows), rows)
            store(d_ff.at[from_, :], far_outs[i // 2].at[pl.ds(rows * (i % 2), rows), :])

    chunk = width // 8
    order = [4 * (j % 2) + j // 2 if small else j for j in range(8)]
    for j in range(0, 8, 4):
        columns = [branch[:, chunk * i : chunk * (i + 1)] for i in order[j : j + 4]]
        d = t_dot(jnp.concatenate(columns, 1), hidden[...])
        d_down[chunk * j : chunk * (j + 4), :] = d.astype(BF16)
    store(d_down, d_down_out)
    sent_ref[...] = part(1).astype(BF16)
    kept_ref[...] = part(0)
    for one in stores:
        one.wait()


def middle_kernel(
    core_ref, weight_ref, part_ref, got_ref, cot_ref, middle_ref, gains_ref, half_ref, other_ref,
    normed_ref, normed_got_ref, grad_middle_ref, gain_ref, own_ref, sent_ref, out_kept_ref,
    out_sent_ref,
):
    core = core_ref[0]
    part = part_ref[...] + got_ref[...].astype(F32)
    middle = middle_ref[...]
    scale = inverse_rms(middle)
    unit = middle * scale
    gain_ref[...] = jnp.broadcast_to(jnp.sum(part * unit, axis=0, keepdims=True), gain_ref.shape)
    grad_middle = cot_ref[...].astype(F32) * weight_ref[0]
    grad_middle = grad_middle + norm_back(part * gains_ref[1:2], unit, scale)
    grad_middle_ref[...] = grad_middle
    attention = grad_middle.astype(BF16)
    n = half_ref.shape[1]
    low, high = attention[:, :n], attention[:, n:]
    kept, rest = jnp.where(core == 0, low, high), jnp.where(core == 0, high, low)
    pairs = ((sent_ref, normed_got_ref, 1 - core), (own_ref, normed_ref, core))
    for ref, heads_ref, at in pairs:
        rows = pl.ds(pl.multiple_of(at * n, n), n)
        ref[...] = (dot_t(kept, half_ref[rows, :]) + dot_t(rest, other_ref[rows, :])).astype(BF16)
        heads = heads_ref[...]
        out_kept_ref[rows, :] = t_dot(heads, kept).astype(BF16)
        out_sent_ref[rows, :] = t_dot(heads, rest).astype(BF16)


def add_kernel(core_ref, a_ref, b_ref, sum_ref):
    sum_ref[...] = (a_ref[...].astype(F32) + b_ref[...].astype(F32)).astype(BF16)


def head_back_kernel(
    core_ref, own_ref, got_ref, mixed_ref, q_ref, c_ref,
    gm_ref, p1_ref, enter_ref, first_p, decay,
):
    step = pl.program_id(0)
    slot = step ^ core_ref[0]
    count = c_ref.shape[0]
    growth = jnp.exp(c_ref[...])
    mask = own_blocks()
    for p in range(PAIRS):
        mixed = mixed_ref[:, q_cols(p)]
        grad = jnp.where(slot == 0, own_ref[:, q_cols(p)], got_ref[:, q_cols(p)]).astype(F32)
        scale = lax.rsqrt(head_sums(mixed * mixed) * (1.0 / HEAD) + head_floor)
        unit = mixed * scale
        back = scale * (grad - unit * (head_sums(grad * unit) * (1.0 / HEAD)))
        gm = back.astype(BF16)
        gm_ref[:, q_cols(p)] = gm
        grown = (q_ref[:, q_cols(p)].astype(F32) * spread_pair(growth, p)).astype(BF16)
        through = jnp.where(mask, t_dot(grown, gm), 0.0)

        @pl.when(step == 0)
        def _():
            first_p[p] = through
            decay[p] = jnp.broadcast_to(spread_pair(growth[count - 1 :], p), (8, WIDE))

        @pl.when(step == 1)
        def _():
            p1_ref[p] = through
            enter_ref[p] = (first_p[p] + decay[p][:1] * through).astype(BF16)


def back_kernel(
    core_ref, qkv_ref, c_ref, ct_ref, z_ref, gm_ref, s0_ref, s1_ref, e1_ref, p1_ref, cos_ref,
    sin_ref, front_ref, bias_ref, later, early,
):
    step = pl.program_id(0)
    count = c_ref.shape[0]
    rows = count // 2
    lane = iota((1, WIDE), 1)
    c, ct = c_ref[...], ct_ref[...]
    growth = jnp.exp(c)
    last = c[count - 1 :]
    tail = jnp.exp(last - c)
    last_row = iota((count, 1), 0) == count - 1
    per_head = jnp.zeros((count, WIDE), F32)
    key_sums, value_sums = [None, None], [None, None]
    cosine, sine_part = cos_ref[...], -sin_ref[...]

    @pl.when(step == 0)
    def _():
        later[...] = e1_ref[...].astype(F32)
        early[...] = s1_ref[...]

    @pl.when(step == 1)
    def _():
        early[...] = s0_ref[...].astype(F32)

    for p in range(PAIRS):
        held, ahead = early[p], later[p]
        query, key, value = qkv_ref[:, q_cols(p)], qkv_ref[:, k_cols(p)], qkv_ref[:, v_cols(p)]
        gm = gm_ref[:, q_cols(p)]
        query_t, gm_t = query.astype(F32).T.astype(BF16), gm.astype(F32).T.astype(BF16)
        d_query, d_key_t, d_value_t = [], [], []
        for h in range(2):
            by_rows, key_t, value_t = [], None, None
            for r in range(2):
                mine, span, upto, scores, decays = tile_of(qkv_ref, c, ct, r, rows, p, h)
                weighted = (scores * decays).astype(BF16)
                grad_weighted = dot_t(jnp.where(mine, gm[span], 0), value[:upto])
                grad_scores = (grad_weighted * decays).astype(BF16)
                by_rows.append(dot(grad_scores, key[:upto]))
                part = slice(HEAD * h, HEAD * (h + 1))
                one_key = dot(query_t[part, span], grad_scores)
                one_value = dot(gm_t[part, span], weighted)
                if r == 0:
                    key_t, value_t = one_key, one_value
                else:
                    key_t = jnp.concatenate([one_key[:, :rows] + key_t, one_key[:, rows:]], 1)
                    value_t = jnp.concatenate(
                        [one_value[:, :rows] + value_t, one_value[:, rows:]], 1
                    )
            d_query.append(jnp.concatenate(by_rows, 0))
            d_key_t.append(key_t)
            d_value_t.append(value_t)
        d_query = jnp.where(lane < HEAD, d_query[0], d_query[1])
        d_query = d_query + spread_pair(growth, p) * dot_t(gm, held.astype(BF16))
        ahead_low = ahead.astype(BF16)
        tails = spread_pair(tail, p)
        d_key_tail = tails * dot_t(value, ahead_low)
        d_key = jnp.concatenate(d_key_t, 0).T + d_key_tail
        d_value = jnp.concatenate(d_value_t, 0).T
        key_f = key.astype(F32)
        d_value = d_value + dot((key_f * tails).astype(BF16), ahead_low)
        total = spread_pair(jnp.exp(last), p)
        at_last = jnp.sum(key_f * d_key_tail, axis=0, keepdims=True)
        at_last = at_last + jnp.sum(ahead * held, axis=0, keepdims=True) * total
        grad_c = query.astype(F32) * d_query - key_f * d_key
        grad_c = grad_c + jnp.where(last_row, at_last, 0.0)
        to_head = iota((WIDE, WIDE), 1) == 2 * p + (iota((WIDE, WIDE), 0) >= HEAD)
        for third in thirds(grad_c):
            per_head = per_head + dot(third, to_head.astype(BF16))
        turned = turn(d_query, cosine, sine_part) * float(HEAD) ** (-0.5)
        front_ref[:, q_cols(p)] = turned.astype(BF16)
        if p < 2:
            key_sums[p], value_sums[p] = d_key, d_value
        else:
            key_sums[p - 2] = key_sums[p - 2] + d_key
            value_sums[p - 2] = value_sums[p - 2] + d_value

        @pl.when(step == 0)
        def _():
            later[p] = p1_ref[p] + total * ahead

    for p in range(2):
        front_ref[:, k_cols(p)] = turn(key_sums[p], cosine, sine_part).astype(BF16)
        front_ref[:, v_cols(p)] = value_sums[p].astype(BF16)
    upper = (iota((count, count), 0) <= iota((count, count), 1)).astype(BF16)
    grad_log = sum(dot(upper, third) for third in thirds(per_head))
    z = z_ref[...]
    grad_gate = jnp.where(lane < HALF, -grad_log / (GATE_TEMP * (1.0 + jnp.exp(-z))), 0.0)
    front_ref[:, N_FRONT - WIDE :] = grad_gate.astype(BF16)
    summed = jnp.broadcast_to(jnp.sum(grad_gate, axis=0, keepdims=True), (8, WIDE))

    @pl.when(step == 0)
    def _():
        bias_ref[...] = summed

    @pl.when(step == 1)
    def _():
        bias_ref[...] += summed


def front_back_kernel(
    core_ref, normed_ref, grad_ref, w_ref, own_ref, other_ref, gain_ref, bias_ref,
    part_ref, sent_ref, *refs,
):
    *outs, d_ref = refs
    grad = grad_ref[...]
    d = t_dot(normed_ref[...], grad)
    part = dot_t(grad, w_ref[...])
    count = own_ref.shape[0]
    part_ref[...] = part[:count]
    sent_ref[...] = part[count:].astype(BF16)
    d_gain = jnp.zeros((1, part.shape[1]), F32)
    for ref, rows in ((own_ref, part[:count]), (other_ref, part[count:])):
        x = ref[...].astype(F32)
        unit = x * lax.rsqrt(jnp.mean(x * x, axis=-1, keepdims=True) + epsilon)
        d_gain = d_gain + jnp.sum(rows * unit, axis=0, keepdims=True)
    main = N_FRONT - WIDE
    d_ref[:, :main] = d[:, :main].astype(BF16)
    rest = jnp.concatenate(
        [jnp.zeros((HALF, d_gain.shape[1]), F32), d_gain, gain_ref[:1]]
        + [jnp.zeros((WIDE - HALF - 2, d_gain.shape[1]), F32)],
        0,
    ).T
    d_ref[:, main:N_FRONT] = (d[:, main:] + rest + pltpu.roll(bias_ref[...], HALF + 2, 1)[:1]).astype(BF16)
    if len(outs) == 1:
        outs[0][...] = d_ref[...]
    else:
        own, over_dp, over_mid, first, second = outs
        rows = own.shape[1]
        for i in range(4):
            for ref, b in ((own, (0, 0)), (over_dp, (1, 0)), (over_mid, (0, 1))):
                ref[i] = d_ref[pl.ds(row_of(core_ref, i, b, rows), rows), :]
            far = first if i < 2 else second
            far[i % 2] = d_ref[pl.ds(row_of(core_ref, i, (1, 1), rows), rows), :]


def beside_each(refs):
    parts = [ref[...].reshape(-1, ref.shape[-1]) for ref in refs]
    return parts[0] if len(parts) == 1 else jnp.concatenate(parts, 1)


def far_kernel(core_ref, *refs):
    *far_refs, to_dp_ref, to_mid_ref = refs
    far = beside_each(far_refs)
    n = to_dp_ref.shape[0]
    to_dp_ref[...] = far[:n]
    to_mid_ref[...] = far[n:]


def sends_kernel(core_ref, *refs):
    *refs, over_dp_ref, over_mid_ref = refs
    n = len(refs) // 4
    to_mid, to_dp, over_dp, over_mid = [beside_each(refs[n * i : n * (i + 1)]) for i in range(4)]
    n = to_dp.shape[0]
    over_dp_ref[:n] = over_dp[:n]
    over_dp_ref[n:] = (over_dp[n:].astype(F32) + to_dp.astype(F32)).astype(BF16)
    over_mid_ref[:n] = (over_mid[:n].astype(F32) + to_mid.astype(F32)).astype(BF16)
    over_mid_ref[n:] = over_mid[n:]


def own_kernel(core_ref, dp_ref, mid_ref, *refs):
    *own_refs, sum_ref = refs
    whole = beside_each(own_refs).astype(F32) + beside_each([dp_ref]).astype(F32)
    whole = whole + beside_each([mid_ref]).astype(F32)
    sum_ref[...] = whole.astype(BF16).reshape(sum_ref.shape)


def sum_kernel(core_ref, own_ref, dp_ref, mid_ref, kept_ref, sent_ref):
    n = kept_ref.shape[0]
    whole = own_ref[...].astype(F32) + dp_ref[...].astype(F32) + mid_ref[...].astype(F32)
    kept_ref[...] = whole[:n]
    sent_ref[...] = whole[n:].astype(BF16)


def down_kernel(core_ref, hidden_ref, w_ref, out_ref):
    out_ref[...] = dot_t(hidden_ref[...], w_ref[...]).astype(BF16)


def output_kernel(core_ref, hidden_ref, w_ref, middle_ref, got_ref, out_ref):
    out = middle_ref[...] + dot_t(hidden_ref[...], w_ref[...])
    out_ref[...] = (out + got_ref[...].astype(F32)).astype(BF16)


def input_kernel(core_ref, part_ref, got_ref, middle_ref, x_ref, gains_ref, out_ref):
    x = x_ref[...].astype(F32)
    scale = inverse_rms(x)
    grad = (part_ref[...] + got_ref[...].astype(F32)) * gains_ref[:1]
    out_ref[...] = (middle_ref[...] + norm_back(grad, x * scale, scale)).astype(BF16)


def last_kernel(core_ref, pair_ref, got_ref, mine_ref, sent_ref):
    whole = (pair_ref[...] + got_ref[...].astype(F32)).astype(BF16)
    n = mine_ref.shape[0]
    low, high = whole[:n], whole[n:]
    mine_ref[...] = jnp.where(core_ref[0] == 0, low, high)
    sent_ref[...] = jnp.where(core_ref[0] == 0, high, low)


def unpack_kernel(
    core_ref, mine_ref, got_ref, q_ref, k_ref, v_ref, a_ref, gains_ref, bias_ref
):
    def both(ref, at):
        n = ref.shape[1] // 2
        a, b = mine_ref[:, at : at + n].astype(F32), got_ref[:, at : at + n].astype(F32)
        ref[:, :n] = jnp.where(core_ref[0] == 0, a, b)
        ref[:, n:] = jnp.where(core_ref[0] == 0, b, a)
        return at + n

    at = both(q_ref, 0)
    at = both(k_ref, at)
    at = both(v_ref, at)
    a = mine_ref[:, at:N_FRONT].astype(F32).T
    b = got_ref[:, at:N_FRONT].astype(F32).T
    low, high = jnp.where(core_ref[0] == 0, a, b), jnp.where(core_ref[0] == 0, b, a)
    a_ref[:HALF] = low[:HALF]
    a_ref[HALF:] = high[:HALF]
    gains_ref[...] = (a + b)[HALF : HALF + 8]
    bias_ref[:HALF] = low[HALF + 2 : 2 * HALF + 2]
    bias_ref[HALF:] = high[HALF + 2 : 2 * HALF + 2]


def call(kernel, ins, outs, name, microseconds, megabytes, steps=1, scratch=(), deps=(), reverse=False):
    once = pl.Buffered(1) if steps > 1 else None
    order = (lambda i, s: (1 - i) ^ s[0]) if reverse else (lambda i, s: i ^ s[0])

    def spec(kind, shape):
        zeros = (0,) * (len(shape) - 1)
        if kind == "all":
            return pl.BlockSpec(shape, lambda i, s: (0,) + zeros, pipeline_mode=once)
        if kind == "low":
            block = (shape[0] * 2 // steps,) + shape[1:]
            return pl.BlockSpec(block, lambda i, s: (jnp.minimum(i, steps // 2 - 1),) + zeros)
        if kind == "high":
            block = (shape[0] * 2 // steps,) + shape[1:]
            return pl.BlockSpec(block, lambda i, s: (jnp.maximum(i - steps // 2, 0),) + zeros)
        if kind in ("scalar", "any"):
            return SCALARS if kind == "scalar" else ANYWHERE
        if kind == "block":
            return pl.BlockSpec((shape[0] // 2,) + shape[1:], lambda i, s: (order(i, s),) + zeros)
        if kind == "rows":
            return pl.BlockSpec((shape[0] // steps,) + shape[1:], lambda i, s: (i,) + zeros)
        if kind == "entry":
            return pl.BlockSpec((None,) + shape[1:], lambda i, s: (order(i, s),) + zeros)
        if kind == "queries":
            return pl.BlockSpec((shape[0] // 2, N_Q), lambda i, s: (order(i, s), 0))
        if kind in ("own", "over_dp", "over_mid", "far"):
            a, b = int(kind in ("over_dp", "far")), int(kind in ("over_mid", "far"))
            block = (1, shape[1], 1) + shape[3:]
            return pl.BlockSpec(block, lambda i, s: (s[1] ^ a, 0, s[3] ^ b, 0, 0))
        block, index = kind
        return pl.BlockSpec(block, lambda i, s: index, pipeline_mode=once)

    where, *ins = ins
    moved = sum(v.size * v.dtype.itemsize for _, v in ins)
    return pl.pallas_call(
        without(kernel, 1 + len(ins), len(deps)),
        grid_spec=pltpu.PrefetchScalarGridSpec(
            num_scalar_prefetch=1,
            grid=(steps,),
            in_specs=[spec(kind, v.shape) for kind, v in ins] + [ANYWHERE] * len(deps),
            out_specs=[spec(kind, shape) for kind, shape, _ in outs],
            scratch_shapes=scratch,
        ),
        out_shape=[jax.ShapeDtypeStruct(shape, kind) for _, shape, kind in outs],
        compiler_params=pltpu.CompilerParams(
            dimension_semantics=("arbitrary",), vmem_limit_bytes=megabytes * 1024 * 1024
        ),
        cost_estimate=pl.CostEstimate(
            flops=int(microseconds * FLOPS), bytes_accessed=moved, transcendentals=0
        ),
        name=name,
    )(where, *[v for _, v in ins], *deps)


def piece(whole, a, b, low, count):
    sizes = (1, count, 1) + whole.shape[3:]
    return lax.dynamic_slice(whole, (a, low, b, 0, 0), sizes).reshape((count,) + whole.shape[3:])


def square_sends(over_dp, over_mid, to_mid, to_dp):
    half = to_mid.shape[0]
    send_mid = jnp.concatenate([over_mid[:half] + to_mid, over_mid[half:]], 0)
    send_dp = jnp.concatenate([over_dp[:half], over_dp[half:] + to_dp], 0)
    return send_dp, send_mid


def hi_swap(v, difference):
    return lax.ppermute(v, "hi", [(i, i ^ difference) for i in range(4)])


def sequence_weights(group_ids, loss_weights):
    group_count = loss_weights.shape[0]
    member = (group_ids[:, None] == jnp.arange(group_count, dtype=jnp.int32)[None, :]).astype(F32)
    counts = jnp.sum(member, axis=0)
    raw_weight = jnp.sum(member * loss_weights.astype(F32)[None, :], axis=1) / jnp.sum(
        member * counts[None, :], axis=1
    )
    return raw_weight * (group_ids.shape[0] / jnp.sum(raw_weight))


def shards(
    tokens,
    cotangent,
    group_ids,
    loss_weights,
    gain_one,
    w_query,
    w_key,
    w_value,
    w_gate,
    gate_bias,
    w_out,
    gain_two,
    w_gate_ff,
    w_up,
    w_down,
):
    count, width = tokens.shape
    both = 2 * count
    n_out, n_ff = w_out.shape[1] // 2, w_up.shape[1] // 2
    n_first = N_FRONT + n_out
    core, mid = lax.axis_index("core"), lax.axis_index("mid")
    dp, hi = lax.axis_index("dp"), lax.axis_index("hi")
    where = jnp.stack([core, dp, hi, mid]).astype(jnp.int32)
    small = small_slice()
    sequence = lax.axis_index(ALL) // SPAN
    square = (PAIRS, WIDE, WIDE)

    packed = pack(
        core, w_query, w_key, w_value, w_gate.T, gain_one[None], gain_two[None], w_out, w_gate_ff,
        w_up, w_down.T,
    )
    first = place(core, packed[0], swap(packed[2], "core"))
    rest = place(core, packed[1], swap(packed[3], "core"))
    w_rest = gather(rest)
    if small:
        pair = jnp.stack([first, hi_swap(first, 2)])
        own = jnp.concatenate([pair, hi_swap(pair, 1)], 0)
        over_dp, over_mid = swap(own, "dp"), swap(own, "mid")
        pieces = (own, over_dp, over_mid, swap(over_dp[:2], "mid"), swap(over_mid[2:], "dp"))
    else:
        pieces = (gather(first),)
    other_tokens, other_cotangent = swap(tokens, "core"), swap(cotangent, "core")

    block = 2 * mid + (core ^ jnp.arange(2))
    positions = (block[:, None] * count + jnp.arange(count)[None, :]).reshape(-1)
    frequency = ROPE_BASE ** (-jnp.arange(HEAD // 2, dtype=F32) / (HEAD // 2))
    angles = positions.astype(F32)[:, None] * frequency[None, :]
    cosine, sine_part = jnp.cos(angles), jnp.sin(angles)
    cosine = jnp.concatenate([cosine] * 4, 1)
    sine_part = jnp.concatenate([-sine_part, sine_part] * 2, 1)
    own_bias = lax.dynamic_slice_in_dim(gate_bias, core * HALF, HALF)
    own_bias = jnp.concatenate([own_bias, jnp.zeros((WIDE - HALF,), F32)])[None, :]
    w_front, w_half, normed_one, qkv, c, ct, z, gains, update, leaving = call(
        front_kernel,
        [where, ("all", tokens), ("all", other_tokens), ("all", own_bias)]
        + [("block", cosine), ("block", sine_part)]
        + [("all", v) for v in pieces],
        [("all", (width, N_FRONT), BF16), ("all", (width, n_out), BF16)]
        + [("block", (both, width), BF16), ("block", (both, 2 * N_Q), BF16)]
        + [("block", (both, WIDE), F32), ("entry", (2, HALF, count), F32)]
        + [("block", (both, WIDE), F32), ("all", (8, width), F32)]
        + [("all", square, F32), ("all", square, BF16)],
        "front",
        14,
        24,
        2,
        [pltpu.VMEM(square, F32)],
    )
    state_0 = lax.ppermute(leaving, "mid", [(0, 1)])
    w_other = swap(w_half, "core")
    mixed_out, normed_own, normed_sent, state_1 = call(
        mix_kernel,
        [where, ("block", qkv), ("block", c), ("entry", ct), ("all", state_0), ("all", update)],
        [("block", (both, N_Q), F32)]
        + [("all", (count, N_Q), BF16)] * 2
        + [("all", square, F32)],
        "mix",
        11,
        16,
        2,
        [pltpu.VMEM(square, F32)],
    )
    normed_got = swap(normed_sent, "core")
    middle, normed_two_own = call(
        out_kernel,
        [where]
        + [("all", v) for v in (normed_own, normed_got, w_half, w_other, tokens, gains)],
        [("all", (count, width), F32), ("all", (count, width), BF16)],
        "out",
        4,
        16,
    )
    normed_two_other = swap(normed_two_own, "core")
    seq_weights = sequence_weights(group_ids, loss_weights)
    own_weight = jnp.sum(jnp.where(jnp.arange(group_ids.shape[0]) == sequence, seq_weights, 0.0))
    own_weight = own_weight.reshape(1)
    far = [("any", (width // 8, 2 * n_ff), BF16)] * 2 if small else []
    hidden, w_down_t, d_ff, d_down, part_kept, part_sent, *ff_sends = call(
        functools.partial(ff_kernel, small),
        [where, ("scalar", own_weight)]
        + [("all", v) for v in (normed_two_own, normed_two_other, cotangent, other_cotangent)]
        + [("any", w_rest)],
        [("any", (both, n_ff), BF16), ("any", (width, n_ff), BF16)]
        + [("any", (width, 2 * n_ff), BF16), ("any", (width, n_ff), BF16)]
        + [("all", (count, width), F32), ("all", (count, width), BF16)]
        + far,
        "ff",
        36,
        52,
        scratch=[pltpu.VMEM((width, n_ff), BF16)] * 3
        + [pltpu.VMEM((both, n_ff), BF16), pltpu.VMEM((both, 2 * n_ff), BF16)]
        + [pltpu.VMEM((both, width), BF16), pltpu.VMEM((width, 2 * n_ff), BF16)]
        + [pltpu.VMEM((width, n_ff), BF16)]
        + [pltpu.SemaphoreType.DMA((3,)), pltpu.SemaphoreType.DMA((8,))],
    )
    if small:
        d_ff = d_ff.reshape(2, 4, 2, -1, 2 * n_ff)
        ff_one = swap(ff_sends[0], "dp"), swap(ff_sends[1], "mid")
        down_hi = d_down.reshape(4, -1, n_ff)
        down_hi = lax.psum_scatter(down_hi, "hi", scatter_dimension=0, tiled=False)
        down_hi = down_hi.reshape(2, 1, 2, -1, n_ff)
    else:
        rest_sum = scatter(d_down)
        ff_one = []
    part_got = swap(part_sent, "core")
    down_rows = ((count, n_ff), (1, 0)), ((count, n_ff), (0, 0))
    (out_sent,) = call(
        down_kernel,
        [where, (down_rows[0], hidden), ("all", w_down_t)],
        [("all", (count, width), BF16)],
        "out_sent",
        5,
        16,
    )
    grad_middle, d_gain_two, grad_own, grad_sent, d_out_kept, d_out_sent = call(
        middle_kernel,
        [where, ("scalar", own_weight)]
        + [("all", v) for v in (part_kept, part_got, cotangent, middle, gains, w_half, w_other)]
        + [("all", v) for v in (normed_own, normed_got)],
        [("all", (count, width), F32), ("all", (8, width), F32)]
        + [("all", (count, N_Q), BF16)] * 2
        + [("all", (width, n_out), BF16)] * 2,
        "middle",
        8,
        24,
        deps=(out_sent,),
    )
    grad_got = swap(grad_sent, "core")
    d_out_got = swap(d_out_sent, "core")
    grad_mixed, through, entering = call(
        head_back_kernel,
        [where, ("all", grad_own), ("all", grad_got), ("block", mixed_out), ("queries", qkv)]
        + [("block", c)],
        [("block", (both, N_Q), BF16), ("all", square, F32), ("all", square, BF16)],
        "head_back",
        8,
        16,
        2,
        [pltpu.VMEM(square, F32), pltpu.VMEM((PAIRS, 8, WIDE), F32)],
        deps=ff_one,
    )
    state_last = lax.ppermute(entering, "mid", [(1, 0)])
    (d_out,) = call(
        add_kernel,
        [where, ("all", d_out_kept), ("all", d_out_got)],
        [("all", (width, n_out), BF16)],
        "out_sum",
        2,
        16,
        deps=(entering,),
    )
    if small:
        d_out = d_out.reshape(2, 4, 2, -1, n_out)
        n_wide = 2 * n_ff + n_out
        out_sends = call(
            far_kernel,
            [where, ("far", d_out)],
            [("all", (width // 8, n_out), BF16)] * 2,
            "out_far",
            1.5,
            16,
        )
        out_one = swap(out_sends[0], "dp"), swap(out_sends[1], "mid")
    else:
        wide_sends = out_sends = [d_out]
        wide_sum = jnp.concatenate([scatter(d_ff), scatter(d_out)], 1)
    if small:
        wide_sends = call(
            sends_kernel,
            [where]
            + [("all", v) for pair in zip(ff_one, out_one) for v in pair]
            + [(kind, v) for kind in ("over_dp", "over_mid") for v in (d_ff, d_out)],
            [("all", (width // 4, n_wide), BF16)] * 2,
            "wide_sends",
            3.5,
            20,
            deps=(state_last,),
        )
        wide_got = swap(wide_sends[0], "dp"), swap(wide_sends[1], "mid")
    grad_front, d_bias = call(
        back_kernel,
        [where, ("block", qkv), ("block", c), ("entry", ct), ("block", z), ("block", grad_mixed)]
        + [("all", v) for v in (state_0, state_1, state_last, through)]
        + [("block", cosine), ("block", sine_part)],
        [("block", (both, N_FRONT), BF16), ("all", (8, WIDE), F32)],
        "back",
        20,
        24,
        2,
        [pltpu.VMEM(square, F32), pltpu.VMEM(square, F32)],
        deps=wide_sends,
        reverse=True,
    )
    if small:
        shapes = [(4, width // 16, N_FRONT)] * 3 + [(2, width // 16, N_FRONT)] * 2
    else:
        shapes = [(width, N_FRONT)]
    part_kept, part_sent, *d_first = call(
        front_back_kernel,
        [where]
        + [("all", v) for v in (normed_one, grad_front, w_front, tokens, other_tokens)]
        + [("all", v) for v in (d_gain_two, d_bias)],
        [("all", (count, width), F32), ("all", (count, width), BF16)]
        + [("all", shape, BF16) for shape in shapes],
        "front_back",
        12,
        32,
        scratch=[pltpu.VMEM((width, N_FRONT), BF16)],
    )
    part_got = swap(part_sent, "core")

    def add_input(deps):
        return call(
            input_kernel,
            [where]
            + [("all", v) for v in (part_kept, part_got, grad_middle, tokens, gains)],
            [("all", (count, width), BF16)],
            "grad_input",
            4.5,
            16,
            deps=deps,
        )

    out_got = swap(out_sent, "core")

    def add_output(deps):
        return call(
            output_kernel,
            [where, (down_rows[1], hidden), ("all", w_down_t)]
            + [("all", v) for v in (middle, out_got)],
            [("all", (count, width), BF16)],
            "output",
            5.5,
            16,
            deps=deps,
        )

    if small:
        own, over_dp, over_mid, far_0, far_1 = d_first
        one = swap(far_0, "dp"), swap(far_1, "mid")
        (wide_hi,) = call(
            own_kernel,
            [where] + [("all", v) for v in wide_got] + [("own", d_ff), ("own", d_out)],
            [("all", (4, width // 16, n_wide), BF16)],
            "wide_own",
            3.5,
            20,
            deps=(far_0,),
        )
        wide_sum = lax.psum_scatter(wide_hi, "hi", scatter_dimension=0, tiled=False)
        rest_sends = call(
            far_kernel,
            [where, ("far", down_hi)],
            [("all", (width // 32, n_ff), BF16)] * 2,
            "rest_far",
            1.5,
            16,
            deps=(wide_hi,),
        )
        rest_one = swap(rest_sends[0], "dp"), swap(rest_sends[1], "mid")
        sends = call(
            sends_kernel,
            [where] + [("all", v) for v in (*one, over_dp, over_mid)],
            [("all", (width // 4, N_FRONT), BF16)] * 2,
            "front_sends",
            2,
            16,
            deps=(wide_hi, *rest_sends),
        )
        front_got = swap(sends[0], "dp"), swap(sends[1], "mid")
        rest_sends = call(
            sends_kernel,
            [where]
            + [("all", v) for v in rest_one]
            + [("over_dp", down_hi), ("over_mid", down_hi)],
            [("all", (width // 16, n_ff), BF16)] * 2,
            "rest_sends",
            2,
            16,
            deps=(sends[0],),
        )
        rest_got = swap(rest_sends[0], "dp"), swap(rest_sends[1], "mid")
        (output,) = add_output((sends[0],))
        (grad_input,) = add_input((sends[0],))
        kept, sent = call(
            sum_kernel,
            [where] + [("all", v.reshape(own.shape)) for v in (own, *front_got)],
            [("all", (2,) + own.shape[1:], F32), ("all", (2,) + own.shape[1:], BF16)],
            "first_sum",
            2,
            16,
            deps=(grad_input, output, *rest_sends),
        )
        pair = kept + hi_swap(sent, 1).astype(F32)
        last, last_got = pair[0], hi_swap(pair[1].astype(BF16), 2)
        (rest_sum,) = call(
            own_kernel,
            [where] + [("all", v) for v in rest_got] + [("own", down_hi)],
            [("all", (width // 16, n_ff), BF16)],
            "rest_own",
            1.5,
            16,
            deps=(kept,),
        )
    else:
        last = scatter(d_first[0]).astype(F32)
        last_got = jnp.zeros_like(last, BF16)
        (output,), (grad_input,) = add_output(()), add_input(())

    def owned(rows):
        n = rows.shape[0] // 2
        mine = lax.dynamic_slice_in_dim(rows, core * n, n)
        return mine, swap(lax.dynamic_slice_in_dim(rows, (1 - core) * n, n), "core")

    outs = []
    for v in (rest_sum, wide_sum):
        mine, theirs = owned(v)
        outs.append((mine, theirs))
    n = last.shape[0] // 2
    mine, sent = call(
        last_kernel,
        [where, ("all", last), ("all", last_got)],
        [("all", (n, N_FRONT), BF16)] * 2,
        "last",
        1.5,
        16,
        deps=tuple(theirs for _, theirs in outs),
    )
    theirs = swap(sent, "core")
    ends = [(0, 0, n_ff), (1, 0, n_ff), (1, n_ff, 2 * n_ff), (1, 2 * n_ff, 2 * n_ff + n_out)]
    g_down, g_gate_ff, g_up, g_out = [
        beside(core, *[v[:, low:high] for v in outs[i]]) for i, low, high in ends
    ]
    g_query, g_key, g_value, g_gate, g_gains, g_bias = call(
        unpack_kernel,
        [where, ("all", mine), ("all", theirs)],
        [("all", (n, 2 * N_Q), F32)]
        + [("all", (n, 2 * N_K), F32)] * 2
        + [("all", (HEADS, n), F32), ("all", (8, n), F32), ("all", (HEADS, n), F32)],
        "unpack",
        1.5,
        16,
    )
    return (
        output,
        grad_input,
        g_gains[0],
        g_query,
        g_key,
        g_value,
        g_gate.T,
        g_bias[:, 0],
        g_out,
        g_gains[1],
        g_gate_ff,
        g_up,
        g_down.T,
    )


def solution(mesh):
    devices = mesh.devices
    fine = Mesh(
        devices.reshape(devices.shape[0], devices.shape[1] // SPAN, SPAN // 2, 2), ALL
    )
    rows, columns, split = P(ALL, None), P(None, ALL), P(ALL)
    in_specs = (rows, rows, P(), P(), split) + (rows,) * 4 + (P(), rows, split, rows, rows, columns)
    out_specs = (rows, rows, split) + (rows,) * 4 + (P(), rows, split, rows, rows, columns)
    return jax.shard_map(shards, mesh=fine, in_specs=in_specs, out_specs=out_specs, check_vma=False)
```

```python
import functools

import jax
import jax.numpy as jnp
from jax import lax
from jax.experimental import pallas as pl
from jax.experimental.pallas import tpu as pltpu
from jax.sharding import Mesh, PartitionSpec as P

HEADS = 16
HEAD = 64
KVH = 2
LATENT = 256
SPAN = 4

epsilon = 1e-05
head_floor = 0.25
ROPE_BASE = 10000.0
GATE_TEMP = 16.0

CHIPS = ("dp", "hi", "mid")
ALL = ("dp", "hi", "mid", "core")
F32 = jnp.float32
BF16 = jnp.bfloat16


def swap(v, axis):
    return lax.ppermute(v, axis, [(0, 1), (1, 0)])


def place(bit, mine, theirs):
    return jnp.where(
        bit == 0, jnp.concatenate([mine, theirs], 0), jnp.concatenate([theirs, mine], 0)
    )


def small_slice():
    return lax.axis_size("dp") == 2 and lax.axis_size("hi") == 4


def gather(part):
    return lax.all_gather(part, CHIPS, axis=0, tiled=True)


def add3(a, b, c):
    return a.astype(F32) + b.astype(F32) + c.astype(F32)


def scatter(whole):
    return lax.psum_scatter(whole, CHIPS, scatter_dimension=0, tiled=True)


def beside(core, mine, theirs):
    return jnp.where(
        core == 0, jnp.concatenate([mine, theirs], 1), jnp.concatenate([theirs, mine], 1)
    ).astype(F32)


HALF = HEADS // 2
PAIRS = HALF // 2
WIDE = 2 * HEAD
N_Q = HALF * HEAD
N_K = N_Q // 2
N_FRONT = N_Q + 2 * N_K + WIDE
FLOPS = 0.55e9


def dot(left, right):
    return jnp.dot(left, right, preferred_element_type=F32)


def dot_t(left, right):
    return lax.dot_general(left, right, (((1,), (1,)), ((), ())), preferred_element_type=F32)


def t_dot(left, right):
    return lax.dot_general(left, right, (((0,), (0,)), ((), ())), preferred_element_type=F32)


def thirds(v):
    high = v.astype(BF16)
    rest = v - high.astype(F32)
    middle = rest.astype(BF16)
    return high, middle, (rest - middle.astype(F32)).astype(BF16)


def halves(v):
    high = v.astype(BF16)
    return high, (v - high.astype(F32)).astype(BF16)


def iota(shape, axis):
    return lax.broadcasted_iota(jnp.int32, shape, axis)


def spread_pair(per_head, p):
    lane = iota((1, WIDE), 1)
    return jnp.where(
        lane < HEAD, per_head[:, 2 * p : 2 * p + 1], per_head[:, 2 * p + 1 : 2 * p + 2]
    )


def head_sums(v):
    ones = own_blocks().astype(BF16)
    high = v.astype(BF16)
    return dot(high, ones) + dot((v - high.astype(F32)).astype(BF16), ones)


def turn(v, cosine, sine_part):
    lane = iota((1, WIDE), 1)
    other = jnp.where(
        lane % HEAD < HEAD // 2,
        pltpu.roll(v, WIDE - HEAD // 2, 1),
        pltpu.roll(v, HEAD // 2, 1),
    )
    return v * cosine + other * sine_part


def own_blocks():
    return (iota((WIDE, WIDE), 0) < HEAD) == (iota((WIDE, WIDE), 1) < HEAD)


def q_cols(p):
    return slice(WIDE * p, WIDE * (p + 1))


def k_cols(p):
    return slice(N_Q + WIDE * (p % 2), N_Q + WIDE * (p % 2 + 1))


def v_cols(p):
    return slice(N_Q + N_K + WIDE * (p % 2), N_Q + N_K + WIDE * (p % 2 + 1))


def without(kernel, start, count):
    return lambda *refs: kernel(*refs[:start], *refs[start + count :])


ANYWHERE = pl.BlockSpec(memory_space=pl.ANY)
SCALARS = pl.BlockSpec(memory_space=pltpu.SMEM)


def inverse_rms(values, added=epsilon):
    return lax.rsqrt(jnp.mean(values * values, axis=-1, keepdims=True) + added)


def norm_back(grad_unit, unit_rows, scale_rows):
    return scale_rows * (
        grad_unit - unit_rows * jnp.mean(grad_unit * unit_rows, axis=-1, keepdims=True)
    )


def row_of(where, i, b, rows):
    hi = where[2] ^ (0, 2, 1, 3)[i]
    index = ((where[1] ^ b[0]) * 4 + hi) * 2 + (where[3] ^ b[1])
    return pl.multiple_of(index * rows, rows)


def pack_kernel(core_ref, q_ref, k_ref, v_ref, a_ref, g1_ref, g2_ref, o_ref, f_ref, u_ref, d_ref, *outs):
    def put(out, at, v):
        out[:, at : at + v.shape[1]] = v
        return at + v.shape[1]

    rows = q_ref.shape[0]
    lane = iota((1, WIDE), 1)
    gates = a_ref[...].astype(F32)
    gains = [g1_ref[...].astype(F32), g2_ref[...].astype(F32)]
    for i in range(2):
        front, rest = outs[2 * i : 2 * i + 2]
        mine = core_ref[0] if i == 0 else 1 - core_ref[0]

        def half(ref):
            n = ref.shape[1] // 2
            return jnp.where(mine == 0, ref[:, :n], ref[:, n:])

        at = put(front, 0, half(q_ref))
        at = put(front, at, half(k_ref))
        at = put(front, at, half(v_ref))
        some = jnp.where(mine == 0, gates[:HALF], gates[HALF:])
        small = jnp.concatenate([some, *gains, jnp.zeros((WIDE - HALF - 2, rows), F32)], 0)
        at = put(front, at, small.T.astype(BF16))
        put(front, at, half(o_ref))
        at = put(rest, 0, half(f_ref))
        at = put(rest, at, half(u_ref))
        put(rest, at, half(d_ref))


def pack(core, *weights):
    rows = weights[0].shape[0]
    n_out, n_ff = weights[6].shape[1] // 2, weights[7].shape[1] // 2
    return pl.pallas_call(
        pack_kernel,
        in_specs=[pl.BlockSpec(memory_space=pltpu.SMEM)]
        + [pl.BlockSpec(memory_space=pltpu.VMEM)] * len(weights),
        out_specs=[pl.BlockSpec(memory_space=pltpu.VMEM)] * 4,
        out_shape=[
            jax.ShapeDtypeStruct((rows, n), BF16) for n in (N_FRONT + n_out, 3 * n_ff)
        ]
        * 2,
        name="pack",
    )(core.reshape(1).astype(jnp.int32), *weights)


def front_kernel(
    core_ref, own_ref, other_ref, bias_ref, cos_ref, sin_ref, *refs
):
    *pieces, w_ref, out_ref = refs[:-9]
    normed_ref, qkv_ref, c_ref, ct_ref, z_ref, gains_ref, u_ref, leave_ref, first_u = refs[-9:]
    step = pl.program_id(0)
    slot = step ^ core_ref[0]

    @pl.when(step == 0)
    def _():
        if len(pieces) == 1:
            w_ref[...] = pieces[0][:, :N_FRONT]
            out_ref[...] = pieces[0][:, N_FRONT:]
        else:
            own, over_dp, over_mid, first, second = pieces
            rows = own.shape[1]
            for i in range(4):
                far = first[i] if i < 2 else second[i - 2]
                for v, b in ((own[i], (0, 0)), (over_dp[i], (1, 0)), (over_mid[i], (0, 1)), (far, (1, 1))):
                    to = pl.ds(row_of(core_ref, i, b, rows), rows)
                    w_ref[to, :] = v[:, :N_FRONT]
                    out_ref[to, :] = v[:, N_FRONT:]

    x = jnp.where(slot == 0, own_ref[...], other_ref[...]).astype(F32)
    gains = w_ref[:, N_FRONT - WIDE :].astype(F32).T[HALF : HALF + 8]
    gains_ref[...] = gains
    scale = lax.rsqrt(jnp.mean(x * x, axis=-1, keepdims=True) + epsilon)
    normed = (x * scale * gains[:1]).astype(BF16)
    normed_ref[...] = normed
    pre = dot(normed, w_ref[...])
    cosine, sine_part = cos_ref[...], sin_ref[...]
    for p in range(PAIRS):
        turned = turn(pre[:, q_cols(p)], cosine, sine_part)
        qkv_ref[:, q_cols(p)] = (turned * float(HEAD) ** (-0.5)).astype(BF16)
    for p in range(PAIRS // 2):
        qkv_ref[:, k_cols(p)] = turn(pre[:, k_cols(p)], cosine, sine_part).astype(BF16)
        qkv_ref[:, v_cols(p)] = pre[:, v_cols(p)].astype(BF16)
    z = pre[:, N_FRONT - WIDE :] + bias_ref[...]
    z_ref[...] = z
    small = jnp.exp(-jnp.abs(z))
    log_part = jnp.where(
        small < 0.01, small * (1.0 - small * (0.5 - small * (1.0 / 3.0))), jnp.log(1.0 + small)
    )
    softplus = jnp.maximum(z, 0.0) + log_part
    log_decay = jnp.where(iota((1, WIDE), 1) < HALF, -softplus / GATE_TEMP, 0.0)
    count = x.shape[0]
    lower = (iota((count, count), 0) >= iota((count, count), 1)).astype(BF16)
    c = sum(dot(lower, third) for third in thirds(log_decay))
    c_ref[...] = c
    ct_ref[...] = c.T[:HALF]
    last = c[count - 1 :]
    tail = jnp.exp(last - c)
    mask = own_blocks()
    for p in range(PAIRS):
        scaled = (qkv_ref[:, k_cols(p)].astype(F32) * spread_pair(tail, p)).astype(BF16)
        update = jnp.where(mask, t_dot(scaled, qkv_ref[:, v_cols(p)]), 0.0)

        @pl.when(step == 0)
        def _():
            u_ref[p] = update
            first_u[p] = update

        @pl.when(step == 1)
        def _():
            grown = spread_pair(jnp.exp(last), p) * first_u[p] + update
            leave_ref[p] = grown.astype(BF16)


def tile_of(qkv_ref, c, ct, r, rows, p, h):
    lane = iota((1, WIDE), 1)
    mine = (lane < HEAD) if h == 0 else (lane >= HEAD)
    span = slice(rows * r, rows * (r + 1))
    upto = rows * (r + 1)
    query = jnp.where(mine, qkv_ref[span, q_cols(p)], 0)
    scores = dot_t(query, qkv_ref[:upto, k_cols(p)])
    head = 2 * p + h
    differences = c[span, head : head + 1] - ct[head : head + 1, :upto]
    causal = iota((rows, upto), 0) + rows * r >= iota((rows, upto), 1)
    decays = jnp.exp(jnp.where(causal, differences, -1e30))
    return mine, span, upto, scores, decays


def mix_kernel(
    core_ref, qkv_ref, c_ref, ct_ref, s0_ref, u_ref,
    mixed_ref, own_ref, sent_ref, s1_ref, state,
):
    step = pl.program_id(0)
    slot = step ^ core_ref[0]
    count = c_ref.shape[0]
    rows = count // 2
    lane = iota((1, WIDE), 1)
    c, ct = c_ref[...], ct_ref[...]

    @pl.when(step == 0)
    def _():
        state[...] = s0_ref[...].astype(F32)

    growth = jnp.exp(c)
    for p in range(PAIRS):
        held = state[p]
        carried = spread_pair(growth, p) * dot(qkv_ref[:, q_cols(p)], held.astype(BF16))
        for r in range(2):
            parts = []
            for h in range(2):
                mine, span, upto, scores, decays = tile_of(qkv_ref, c, ct, r, rows, p, h)
                weighted = (scores * decays).astype(BF16)
                parts.append(dot(weighted, qkv_ref[:upto, v_cols(p)]))
            mixed = jnp.where(lane < HEAD, parts[0], parts[1]) + carried[span]
            mixed_ref[span, q_cols(p)] = mixed
            scale = lax.rsqrt(head_sums(mixed * mixed) * (1.0 / HEAD) + head_floor)
            normed = (mixed * scale).astype(BF16)

            @pl.when(slot == 0)
            def _():
                own_ref[span, q_cols(p)] = normed

            @pl.when(slot == 1)
            def _():
                sent_ref[span, q_cols(p)] = normed

        @pl.when(step == 0)
        def _():
            grown = spread_pair(growth[count - 1 :], p) * held + u_ref[p]
            s1_ref[p] = grown
            state[p] = grown


def out_kernel(
    core_ref, own_ref, got_ref, half_ref, other_ref, x_ref, gains_ref, middle_ref, normed_ref
):
    core = core_ref[0]
    n = own_ref.shape[1]
    mine = pl.ds(pl.multiple_of(core * n, n), n)
    theirs = pl.ds(pl.multiple_of((1 - core) * n, n), n)
    own, got = own_ref[...], got_ref[...]
    a = dot(own, half_ref[mine, :]) + dot(got, half_ref[theirs, :])
    b = dot(own, other_ref[mine, :]) + dot(got, other_ref[theirs, :])
    attention = jnp.where(core == 0, jnp.concatenate([a, b], 1), jnp.concatenate([b, a], 1))
    middle = x_ref[...].astype(F32) + attention
    middle_ref[...] = middle
    normed_ref[...] = (middle * inverse_rms(middle) * gains_ref[1:2]).astype(BF16)


def ff_kernel(
    small, where_ref, weight_ref, own_ref, other_ref, cot_ref, cot_other_ref, w_ref,
    hidden_out, down_out, d_ff_out, d_down_out, kept_ref, sent_ref, *refs,
):
    *far_outs, wide, down, hidden, grads, branch, d_ff, d_down, in_sems, out_sems = refs
    count = own_ref.shape[0]
    n = down.shape[1]
    loads = [
        pltpu.make_async_copy(w_ref.at[:, pl.ds(at, to.shape[1])], to, in_sems.at[i])
        for i, (to, at) in enumerate(((wide, 0), (down, 2 * n)))
    ]
    for load in loads:
        load.start()
    stores = []

    def store(piece, to):
        stores.append(pltpu.make_async_copy(piece, to, out_sems.at[len(stores)]))
        stores[-1].start()

    for i, ref in enumerate((cot_ref, cot_other_ref)):
        scaled = (ref[...].astype(F32) * weight_ref[0]).astype(BF16)
        branch[count * i : count * (i + 1), :] = scaled
    for i, ref in enumerate((own_ref, other_ref)):
        at = slice(count * i, count * (i + 1))
        if i == 0:
            loads[0].wait()
        pre = dot(ref[...], wide[...])
        g, u = pre[:, :n], pre[:, n:]
        sigmoid = 1.0 / (1.0 + jnp.exp(-g))
        silu = g * sigmoid
        slope = u * sigmoid * (1.0 + g * (1.0 - sigmoid))
        hidden[at, :] = (silu * u).astype(BF16)
        if i == 0:
            loads[1].wait()
        grad = dot(branch[at, :], down[...])
        grads[at, :n] = (grad * slope).astype(BF16)
        grads[at, n:] = (grad * silu).astype(BF16)

    store(hidden, hidden_out)
    store(down, down_out)

    def part(i):
        at = slice(count * i, count * (i + 1))
        return dot_t(grads[at, :], wide[...])

    width = own_ref.shape[1]
    block = 512

    @pl.loop(0, width // block)
    def _(j):
        at = pl.ds(pl.multiple_of(j * block, block), block)
        d = t_dot(own_ref[:, at], grads[:count, :]) + t_dot(other_ref[:, at], grads[count:, :])
        d_ff[at, :] = d.astype(BF16)

    store(d_ff, d_ff_out)
    if small:
        rows = width // 16
        for i in range(4):
            index = ((1 - where_ref[1]) * 4 + i) * 2 + 1 - where_ref[3]
            from_ = pl.ds(pl.multiple_of(index * rows, rows), rows)
            store(d_ff.at[from_, :], far_outs[i // 2].at[pl.ds(rows * (i % 2), rows), :])

    chunk = width // 8
    order = [4 * (j % 2) + j // 2 if small else j for j in range(8)]
    for j in range(0, 8, 4):
        columns = [branch[:, chunk * i : chunk * (i + 1)] for i in order[j : j + 4]]
        d = t_dot(jnp.concatenate(columns, 1), hidden[...])
        d_down[chunk * j : chunk * (j + 4), :] = d.astype(BF16)
    store(d_down, d_down_out)
    sent_ref[...] = part(1).astype(BF16)
    kept_ref[...] = part(0)
    for one in stores:
        one.wait()


def middle_kernel(
    core_ref, weight_ref, part_ref, got_ref, cot_ref, middle_ref, gains_ref, half_ref, other_ref,
    normed_ref, normed_got_ref, grad_middle_ref, gain_ref, own_ref, sent_ref, out_kept_ref,
    out_sent_ref,
):
    core = core_ref[0]
    part = part_ref[...] + got_ref[...].astype(F32)
    middle = middle_ref[...]
    scale = inverse_rms(middle)
    unit = middle * scale
    gain_ref[...] = jnp.broadcast_to(jnp.sum(part * unit, axis=0, keepdims=True), gain_ref.shape)
    grad_middle = cot_ref[...].astype(F32) * weight_ref[0]
    grad_middle = grad_middle + norm_back(part * gains_ref[1:2], unit, scale)
    grad_middle_ref[...] = grad_middle
    attention = grad_middle.astype(BF16)
    n = half_ref.shape[1]
    low, high = attention[:, :n], attention[:, n:]
    kept, rest = jnp.where(core == 0, low, high), jnp.where(core == 0, high, low)
    pairs = ((sent_ref, normed_got_ref, 1 - core), (own_ref, normed_ref, core))
    for ref, heads_ref, at in pairs:
        rows = pl.ds(pl.multiple_of(at * n, n), n)
        ref[...] = (dot_t(kept, half_ref[rows, :]) + dot_t(rest, other_ref[rows, :])).astype(BF16)
        heads = heads_ref[...]
        out_kept_ref[rows, :] = t_dot(heads, kept).astype(BF16)
        out_sent_ref[rows, :] = t_dot(heads, rest).astype(BF16)


def add_kernel(core_ref, a_ref, b_ref, sum_ref):
    sum_ref[...] = (a_ref[...].astype(F32) + b_ref[...].astype(F32)).astype(BF16)


def head_back_kernel(
    core_ref, own_ref, got_ref, mixed_ref, q_ref, c_ref,
    gm_ref, p1_ref, enter_ref, first_p, decay,
):
    step = pl.program_id(0)
    slot = step ^ core_ref[0]
    count = c_ref.shape[0]
    growth = jnp.exp(c_ref[...])
    mask = own_blocks()
    for p in range(PAIRS):
        mixed = mixed_ref[:, q_cols(p)]
        grad = jnp.where(slot == 0, own_ref[:, q_cols(p)], got_ref[:, q_cols(p)]).astype(F32)
        scale = lax.rsqrt(head_sums(mixed * mixed) * (1.0 / HEAD) + head_floor)
        unit = mixed * scale
        back = scale * (grad - unit * (head_sums(grad * unit) * (1.0 / HEAD)))
        gm = back.astype(BF16)
        gm_ref[:, q_cols(p)] = gm
        grown = (q_ref[:, q_cols(p)].astype(F32) * spread_pair(growth, p)).astype(BF16)
        through = jnp.where(mask, t_dot(grown, gm), 0.0)

        @pl.when(step == 0)
        def _():
            first_p[p] = through
            decay[p] = jnp.broadcast_to(spread_pair(growth[count - 1 :], p), (8, WIDE))

        @pl.when(step == 1)
        def _():
            p1_ref[p] = through
            enter_ref[p] = (first_p[p] + decay[p][:1] * through).astype(BF16)


def back_kernel(
    core_ref, qkv_ref, c_ref, ct_ref, z_ref, gm_ref, s0_ref, s1_ref, e1_ref, p1_ref, cos_ref,
    sin_ref, front_ref, bias_ref, later, early,
):
    step = pl.program_id(0)
    count = c_ref.shape[0]
    rows = count // 2
    lane = iota((1, WIDE), 1)
    c, ct = c_ref[...], ct_ref[...]
    growth = jnp.exp(c)
    last = c[count - 1 :]
    tail = jnp.exp(last - c)
    last_row = iota((count, 1), 0) == count - 1
    per_head = jnp.zeros((count, WIDE), F32)
    key_sums, value_sums = [None, None], [None, None]
    cosine, sine_part = cos_ref[...], -sin_ref[...]

    @pl.when(step == 0)
    def _():
        later[...] = e1_ref[...].astype(F32)
        early[...] = s1_ref[...]

    @pl.when(step == 1)
    def _():
        early[...] = s0_ref[...].astype(F32)

    for p in range(PAIRS):
        held, ahead = early[p], later[p]
        query, key, value = qkv_ref[:, q_cols(p)], qkv_ref[:, k_cols(p)], qkv_ref[:, v_cols(p)]
        gm = gm_ref[:, q_cols(p)]
        query_t, gm_t = query.astype(F32).T.astype(BF16), gm.astype(F32).T.astype(BF16)
        d_query, d_key_t, d_value_t = [], [], []
        for h in range(2):
            by_rows, key_t, value_t = [], None, None
            for r in range(2):
                mine, span, upto, scores, decays = tile_of(qkv_ref, c, ct, r, rows, p, h)
                weighted = (scores * decays).astype(BF16)
                grad_weighted = dot_t(jnp.where(mine, gm[span], 0), value[:upto])
                grad_scores = (grad_weighted * decays).astype(BF16)
                by_rows.append(dot(grad_scores, key[:upto]))
                part = slice(HEAD * h, HEAD * (h + 1))
                one_key = dot(query_t[part, span], grad_scores)
                one_value = dot(gm_t[part, span], weighted)
                if r == 0:
                    key_t, value_t = one_key, one_value
                else:
                    key_t = jnp.concatenate([one_key[:, :rows] + key_t, one_key[:, rows:]], 1)
                    value_t = jnp.concatenate(
                        [one_value[:, :rows] + value_t, one_value[:, rows:]], 1
                    )
            d_query.append(jnp.concatenate(by_rows, 0))
            d_key_t.append(key_t)
            d_value_t.append(value_t)
        d_query = jnp.where(lane < HEAD, d_query[0], d_query[1])
        d_query = d_query + spread_pair(growth, p) * dot_t(gm, held.astype(BF16))
        ahead_low = ahead.astype(BF16)
        tails = spread_pair(tail, p)
        d_key_tail = tails * dot_t(value, ahead_low)
        d_key = jnp.concatenate(d_key_t, 0).T + d_key_tail
        d_value = jnp.concatenate(d_value_t, 0).T
        key_f = key.astype(F32)
        d_value = d_value + dot((key_f * tails).astype(BF16), ahead_low)
        total = spread_pair(jnp.exp(last), p)
        at_last = jnp.sum(key_f * d_key_tail, axis=0, keepdims=True)
        at_last = at_last + jnp.sum(ahead * held, axis=0, keepdims=True) * total
        grad_c = query.astype(F32) * d_query - key_f * d_key
        grad_c = grad_c + jnp.where(last_row, at_last, 0.0)
        to_head = iota((WIDE, WIDE), 1) == 2 * p + (iota((WIDE, WIDE), 0) >= HEAD)
        for some in halves(grad_c):
            per_head = per_head + dot(some, to_head.astype(BF16))
        turned = turn(d_query, cosine, sine_part) * float(HEAD) ** (-0.5)
        front_ref[:, q_cols(p)] = turned.astype(BF16)
        if p < 2:
            key_sums[p], value_sums[p] = d_key, d_value
        else:
            key_sums[p - 2] = key_sums[p - 2] + d_key
            value_sums[p - 2] = value_sums[p - 2] + d_value

        @pl.when(step == 0)
        def _():
            later[p] = p1_ref[p] + total * ahead

    for p in range(2):
        front_ref[:, k_cols(p)] = turn(key_sums[p], cosine, sine_part).astype(BF16)
        front_ref[:, v_cols(p)] = value_sums[p].astype(BF16)
    upper = (iota((count, count), 0) <= iota((count, count), 1)).astype(BF16)
    grad_log = sum(dot(upper, some) for some in halves(per_head))
    z = z_ref[...]
    grad_gate = jnp.where(lane < HALF, -grad_log / (GATE_TEMP * (1.0 + jnp.exp(-z))), 0.0)
    front_ref[:, N_FRONT - WIDE :] = grad_gate.astype(BF16)
    summed = jnp.broadcast_to(jnp.sum(grad_gate, axis=0, keepdims=True), (8, WIDE))

    @pl.when(step == 0)
    def _():
        bias_ref[...] = summed

    @pl.when(step == 1)
    def _():
        bias_ref[...] += summed


def front_back_kernel(
    core_ref, normed_ref, grad_ref, w_ref, own_ref, other_ref, gain_ref, bias_ref,
    part_ref, sent_ref, *refs,
):
    *outs, d_ref = refs
    grad = grad_ref[...]
    d = t_dot(normed_ref[...], grad)
    part = dot_t(grad, w_ref[...])
    count = own_ref.shape[0]
    part_ref[...] = part[:count]
    sent_ref[...] = part[count:].astype(BF16)
    d_gain = jnp.zeros((1, part.shape[1]), F32)
    for ref, rows in ((own_ref, part[:count]), (other_ref, part[count:])):
        x = ref[...].astype(F32)
        unit = x * lax.rsqrt(jnp.mean(x * x, axis=-1, keepdims=True) + epsilon)
        d_gain = d_gain + jnp.sum(rows * unit, axis=0, keepdims=True)
    main = N_FRONT - WIDE
    d_ref[:, :main] = d[:, :main].astype(BF16)
    rest = jnp.concatenate(
        [jnp.zeros((HALF, d_gain.shape[1]), F32), d_gain, gain_ref[:1]]
        + [jnp.zeros((WIDE - HALF - 2, d_gain.shape[1]), F32)],
        0,
    ).T
    d_ref[:, main:N_FRONT] = (d[:, main:] + rest + pltpu.roll(bias_ref[...], HALF + 2, 1)[:1]).astype(BF16)
    if len(outs) == 1:
        outs[0][...] = d_ref[...]
    else:
        own, over_dp, over_mid, first, second = outs
        rows = own.shape[1]
        for i in range(4):
            for ref, b in ((own, (0, 0)), (over_dp, (1, 0)), (over_mid, (0, 1))):
                ref[i] = d_ref[pl.ds(row_of(core_ref, i, b, rows), rows), :]
            far = first if i < 2 else second
            far[i % 2] = d_ref[pl.ds(row_of(core_ref, i, (1, 1), rows), rows), :]


def beside_each(refs):
    parts = [ref[...].reshape(-1, ref.shape[-1]) for ref in refs]
    return parts[0] if len(parts) == 1 else jnp.concatenate(parts, 1)


def far_kernel(core_ref, *refs):
    *far_refs, to_dp_ref, to_mid_ref = refs
    far = beside_each(far_refs)
    n = to_dp_ref.shape[0]
    to_dp_ref[...] = far[:n]
    to_mid_ref[...] = far[n:]


def sends_kernel(core_ref, *refs):
    *refs, over_dp_ref, over_mid_ref = refs
    n = len(refs) // 4
    to_mid, to_dp, over_dp, over_mid = [beside_each(refs[n * i : n * (i + 1)]) for i in range(4)]
    n = to_dp.shape[0]
    over_dp_ref[:n] = over_dp[:n]
    over_dp_ref[n:] = (over_dp[n:].astype(F32) + to_dp.astype(F32)).astype(BF16)
    over_mid_ref[:n] = (over_mid[:n].astype(F32) + to_mid.astype(F32)).astype(BF16)
    over_mid_ref[n:] = over_mid[n:]


def own_kernel(core_ref, dp_ref, mid_ref, *refs):
    *own_refs, sum_ref = refs
    whole = beside_each(own_refs).astype(F32) + beside_each([dp_ref]).astype(F32)
    whole = whole + beside_each([mid_ref]).astype(F32)
    sum_ref[...] = whole.astype(BF16).reshape(sum_ref.shape)


def sum_kernel(core_ref, own_ref, dp_ref, mid_ref, kept_ref, sent_ref):
    n = kept_ref.shape[0]
    whole = own_ref[...].astype(F32) + dp_ref[...].astype(F32) + mid_ref[...].astype(F32)
    kept_ref[...] = whole[:n]
    sent_ref[...] = whole[n:].astype(BF16)


def down_kernel(core_ref, hidden_ref, w_ref, out_ref):
    out_ref[...] = dot_t(hidden_ref[...], w_ref[...]).astype(BF16)


def output_kernel(core_ref, hidden_ref, w_ref, middle_ref, got_ref, out_ref):
    out = middle_ref[...] + dot_t(hidden_ref[...], w_ref[...])
    out_ref[...] = (out + got_ref[...].astype(F32)).astype(BF16)


def input_kernel(core_ref, part_ref, got_ref, middle_ref, x_ref, gains_ref, out_ref):
    x = x_ref[...].astype(F32)
    scale = inverse_rms(x)
    grad = (part_ref[...] + got_ref[...].astype(F32)) * gains_ref[:1]
    out_ref[...] = (middle_ref[...] + norm_back(grad, x * scale, scale)).astype(BF16)


def last_kernel(core_ref, pair_ref, got_ref, mine_ref, sent_ref):
    whole = (pair_ref[...] + got_ref[...].astype(F32)).astype(BF16)
    n = mine_ref.shape[0]
    low, high = whole[:n], whole[n:]
    mine_ref[...] = jnp.where(core_ref[0] == 0, low, high)
    sent_ref[...] = jnp.where(core_ref[0] == 0, high, low)


def unpack_kernel(
    core_ref, mine_ref, got_ref, q_ref, k_ref, v_ref, a_ref, gains_ref, bias_ref
):
    def both(ref, at):
        n = ref.shape[1] // 2
        a, b = mine_ref[:, at : at + n].astype(F32), got_ref[:, at : at + n].astype(F32)
        ref[:, :n] = jnp.where(core_ref[0] == 0, a, b)
        ref[:, n:] = jnp.where(core_ref[0] == 0, b, a)
        return at + n

    at = both(q_ref, 0)
    at = both(k_ref, at)
    at = both(v_ref, at)
    a = mine_ref[:, at:N_FRONT].astype(F32).T
    b = got_ref[:, at:N_FRONT].astype(F32).T
    low, high = jnp.where(core_ref[0] == 0, a, b), jnp.where(core_ref[0] == 0, b, a)
    a_ref[:HALF] = low[:HALF]
    a_ref[HALF:] = high[:HALF]
    gains_ref[...] = (a + b)[HALF : HALF + 8]
    bias_ref[:HALF] = low[HALF + 2 : 2 * HALF + 2]
    bias_ref[HALF:] = high[HALF + 2 : 2 * HALF + 2]


def call(kernel, ins, outs, name, microseconds, megabytes, steps=1, scratch=(), deps=(), reverse=False):
    once = pl.Buffered(1) if steps > 1 else None
    order = (lambda i, s: (1 - i) ^ s[0]) if reverse else (lambda i, s: i ^ s[0])

    def spec(kind, shape):
        zeros = (0,) * (len(shape) - 1)
        if kind == "all":
            return pl.BlockSpec(shape, lambda i, s: (0,) + zeros, pipeline_mode=once)
        if kind == "low":
            block = (shape[0] * 2 // steps,) + shape[1:]
            return pl.BlockSpec(block, lambda i, s: (jnp.minimum(i, steps // 2 - 1),) + zeros)
        if kind == "high":
            block = (shape[0] * 2 // steps,) + shape[1:]
            return pl.BlockSpec(block, lambda i, s: (jnp.maximum(i - steps // 2, 0),) + zeros)
        if kind in ("scalar", "any"):
            return SCALARS if kind == "scalar" else ANYWHERE
        if kind == "block":
            return pl.BlockSpec((shape[0] // 2,) + shape[1:], lambda i, s: (order(i, s),) + zeros)
        if kind == "rows":
            return pl.BlockSpec((shape[0] // steps,) + shape[1:], lambda i, s: (i,) + zeros)
        if kind == "entry":
            return pl.BlockSpec((None,) + shape[1:], lambda i, s: (order(i, s),) + zeros)
        if kind == "queries":
            return pl.BlockSpec((shape[0] // 2, N_Q), lambda i, s: (order(i, s), 0))
        if kind in ("own", "over_dp", "over_mid", "far"):
            a, b = int(kind in ("over_dp", "far")), int(kind in ("over_mid", "far"))
            block = (1, shape[1], 1) + shape[3:]
            return pl.BlockSpec(block, lambda i, s: (s[1] ^ a, 0, s[3] ^ b, 0, 0))
        block, index = kind
        return pl.BlockSpec(block, lambda i, s: index, pipeline_mode=once)

    where, *ins = ins
    moved = sum(v.size * v.dtype.itemsize for _, v in ins)
    return pl.pallas_call(
        without(kernel, 1 + len(ins), len(deps)),
        grid_spec=pltpu.PrefetchScalarGridSpec(
            num_scalar_prefetch=1,
            grid=(steps,),
            in_specs=[spec(kind, v.shape) for kind, v in ins] + [ANYWHERE] * len(deps),
            out_specs=[spec(kind, shape) for kind, shape, _ in outs],
            scratch_shapes=scratch,
        ),
        out_shape=[jax.ShapeDtypeStruct(shape, kind) for _, shape, kind in outs],
        compiler_params=pltpu.CompilerParams(
            dimension_semantics=("arbitrary",), vmem_limit_bytes=megabytes * 1024 * 1024
        ),
        cost_estimate=pl.CostEstimate(
            flops=int(microseconds * FLOPS), bytes_accessed=moved, transcendentals=0
        ),
        name=name,
    )(where, *[v for _, v in ins], *deps)


def piece(whole, a, b, low, count):
    sizes = (1, count, 1) + whole.shape[3:]
    return lax.dynamic_slice(whole, (a, low, b, 0, 0), sizes).reshape((count,) + whole.shape[3:])


def square_sends(over_dp, over_mid, to_mid, to_dp):
    half = to_mid.shape[0]
    send_mid = jnp.concatenate([over_mid[:half] + to_mid, over_mid[half:]], 0)
    send_dp = jnp.concatenate([over_dp[:half], over_dp[half:] + to_dp], 0)
    return send_dp, send_mid


def hi_swap(v, difference):
    return lax.ppermute(v, "hi", [(i, i ^ difference) for i in range(4)])


def sequence_weights(group_ids, loss_weights):
    group_count = loss_weights.shape[0]
    member = (group_ids[:, None] == jnp.arange(group_count, dtype=jnp.int32)[None, :]).astype(F32)
    counts = jnp.sum(member, axis=0)
    raw_weight = jnp.sum(member * loss_weights.astype(F32)[None, :], axis=1) / jnp.sum(
        member * counts[None, :], axis=1
    )
    return raw_weight * (group_ids.shape[0] / jnp.sum(raw_weight))


def shards(
    tokens,
    cotangent,
    group_ids,
    loss_weights,
    gain_one,
    w_query,
    w_key,
    w_value,
    w_gate,
    gate_bias,
    w_out,
    gain_two,
    w_gate_ff,
    w_up,
    w_down,
):
    count, width = tokens.shape
    both = 2 * count
    n_out, n_ff = w_out.shape[1] // 2, w_up.shape[1] // 2
    n_first = N_FRONT + n_out
    core, mid = lax.axis_index("core"), lax.axis_index("mid")
    dp, hi = lax.axis_index("dp"), lax.axis_index("hi")
    where = jnp.stack([core, dp, hi, mid]).astype(jnp.int32)
    small = small_slice()
    sequence = lax.axis_index(ALL) // SPAN
    square = (PAIRS, WIDE, WIDE)

    packed = pack(
        core, w_query, w_key, w_value, w_gate.T, gain_one[None], gain_two[None], w_out, w_gate_ff,
        w_up, w_down.T,
    )
    first = place(core, packed[0], swap(packed[2], "core"))
    rest = place(core, packed[1], swap(packed[3], "core"))
    w_rest = gather(rest)
    if small:
        pair = jnp.stack([first, hi_swap(first, 2)])
        own = jnp.concatenate([pair, hi_swap(pair, 1)], 0)
        over_dp, over_mid = swap(own, "dp"), swap(own, "mid")
        pieces = (own, over_dp, over_mid, swap(over_dp[:2], "mid"), swap(over_mid[2:], "dp"))
    else:
        pieces = (gather(first),)
    other_tokens, other_cotangent = swap(tokens, "core"), swap(cotangent, "core")

    block = 2 * mid + (core ^ jnp.arange(2))
    positions = (block[:, None] * count + jnp.arange(count)[None, :]).reshape(-1)
    frequency = ROPE_BASE ** (-jnp.arange(HEAD // 2, dtype=F32) / (HEAD // 2))
    angles = positions.astype(F32)[:, None] * frequency[None, :]
    cosine, sine_part = jnp.cos(angles), jnp.sin(angles)
    cosine = jnp.concatenate([cosine] * 4, 1)
    sine_part = jnp.concatenate([-sine_part, sine_part] * 2, 1)
    own_bias = lax.dynamic_slice_in_dim(gate_bias, core * HALF, HALF)
    own_bias = jnp.concatenate([own_bias, jnp.zeros((WIDE - HALF,), F32)])[None, :]
    w_front, w_half, normed_one, qkv, c, ct, z, gains, update, leaving = call(
        front_kernel,
        [where, ("all", tokens), ("all", other_tokens), ("all", own_bias)]
        + [("block", cosine), ("block", sine_part)]
        + [("all", v) for v in pieces],
        [("all", (width, N_FRONT), BF16), ("all", (width, n_out), BF16)]
        + [("block", (both, width), BF16), ("block", (both, 2 * N_Q), BF16)]
        + [("block", (both, WIDE), F32), ("entry", (2, HALF, count), F32)]
        + [("block", (both, WIDE), F32), ("all", (8, width), F32)]
        + [("all", square, F32), ("all", square, BF16)],
        "front",
        14,
        24,
        2,
        [pltpu.VMEM(square, F32)],
    )
    state_0 = lax.ppermute(leaving, "mid", [(0, 1)])
    w_other = swap(w_half, "core")
    mixed_out, normed_own, normed_sent, state_1 = call(
        mix_kernel,
        [where, ("block", qkv), ("block", c), ("entry", ct), ("all", state_0), ("all", update)],
        [("block", (both, N_Q), F32)]
        + [("all", (count, N_Q), BF16)] * 2
        + [("all", square, F32)],
        "mix",
        11,
        16,
        2,
        [pltpu.VMEM(square, F32)],
    )
    normed_got = swap(normed_sent, "core")
    middle, normed_two_own = call(
        out_kernel,
        [where]
        + [("all", v) for v in (normed_own, normed_got, w_half, w_other, tokens, gains)],
        [("all", (count, width), F32), ("all", (count, width), BF16)],
        "out",
        4,
        16,
    )
    normed_two_other = swap(normed_two_own, "core")
    seq_weights = sequence_weights(group_ids, loss_weights)
    own_weight = jnp.sum(jnp.where(jnp.arange(group_ids.shape[0]) == sequence, seq_weights, 0.0))
    own_weight = own_weight.reshape(1)
    far = [("any", (width // 8, 2 * n_ff), BF16)] * 2 if small else []
    hidden, w_down_t, d_ff, d_down, part_kept, part_sent, *ff_sends = call(
        functools.partial(ff_kernel, small),
        [where, ("scalar", own_weight)]
        + [("all", v) for v in (normed_two_own, normed_two_other, cotangent, other_cotangent)]
        + [("any", w_rest)],
        [("any", (both, n_ff), BF16), ("any", (width, n_ff), BF16)]
        + [("any", (width, 2 * n_ff), BF16), ("any", (width, n_ff), BF16)]
        + [("all", (count, width), F32), ("all", (count, width), BF16)]
        + far,
        "ff",
        36,
        52,
        scratch=[pltpu.VMEM((width, 2 * n_ff), BF16), pltpu.VMEM((width, n_ff), BF16)]
        + [pltpu.VMEM((both, n_ff), BF16), pltpu.VMEM((both, 2 * n_ff), BF16)]
        + [pltpu.VMEM((both, width), BF16), pltpu.VMEM((width, 2 * n_ff), BF16)]
        + [pltpu.VMEM((width, n_ff), BF16)]
        + [pltpu.SemaphoreType.DMA((2,)), pltpu.SemaphoreType.DMA((8,))],
    )
    if small:
        d_ff = d_ff.reshape(2, 4, 2, -1, 2 * n_ff)
        ff_one = swap(ff_sends[0], "dp"), swap(ff_sends[1], "mid")
        down_hi = d_down.reshape(4, -1, n_ff)
        down_hi = lax.psum_scatter(down_hi, "hi", scatter_dimension=0, tiled=False)
        down_hi = down_hi.reshape(2, 1, 2, -1, n_ff)
    else:
        rest_sum = scatter(d_down)
        ff_one = []
    part_got = swap(part_sent, "core")
    down_rows = ((count, n_ff), (1, 0)), ((count, n_ff), (0, 0))
    (out_sent,) = call(
        down_kernel,
        [where, (down_rows[0], hidden), ("all", w_down_t)],
        [("all", (count, width), BF16)],
        "out_sent",
        5,
        16,
    )
    grad_middle, d_gain_two, grad_own, grad_sent, d_out_kept, d_out_sent = call(
        middle_kernel,
        [where, ("scalar", own_weight)]
        + [("all", v) for v in (part_kept, part_got, cotangent, middle, gains, w_half, w_other)]
        + [("all", v) for v in (normed_own, normed_got)],
        [("all", (count, width), F32), ("all", (8, width), F32)]
        + [("all", (count, N_Q), BF16)] * 2
        + [("all", (width, n_out), BF16)] * 2,
        "middle",
        8,
        24,
        deps=(out_sent,),
    )
    grad_got = swap(grad_sent, "core")
    d_out_got = swap(d_out_sent, "core")
    grad_mixed, through, entering = call(
        head_back_kernel,
        [where, ("all", grad_own), ("all", grad_got), ("block", mixed_out), ("queries", qkv)]
        + [("block", c)],
        [("block", (both, N_Q), BF16), ("all", square, F32), ("all", square, BF16)],
        "head_back",
        8,
        16,
        2,
        [pltpu.VMEM(square, F32), pltpu.VMEM((PAIRS, 8, WIDE), F32)],
        deps=ff_one,
    )
    state_last = lax.ppermute(entering, "mid", [(1, 0)])
    (d_out,) = call(
        add_kernel,
        [where, ("all", d_out_kept), ("all", d_out_got)],
        [("all", (width, n_out), BF16)],
        "out_sum",
        2,
        16,
        deps=(entering,),
    )
    if small:
        d_out = d_out.reshape(2, 4, 2, -1, n_out)
        n_wide = 2 * n_ff + n_out
        out_sends = call(
            far_kernel,
            [where, ("far", d_out)],
            [("all", (width // 8, n_out), BF16)] * 2,
            "out_far",
            1.5,
            16,
        )
        out_one = swap(out_sends[0], "dp"), swap(out_sends[1], "mid")
    else:
        wide_sends = out_sends = [d_out]
        wide_sum = jnp.concatenate([scatter(d_ff), scatter(d_out)], 1)
    if small:
        wide_sends = call(
            sends_kernel,
            [where]
            + [("all", v) for pair in zip(ff_one, out_one) for v in pair]
            + [(kind, v) for kind in ("over_dp", "over_mid") for v in (d_ff, d_out)],
            [("all", (width // 4, n_wide), BF16)] * 2,
            "wide_sends",
            3.5,
            20,
            deps=(state_last,),
        )
        wide_got = swap(wide_sends[0], "dp"), swap(wide_sends[1], "mid")
    grad_front, d_bias = call(
        back_kernel,
        [where, ("block", qkv), ("block", c), ("entry", ct), ("block", z), ("block", grad_mixed)]
        + [("all", v) for v in (state_0, state_1, state_last, through)]
        + [("block", cosine), ("block", sine_part)],
        [("block", (both, N_FRONT), BF16), ("all", (8, WIDE), F32)],
        "back",
        20,
        24,
        2,
        [pltpu.VMEM(square, F32), pltpu.VMEM(square, F32)],
        deps=wide_sends,
        reverse=True,
    )
    if small:
        shapes = [(4, width // 16, N_FRONT)] * 3 + [(2, width // 16, N_FRONT)] * 2
    else:
        shapes = [(width, N_FRONT)]
    part_kept, part_sent, *d_first = call(
        front_back_kernel,
        [where]
        + [("all", v) for v in (normed_one, grad_front, w_front, tokens, other_tokens)]
        + [("all", v) for v in (d_gain_two, d_bias)],
        [("all", (count, width), F32), ("all", (count, width), BF16)]
        + [("all", shape, BF16) for shape in shapes],
        "front_back",
        12,
        32,
        scratch=[pltpu.VMEM((width, N_FRONT), BF16)],
    )
    part_got = swap(part_sent, "core")

    def add_input(deps):
        return call(
            input_kernel,
            [where]
            + [("all", v) for v in (part_kept, part_got, grad_middle, tokens, gains)],
            [("all", (count, width), BF16)],
            "grad_input",
            4.5,
            16,
            deps=deps,
        )

    out_got = swap(out_sent, "core")

    def add_output(deps):
        return call(
            output_kernel,
            [where, (down_rows[1], hidden), ("all", w_down_t)]
            + [("all", v) for v in (middle, out_got)],
            [("all", (count, width), BF16)],
            "output",
            5.5,
            16,
            deps=deps,
        )

    if small:
        own, over_dp, over_mid, far_0, far_1 = d_first
        one = swap(far_0, "dp"), swap(far_1, "mid")
        (wide_hi,) = call(
            own_kernel,
            [where] + [("all", v) for v in wide_got] + [("own", d_ff), ("own", d_out)],
            [("all", (4, width // 16, n_wide), BF16)],
            "wide_own",
            3.5,
            20,
            deps=(far_0,),
        )
        wide_sum = lax.psum_scatter(wide_hi, "hi", scatter_dimension=0, tiled=False)
        rest_sends = call(
            far_kernel,
            [where, ("far", down_hi)],
            [("all", (width // 32, n_ff), BF16)] * 2,
            "rest_far",
            1.5,
            16,
            deps=(wide_hi,),
        )
        rest_one = swap(rest_sends[0], "dp"), swap(rest_sends[1], "mid")
        sends = call(
            sends_kernel,
            [where] + [("all", v) for v in (*one, over_dp, over_mid)],
            [("all", (width // 4, N_FRONT), BF16)] * 2,
            "front_sends",
            2,
            16,
            deps=(wide_hi, *rest_sends),
        )
        front_got = swap(sends[0], "dp"), swap(sends[1], "mid")
        rest_sends = call(
            sends_kernel,
            [where]
            + [("all", v) for v in rest_one]
            + [("over_dp", down_hi), ("over_mid", down_hi)],
            [("all", (width // 16, n_ff), BF16)] * 2,
            "rest_sends",
            2,
            16,
            deps=(sends[0],),
        )
        rest_got = swap(rest_sends[0], "dp"), swap(rest_sends[1], "mid")
        (output,) = add_output((sends[0],))
        (grad_input,) = add_input((sends[0],))
        kept, sent = call(
            sum_kernel,
            [where] + [("all", v.reshape(own.shape)) for v in (own, *front_got)],
            [("all", (2,) + own.shape[1:], F32), ("all", (2,) + own.shape[1:], BF16)],
            "first_sum",
            2,
            16,
            deps=(grad_input, output, *rest_sends),
        )
        pair = kept + hi_swap(sent, 1).astype(F32)
        last, last_got = pair[0], hi_swap(pair[1].astype(BF16), 2)
        (rest_sum,) = call(
            own_kernel,
            [where] + [("all", v) for v in rest_got] + [("own", down_hi)],
            [("all", (width // 16, n_ff), BF16)],
            "rest_own",
            1.5,
            16,
            deps=(kept,),
        )
    else:
        last = scatter(d_first[0]).astype(F32)
        last_got = jnp.zeros_like(last, BF16)
        (output,), (grad_input,) = add_output(()), add_input(())

    def owned(rows):
        n = rows.shape[0] // 2
        mine = lax.dynamic_slice_in_dim(rows, core * n, n)
        return mine, swap(lax.dynamic_slice_in_dim(rows, (1 - core) * n, n), "core")

    outs = []
    for v in (rest_sum, wide_sum):
        mine, theirs = owned(v)
        outs.append((mine, theirs))
    n = last.shape[0] // 2
    mine, sent = call(
        last_kernel,
        [where, ("all", last), ("all", last_got)],
        [("all", (n, N_FRONT), BF16)] * 2,
        "last",
        1.5,
        16,
        deps=tuple(theirs for _, theirs in outs),
    )
    theirs = swap(sent, "core")
    ends = [(0, 0, n_ff), (1, 0, n_ff), (1, n_ff, 2 * n_ff), (1, 2 * n_ff, 2 * n_ff + n_out)]
    g_down, g_gate_ff, g_up, g_out = [
        beside(core, *[v[:, low:high] for v in outs[i]]) for i, low, high in ends
    ]
    g_query, g_key, g_value, g_gate, g_gains, g_bias = call(
        unpack_kernel,
        [where, ("all", mine), ("all", theirs)],
        [("all", (n, 2 * N_Q), F32)]
        + [("all", (n, 2 * N_K), F32)] * 2
        + [("all", (HEADS, n), F32), ("all", (8, n), F32), ("all", (HEADS, n), F32)],
        "unpack",
        1.5,
        16,
    )
    return (
        output,
        grad_input,
        g_gains[0],
        g_query,
        g_key,
        g_value,
        g_gate.T,
        g_bias[:, 0],
        g_out,
        g_gains[1],
        g_gate_ff,
        g_up,
        g_down.T,
    )


def solution(mesh):
    devices = mesh.devices
    fine = Mesh(
        devices.reshape(devices.shape[0], devices.shape[1] // SPAN, SPAN // 2, 2), ALL
    )
    rows, columns, split = P(ALL, None), P(None, ALL), P(ALL)
    in_specs = (rows, rows, P(), P(), split) + (rows,) * 4 + (P(), rows, split, rows, rows, columns)
    out_specs = (rows, rows, split) + (rows,) * 4 + (P(), rows, split, rows, rows, columns)
    return jax.shard_map(shards, mesh=fine, in_specs=in_specs, out_specs=out_specs, check_vma=False)
```

```python
import functools

import jax
import jax.numpy as jnp
from jax import lax
from jax.experimental import pallas as pl
from jax.experimental.pallas import tpu as pltpu
from jax.sharding import Mesh, PartitionSpec as P

HEADS = 16
HEAD = 64
KVH = 2
LATENT = 256
SPAN = 4

epsilon = 1e-05
head_floor = 0.25
ROPE_BASE = 10000.0
GATE_TEMP = 16.0

CHIPS = ("dp", "hi", "mid")
ALL = ("dp", "hi", "mid", "core")
F32 = jnp.float32
BF16 = jnp.bfloat16


def swap(v, axis):
    return lax.ppermute(v, axis, [(0, 1), (1, 0)])


def place(bit, mine, theirs):
    return jnp.where(
        bit == 0, jnp.concatenate([mine, theirs], 0), jnp.concatenate([theirs, mine], 0)
    )


def small_slice():
    return lax.axis_size("dp") == 2 and lax.axis_size("hi") == 4


def gather(part):
    return lax.all_gather(part, CHIPS, axis=0, tiled=True)


def add3(a, b, c):
    return a.astype(F32) + b.astype(F32) + c.astype(F32)


def scatter(whole):
    return lax.psum_scatter(whole, CHIPS, scatter_dimension=0, tiled=True)


def beside(core, mine, theirs):
    return jnp.where(
        core == 0, jnp.concatenate([mine, theirs], 1), jnp.concatenate([theirs, mine], 1)
    ).astype(F32)


HALF = HEADS // 2
PAIRS = HALF // 2
WIDE = 2 * HEAD
N_Q = HALF * HEAD
N_K = N_Q // 2
N_FRONT = N_Q + 2 * N_K + WIDE
FLOPS = 0.55e9


def dot(left, right):
    return jnp.dot(left, right, preferred_element_type=F32)


def dot_t(left, right):
    return lax.dot_general(left, right, (((1,), (1,)), ((), ())), preferred_element_type=F32)


def t_dot(left, right):
    return lax.dot_general(left, right, (((0,), (0,)), ((), ())), preferred_element_type=F32)


def thirds(v):
    high = v.astype(BF16)
    rest = v - high.astype(F32)
    middle = rest.astype(BF16)
    return high, middle, (rest - middle.astype(F32)).astype(BF16)


def halves(v):
    high = v.astype(BF16)
    return high, (v - high.astype(F32)).astype(BF16)


def iota(shape, axis):
    return lax.broadcasted_iota(jnp.int32, shape, axis)


def spread_pair(per_head, p):
    lane = iota((1, WIDE), 1)
    return jnp.where(
        lane < HEAD, per_head[:, 2 * p : 2 * p + 1], per_head[:, 2 * p + 1 : 2 * p + 2]
    )


def head_sums(v):
    ones = own_blocks().astype(BF16)
    high = v.astype(BF16)
    return dot(high, ones) + dot((v - high.astype(F32)).astype(BF16), ones)


def turn(v, cosine, sine_part):
    lane = iota((1, WIDE), 1)
    other = jnp.where(
        lane % HEAD < HEAD // 2,
        pltpu.roll(v, WIDE - HEAD // 2, 1),
        pltpu.roll(v, HEAD // 2, 1),
    )
    return v * cosine + other * sine_part


def own_blocks():
    return (iota((WIDE, WIDE), 0) < HEAD) == (iota((WIDE, WIDE), 1) < HEAD)


def folded(state):
    return (state[:HEAD] + state[HEAD:]).astype(BF16)


def unfolded(state):
    both = jnp.concatenate([state, state], 0).astype(F32)
    return jnp.where(own_blocks(), both, 0.0)


def q_cols(p):
    return slice(WIDE * p, WIDE * (p + 1))


def k_cols(p):
    return slice(N_Q + WIDE * (p % 2), N_Q + WIDE * (p % 2 + 1))


def v_cols(p):
    return slice(N_Q + N_K + WIDE * (p % 2), N_Q + N_K + WIDE * (p % 2 + 1))


def without(kernel, start, count):
    return lambda *refs: kernel(*refs[:start], *refs[start + count :])


ANYWHERE = pl.BlockSpec(memory_space=pl.ANY)
SCALARS = pl.BlockSpec(memory_space=pltpu.SMEM)


def inverse_rms(values, added=epsilon):
    return lax.rsqrt(jnp.mean(values * values, axis=-1, keepdims=True) + added)


def norm_back(grad_unit, unit_rows, scale_rows):
    return scale_rows * (
        grad_unit - unit_rows * jnp.mean(grad_unit * unit_rows, axis=-1, keepdims=True)
    )


def row_of(where, i, b, rows):
    hi = where[2] ^ (0, 2, 1, 3)[i]
    index = ((where[1] ^ b[0]) * 4 + hi) * 2 + (where[3] ^ b[1])
    return pl.multiple_of(index * rows, rows)


def pack_kernel(core_ref, q_ref, k_ref, v_ref, a_ref, g1_ref, g2_ref, o_ref, f_ref, u_ref, d_ref, *outs):
    def put(out, at, v):
        out[:, at : at + v.shape[1]] = v
        return at + v.shape[1]

    rows = q_ref.shape[0]
    lane = iota((1, WIDE), 1)
    gates = a_ref[...].astype(F32)
    gains = [g1_ref[...].astype(F32), g2_ref[...].astype(F32)]
    for i in range(2):
        front, rest = outs[2 * i : 2 * i + 2]
        mine = core_ref[0] if i == 0 else 1 - core_ref[0]

        def half(ref):
            n = ref.shape[1] // 2
            return jnp.where(mine == 0, ref[:, :n], ref[:, n:])

        at = put(front, 0, half(q_ref))
        at = put(front, at, half(k_ref))
        at = put(front, at, half(v_ref))
        some = jnp.where(mine == 0, gates[:HALF], gates[HALF:])
        small = jnp.concatenate([some, *gains, jnp.zeros((WIDE - HALF - 2, rows), F32)], 0)
        at = put(front, at, small.T.astype(BF16))
        put(front, at, half(o_ref))
        at = put(rest, 0, half(f_ref))
        at = put(rest, at, half(u_ref))
        put(rest, at, half(d_ref))


def pack(core, *weights):
    rows = weights[0].shape[0]
    n_out, n_ff = weights[6].shape[1] // 2, weights[7].shape[1] // 2
    return pl.pallas_call(
        pack_kernel,
        in_specs=[pl.BlockSpec(memory_space=pltpu.SMEM)]
        + [pl.BlockSpec(memory_space=pltpu.VMEM)] * len(weights),
        out_specs=[pl.BlockSpec(memory_space=pltpu.VMEM)] * 4,
        out_shape=[
            jax.ShapeDtypeStruct((rows, n), BF16) for n in (N_FRONT + n_out, 3 * n_ff)
        ]
        * 2,
        name="pack",
    )(core.reshape(1).astype(jnp.int32), *weights)


def front_kernel(
    core_ref, own_ref, other_ref, bias_ref, cos_ref, sin_ref, *refs
):
    *pieces, w_ref, out_ref = refs[:-9]
    normed_ref, qkv_ref, c_ref, ct_ref, z_ref, gains_ref, u_ref, leave_ref, first_u = refs[-9:]
    step = pl.program_id(0)
    slot = step ^ core_ref[0]

    @pl.when(step == 0)
    def _():
        if len(pieces) == 1:
            w_ref[...] = pieces[0][:, :N_FRONT]
            out_ref[...] = pieces[0][:, N_FRONT:]
        else:
            own, over_dp, over_mid, first, second = pieces
            rows = own.shape[1]
            for i in range(4):
                far = first[i] if i < 2 else second[i - 2]
                for v, b in ((own[i], (0, 0)), (over_dp[i], (1, 0)), (over_mid[i], (0, 1)), (far, (1, 1))):
                    to = pl.ds(row_of(core_ref, i, b, rows), rows)
                    w_ref[to, :] = v[:, :N_FRONT]
                    out_ref[to, :] = v[:, N_FRONT:]

    x = jnp.where(slot == 0, own_ref[...], other_ref[...]).astype(F32)
    gains = w_ref[:, N_FRONT - WIDE :].astype(F32).T[HALF : HALF + 8]
    gains_ref[...] = gains
    scale = lax.rsqrt(jnp.mean(x * x, axis=-1, keepdims=True) + epsilon)
    normed = (x * scale * gains[:1]).astype(BF16)
    normed_ref[...] = normed
    pre = dot(normed, w_ref[...])
    cosine, sine_part = cos_ref[...], sin_ref[...]
    for p in range(PAIRS):
        turned = turn(pre[:, q_cols(p)], cosine, sine_part)
        qkv_ref[:, q_cols(p)] = (turned * float(HEAD) ** (-0.5)).astype(BF16)
    for p in range(PAIRS // 2):
        qkv_ref[:, k_cols(p)] = turn(pre[:, k_cols(p)], cosine, sine_part).astype(BF16)
        qkv_ref[:, v_cols(p)] = pre[:, v_cols(p)].astype(BF16)
    z = pre[:, N_FRONT - WIDE :] + bias_ref[...]
    z_ref[...] = z
    small = jnp.exp(-jnp.abs(z))
    log_part = jnp.where(
        small < 0.01, small * (1.0 - small * (0.5 - small * (1.0 / 3.0))), jnp.log(1.0 + small)
    )
    softplus = jnp.maximum(z, 0.0) + log_part
    log_decay = jnp.where(iota((1, WIDE), 1) < HALF, -softplus / GATE_TEMP, 0.0)
    count = x.shape[0]
    lower = (iota((count, count), 0) >= iota((count, count), 1)).astype(BF16)
    c = sum(dot(lower, third) for third in thirds(log_decay))
    c_ref[...] = c
    ct_ref[...] = c.T[:HALF]
    last = c[count - 1 :]
    tail = jnp.exp(last - c)
    mask = own_blocks()
    for p in range(PAIRS):
        scaled = (qkv_ref[:, k_cols(p)].astype(F32) * spread_pair(tail, p)).astype(BF16)
        update = jnp.where(mask, t_dot(scaled, qkv_ref[:, v_cols(p)]), 0.0)

        @pl.when(step == 0)
        def _():
            u_ref[p] = update
            first_u[p] = update

        @pl.when(step == 1)
        def _():
            grown = spread_pair(jnp.exp(last), p) * first_u[p] + update
            leave_ref[p] = folded(grown)


def tile_of(qkv_ref, c, ct, r, rows, p, h):
    lane = iota((1, WIDE), 1)
    mine = (lane < HEAD) if h == 0 else (lane >= HEAD)
    span = slice(rows * r, rows * (r + 1))
    upto = rows * (r + 1)
    query = jnp.where(mine, qkv_ref[span, q_cols(p)], 0)
    scores = dot_t(query, qkv_ref[:upto, k_cols(p)])
    head = 2 * p + h
    differences = c[span, head : head + 1] - ct[head : head + 1, :upto]
    causal = iota((rows, upto), 0) + rows * r >= iota((rows, upto), 1)
    decays = jnp.exp(jnp.where(causal, differences, -1e30))
    return mine, span, upto, scores, decays


def mix_kernel(
    core_ref, qkv_ref, c_ref, ct_ref, s0_ref, u_ref,
    mixed_ref, own_ref, sent_ref, s1_ref, state,
):
    step = pl.program_id(0)
    slot = step ^ core_ref[0]
    count = c_ref.shape[0]
    rows = count // 2
    lane = iota((1, WIDE), 1)
    c, ct = c_ref[...], ct_ref[...]

    @pl.when(step == 0)
    def _():
        for p in range(PAIRS):
            state[p] = unfolded(s0_ref[p])

    growth = jnp.exp(c)
    for p in range(PAIRS):
        held = state[p]
        carried = spread_pair(growth, p) * dot(qkv_ref[:, q_cols(p)], held.astype(BF16))
        for r in range(2):
            parts = []
            for h in range(2):
                mine, span, upto, scores, decays = tile_of(qkv_ref, c, ct, r, rows, p, h)
                weighted = (scores * decays).astype(BF16)
                parts.append(dot(weighted, qkv_ref[:upto, v_cols(p)]))
            mixed = jnp.where(lane < HEAD, parts[0], parts[1]) + carried[span]
            mixed_ref[span, q_cols(p)] = mixed
            scale = lax.rsqrt(head_sums(mixed * mixed) * (1.0 / HEAD) + head_floor)
            normed = (mixed * scale).astype(BF16)

            @pl.when(slot == 0)
            def _():
                own_ref[span, q_cols(p)] = normed

            @pl.when(slot == 1)
            def _():
                sent_ref[span, q_cols(p)] = normed

        @pl.when(step == 0)
        def _():
            grown = spread_pair(growth[count - 1 :], p) * held + u_ref[p]
            s1_ref[p] = grown
            state[p] = grown


def out_kernel(
    core_ref, own_ref, got_ref, half_ref, other_ref, x_ref, gains_ref, middle_ref, normed_ref
):
    core = core_ref[0]
    n = own_ref.shape[1]
    mine = pl.ds(pl.multiple_of(core * n, n), n)
    theirs = pl.ds(pl.multiple_of((1 - core) * n, n), n)
    own, got = own_ref[...], got_ref[...]
    a = dot(own, half_ref[mine, :]) + dot(got, half_ref[theirs, :])
    b = dot(own, other_ref[mine, :]) + dot(got, other_ref[theirs, :])
    attention = jnp.where(core == 0, jnp.concatenate([a, b], 1), jnp.concatenate([b, a], 1))
    middle = x_ref[...].astype(F32) + attention
    middle_ref[...] = middle
    normed_ref[...] = (middle * inverse_rms(middle) * gains_ref[1:2]).astype(BF16)


def ff_kernel(
    small, where_ref, weight_ref, own_ref, other_ref, cot_ref, cot_other_ref, w_ref,
    hidden_out, down_out, d_ff_out, d_down_out, kept_ref, sent_ref, *refs,
):
    *far_outs, wide, down, hidden, grads, branch, d_ff, d_down, in_sems, out_sems = refs
    count = own_ref.shape[0]
    n = down.shape[1]
    loads = [
        pltpu.make_async_copy(w_ref.at[:, pl.ds(at, to.shape[1])], to, in_sems.at[i])
        for i, (to, at) in enumerate(((wide, 0), (down, 2 * n)))
    ]
    for load in loads:
        load.start()
    stores = []

    def store(piece, to):
        stores.append(pltpu.make_async_copy(piece, to, out_sems.at[len(stores)]))
        stores[-1].start()

    for i, ref in enumerate((cot_ref, cot_other_ref)):
        scaled = (ref[...].astype(F32) * weight_ref[0]).astype(BF16)
        branch[count * i : count * (i + 1), :] = scaled
    for i, ref in enumerate((own_ref, other_ref)):
        at = slice(count * i, count * (i + 1))
        if i == 0:
            loads[0].wait()
        pre = dot(ref[...], wide[...])
        g, u = pre[:, :n], pre[:, n:]
        sigmoid = 1.0 / (1.0 + jnp.exp(-g))
        silu = g * sigmoid
        slope = u * sigmoid * (1.0 + g * (1.0 - sigmoid))
        hidden[at, :] = (silu * u).astype(BF16)
        if i == 0:
            loads[1].wait()
        grad = dot(branch[at, :], down[...])
        grads[at, :n] = (grad * slope).astype(BF16)
        grads[at, n:] = (grad * silu).astype(BF16)

    store(hidden, hidden_out)
    store(down, down_out)

    def part(i):
        at = slice(count * i, count * (i + 1))
        return dot_t(grads[at, :], wide[...])

    width = own_ref.shape[1]
    block = 512

    @pl.loop(0, width // block)
    def _(j):
        at = pl.ds(pl.multiple_of(j * block, block), block)
        d = t_dot(own_ref[:, at], grads[:count, :]) + t_dot(other_ref[:, at], grads[count:, :])
        d_ff[at, :] = d.astype(BF16)

    store(d_ff, d_ff_out)
    if small:
        rows = width // 16
        for i in range(4):
            index = ((1 - where_ref[1]) * 4 + i) * 2 + 1 - where_ref[3]
            from_ = pl.ds(pl.multiple_of(index * rows, rows), rows)
            store(d_ff.at[from_, :], far_outs[i // 2].at[pl.ds(rows * (i % 2), rows), :])

    chunk = width // 8
    order = [4 * (j % 2) + j // 2 if small else j for j in range(8)]
    for j in range(0, 8, 4):
        columns = [branch[:, chunk * i : chunk * (i + 1)] for i in order[j : j + 4]]
        d = t_dot(jnp.concatenate(columns, 1), hidden[...])
        d_down[chunk * j : chunk * (j + 4), :] = d.astype(BF16)
    store(d_down, d_down_out)
    sent_ref[...] = part(1).astype(BF16)
    kept_ref[...] = part(0)
    for one in stores:
        one.wait()


def middle_kernel(
    core_ref, weight_ref, part_ref, got_ref, cot_ref, middle_ref, gains_ref, half_ref, other_ref,
    normed_ref, normed_got_ref, grad_middle_ref, gain_ref, own_ref, sent_ref, out_kept_ref,
    out_sent_ref,
):
    core = core_ref[0]
    part = part_ref[...] + got_ref[...].astype(F32)
    middle = middle_ref[...]
    scale = inverse_rms(middle)
    unit = middle * scale
    gain_ref[...] = jnp.broadcast_to(jnp.sum(part * unit, axis=0, keepdims=True), gain_ref.shape)
    grad_middle = cot_ref[...].astype(F32) * weight_ref[0]
    grad_middle = grad_middle + norm_back(part * gains_ref[1:2], unit, scale)
    grad_middle_ref[...] = grad_middle
    attention = grad_middle.astype(BF16)
    n = half_ref.shape[1]
    low, high = attention[:, :n], attention[:, n:]
    kept, rest = jnp.where(core == 0, low, high), jnp.where(core == 0, high, low)
    pairs = ((sent_ref, normed_got_ref, 1 - core), (own_ref, normed_ref, core))
    for ref, heads_ref, at in pairs:
        rows = pl.ds(pl.multiple_of(at * n, n), n)
        ref[...] = (dot_t(kept, half_ref[rows, :]) + dot_t(rest, other_ref[rows, :])).astype(BF16)
        heads = heads_ref[...]
        out_kept_ref[rows, :] = t_dot(heads, kept).astype(BF16)
        out_sent_ref[rows, :] = t_dot(heads, rest).astype(BF16)


def add_kernel(core_ref, a_ref, b_ref, sum_ref):
    sum_ref[...] = (a_ref[...].astype(F32) + b_ref[...].astype(F32)).astype(BF16)


def head_back_kernel(
    core_ref, own_ref, got_ref, mixed_ref, q_ref, c_ref,
    gm_ref, p1_ref, enter_ref, first_p, decay,
):
    step = pl.program_id(0)
    slot = step ^ core_ref[0]
    count = c_ref.shape[0]
    growth = jnp.exp(c_ref[...])
    mask = own_blocks()
    for p in range(PAIRS):
        mixed = mixed_ref[:, q_cols(p)]
        grad = jnp.where(slot == 0, own_ref[:, q_cols(p)], got_ref[:, q_cols(p)]).astype(F32)
        scale = lax.rsqrt(head_sums(mixed * mixed) * (1.0 / HEAD) + head_floor)
        unit = mixed * scale
        back = scale * (grad - unit * (head_sums(grad * unit) * (1.0 / HEAD)))
        gm = back.astype(BF16)
        gm_ref[:, q_cols(p)] = gm
        grown = (q_ref[:, q_cols(p)].astype(F32) * spread_pair(growth, p)).astype(BF16)
        through = jnp.where(mask, t_dot(grown, gm), 0.0)

        @pl.when(step == 0)
        def _():
            first_p[p] = through
            decay[p] = jnp.broadcast_to(spread_pair(growth[count - 1 :], p), (8, WIDE))

        @pl.when(step == 1)
        def _():
            p1_ref[p] = through
            enter_ref[p] = folded(first_p[p] + decay[p][:1] * through)


def back_kernel(
    core_ref, qkv_ref, c_ref, ct_ref, z_ref, gm_ref, s0_ref, s1_ref, e1_ref, p1_ref, cos_ref,
    sin_ref, front_ref, bias_ref, later, early,
):
    step = pl.program_id(0)
    count = c_ref.shape[0]
    rows = count // 2
    lane = iota((1, WIDE), 1)
    c, ct = c_ref[...], ct_ref[...]
    growth = jnp.exp(c)
    last = c[count - 1 :]
    tail = jnp.exp(last - c)
    last_row = iota((count, 1), 0) == count - 1
    per_head = jnp.zeros((count, WIDE), F32)
    key_sums, value_sums = [None, None], [None, None]
    cosine, sine_part = cos_ref[...], -sin_ref[...]

    @pl.when(step == 0)
    def _():
        for p in range(PAIRS):
            later[p] = unfolded(e1_ref[p])
        early[...] = s1_ref[...]

    @pl.when(step == 1)
    def _():
        for p in range(PAIRS):
            early[p] = unfolded(s0_ref[p])

    for p in range(PAIRS):
        held, ahead = early[p], later[p]
        query, key, value = qkv_ref[:, q_cols(p)], qkv_ref[:, k_cols(p)], qkv_ref[:, v_cols(p)]
        gm = gm_ref[:, q_cols(p)]
        query_t, gm_t = query.astype(F32).T.astype(BF16), gm.astype(F32).T.astype(BF16)
        d_query, d_key_t, d_value_t = [], [], []
        for h in range(2):
            by_rows, key_t, value_t = [], None, None
            for r in range(2):
                mine, span, upto, scores, decays = tile_of(qkv_ref, c, ct, r, rows, p, h)
                weighted = (scores * decays).astype(BF16)
                grad_weighted = dot_t(jnp.where(mine, gm[span], 0), value[:upto])
                grad_scores = (grad_weighted * decays).astype(BF16)
                by_rows.append(dot(grad_scores, key[:upto]))
                part = slice(HEAD * h, HEAD * (h + 1))
                one_key = dot(query_t[part, span], grad_scores)
                one_value = dot(gm_t[part, span], weighted)
                if r == 0:
                    key_t, value_t = one_key, one_value
                else:
                    key_t = jnp.concatenate([one_key[:, :rows] + key_t, one_key[:, rows:]], 1)
                    value_t = jnp.concatenate(
                        [one_value[:, :rows] + value_t, one_value[:, rows:]], 1
                    )
            d_query.append(jnp.concatenate(by_rows, 0))
            d_key_t.append(key_t)
            d_value_t.append(value_t)
        d_query = jnp.where(lane < HEAD, d_query[0], d_query[1])
        d_query = d_query + spread_pair(growth, p) * dot_t(gm, held.astype(BF16))
        ahead_low = ahead.astype(BF16)
        tails = spread_pair(tail, p)
        d_key_tail = tails * dot_t(value, ahead_low)
        d_key = jnp.concatenate(d_key_t, 0).T + d_key_tail
        d_value = jnp.concatenate(d_value_t, 0).T
        key_f = key.astype(F32)
        d_value = d_value + dot((key_f * tails).astype(BF16), ahead_low)
        total = spread_pair(jnp.exp(last), p)
        at_last = jnp.sum(key_f * d_key_tail, axis=0, keepdims=True)
        at_last = at_last + jnp.sum(ahead * held, axis=0, keepdims=True) * total
        grad_c = query.astype(F32) * d_query - key_f * d_key
        grad_c = grad_c + jnp.where(last_row, at_last, 0.0)
        to_head = iota((WIDE, WIDE), 1) == 2 * p + (iota((WIDE, WIDE), 0) >= HEAD)
        for some in halves(grad_c):
            per_head = per_head + dot(some, to_head.astype(BF16))
        turned = turn(d_query, cosine, sine_part) * float(HEAD) ** (-0.5)
        front_ref[:, q_cols(p)] = turned.astype(BF16)
        if p < 2:
            key_sums[p], value_sums[p] = d_key, d_value
        else:
            key_sums[p - 2] = key_sums[p - 2] + d_key
            value_sums[p - 2] = value_sums[p - 2] + d_value

        @pl.when(step == 0)
        def _():
            later[p] = p1_ref[p] + total * ahead

    for p in range(2):
        front_ref[:, k_cols(p)] = turn(key_sums[p], cosine, sine_part).astype(BF16)
        front_ref[:, v_cols(p)] = value_sums[p].astype(BF16)
    upper = (iota((count, count), 0) <= iota((count, count), 1)).astype(BF16)
    grad_log = sum(dot(upper, some) for some in halves(per_head))
    z = z_ref[...]
    grad_gate = jnp.where(lane < HALF, -grad_log / (GATE_TEMP * (1.0 + jnp.exp(-z))), 0.0)
    front_ref[:, N_FRONT - WIDE :] = grad_gate.astype(BF16)
    summed = jnp.broadcast_to(jnp.sum(grad_gate, axis=0, keepdims=True), (8, WIDE))

    @pl.when(step == 0)
    def _():
        bias_ref[...] = summed

    @pl.when(step == 1)
    def _():
        bias_ref[...] += summed


def front_back_kernel(
    core_ref, normed_ref, grad_ref, w_ref, own_ref, other_ref, gain_ref, bias_ref,
    part_ref, sent_ref, *refs,
):
    *outs, d_ref = refs
    grad = grad_ref[...]
    d = t_dot(normed_ref[...], grad)
    part = dot_t(grad, w_ref[...])
    count = own_ref.shape[0]
    part_ref[...] = part[:count]
    sent_ref[...] = part[count:].astype(BF16)
    d_gain = jnp.zeros((1, part.shape[1]), F32)
    for ref, rows in ((own_ref, part[:count]), (other_ref, part[count:])):
        x = ref[...].astype(F32)
        unit = x * lax.rsqrt(jnp.mean(x * x, axis=-1, keepdims=True) + epsilon)
        d_gain = d_gain + jnp.sum(rows * unit, axis=0, keepdims=True)
    main = N_FRONT - WIDE
    d_ref[:, :main] = d[:, :main].astype(BF16)
    rest = jnp.concatenate(
        [jnp.zeros((HALF, d_gain.shape[1]), F32), d_gain, gain_ref[:1]]
        + [jnp.zeros((WIDE - HALF - 2, d_gain.shape[1]), F32)],
        0,
    ).T
    d_ref[:, main:N_FRONT] = (d[:, main:] + rest + pltpu.roll(bias_ref[...], HALF + 2, 1)[:1]).astype(BF16)
    if len(outs) == 1:
        outs[0][...] = d_ref[...]
    else:
        own, over_dp, over_mid, first, second = outs
        rows = own.shape[1]
        for i in range(4):
            for ref, b in ((own, (0, 0)), (over_dp, (1, 0)), (over_mid, (0, 1))):
                ref[i] = d_ref[pl.ds(row_of(core_ref, i, b, rows), rows), :]
            far = first if i < 2 else second
            far[i % 2] = d_ref[pl.ds(row_of(core_ref, i, (1, 1), rows), rows), :]


def beside_each(refs):
    parts = [ref[...].reshape(-1, ref.shape[-1]) for ref in refs]
    return parts[0] if len(parts) == 1 else jnp.concatenate(parts, 1)


def far_kernel(core_ref, *refs):
    *far_refs, to_dp_ref, to_mid_ref = refs
    far = beside_each(far_refs)
    n = to_dp_ref.shape[0]
    to_dp_ref[...] = far[:n]
    to_mid_ref[...] = far[n:]


def sends_kernel(core_ref, *refs):
    *refs, over_dp_ref, over_mid_ref = refs
    n = len(refs) // 4
    to_mid, to_dp, over_dp, over_mid = [beside_each(refs[n * i : n * (i + 1)]) for i in range(4)]
    n = to_dp.shape[0]
    over_dp_ref[:n] = over_dp[:n]
    over_dp_ref[n:] = (over_dp[n:].astype(F32) + to_dp.astype(F32)).astype(BF16)
    over_mid_ref[:n] = (over_mid[:n].astype(F32) + to_mid.astype(F32)).astype(BF16)
    over_mid_ref[n:] = over_mid[n:]


def own_kernel(core_ref, dp_ref, mid_ref, *refs):
    *own_refs, sum_ref = refs
    whole = beside_each(own_refs).astype(F32) + beside_each([dp_ref]).astype(F32)
    whole = whole + beside_each([mid_ref]).astype(F32)
    sum_ref[...] = whole.astype(BF16).reshape(sum_ref.shape)


def sum_kernel(core_ref, own_ref, dp_ref, mid_ref, kept_ref, sent_ref):
    n = kept_ref.shape[0]
    whole = own_ref[...].astype(F32) + dp_ref[...].astype(F32) + mid_ref[...].astype(F32)
    kept_ref[...] = whole[:n]
    sent_ref[...] = whole[n:].astype(BF16)


def down_kernel(core_ref, hidden_ref, w_ref, out_ref):
    out_ref[...] = dot_t(hidden_ref[...], w_ref[...]).astype(BF16)


def output_kernel(core_ref, hidden_ref, w_ref, middle_ref, got_ref, out_ref):
    out = middle_ref[...] + dot_t(hidden_ref[...], w_ref[...])
    out_ref[...] = (out + got_ref[...].astype(F32)).astype(BF16)


def input_kernel(core_ref, part_ref, got_ref, middle_ref, x_ref, gains_ref, out_ref):
    x = x_ref[...].astype(F32)
    scale = inverse_rms(x)
    grad = (part_ref[...] + got_ref[...].astype(F32)) * gains_ref[:1]
    out_ref[...] = (middle_ref[...] + norm_back(grad, x * scale, scale)).astype(BF16)


def last_kernel(core_ref, pair_ref, got_ref, mine_ref, sent_ref):
    whole = (pair_ref[...] + got_ref[...].astype(F32)).astype(BF16)
    n = mine_ref.shape[0]
    low, high = whole[:n], whole[n:]
    mine_ref[...] = jnp.where(core_ref[0] == 0, low, high)
    sent_ref[...] = jnp.where(core_ref[0] == 0, high, low)


def unpack_kernel(
    core_ref, mine_ref, got_ref, q_ref, k_ref, v_ref, a_ref, gains_ref, bias_ref
):
    def both(ref, at):
        n = ref.shape[1] // 2
        a, b = mine_ref[:, at : at + n].astype(F32), got_ref[:, at : at + n].astype(F32)
        ref[:, :n] = jnp.where(core_ref[0] == 0, a, b)
        ref[:, n:] = jnp.where(core_ref[0] == 0, b, a)
        return at + n

    at = both(q_ref, 0)
    at = both(k_ref, at)
    at = both(v_ref, at)
    a = mine_ref[:, at:N_FRONT].astype(F32).T
    b = got_ref[:, at:N_FRONT].astype(F32).T
    low, high = jnp.where(core_ref[0] == 0, a, b), jnp.where(core_ref[0] == 0, b, a)
    a_ref[:HALF] = low[:HALF]
    a_ref[HALF:] = high[:HALF]
    gains_ref[...] = (a + b)[HALF : HALF + 8]
    bias_ref[:HALF] = low[HALF + 2 : 2 * HALF + 2]
    bias_ref[HALF:] = high[HALF + 2 : 2 * HALF + 2]


def call(kernel, ins, outs, name, microseconds, megabytes, steps=1, scratch=(), deps=(), reverse=False):
    once = pl.Buffered(1) if steps > 1 else None
    order = (lambda i, s: (1 - i) ^ s[0]) if reverse else (lambda i, s: i ^ s[0])

    def spec(kind, shape):
        zeros = (0,) * (len(shape) - 1)
        if kind == "all":
            return pl.BlockSpec(shape, lambda i, s: (0,) + zeros, pipeline_mode=once)
        if kind == "low":
            block = (shape[0] * 2 // steps,) + shape[1:]
            return pl.BlockSpec(block, lambda i, s: (jnp.minimum(i, steps // 2 - 1),) + zeros)
        if kind == "high":
            block = (shape[0] * 2 // steps,) + shape[1:]
            return pl.BlockSpec(block, lambda i, s: (jnp.maximum(i - steps // 2, 0),) + zeros)
        if kind in ("scalar", "any"):
            return SCALARS if kind == "scalar" else ANYWHERE
        if kind == "block":
            return pl.BlockSpec((shape[0] // 2,) + shape[1:], lambda i, s: (order(i, s),) + zeros)
        if kind == "rows":
            return pl.BlockSpec((shape[0] // steps,) + shape[1:], lambda i, s: (i,) + zeros)
        if kind == "entry":
            return pl.BlockSpec((None,) + shape[1:], lambda i, s: (order(i, s),) + zeros)
        if kind == "queries":
            return pl.BlockSpec((shape[0] // 2, N_Q), lambda i, s: (order(i, s), 0))
        if kind in ("own", "over_dp", "over_mid", "far"):
            a, b = int(kind in ("over_dp", "far")), int(kind in ("over_mid", "far"))
            block = (1, shape[1], 1) + shape[3:]
            return pl.BlockSpec(block, lambda i, s: (s[1] ^ a, 0, s[3] ^ b, 0, 0))
        block, index = kind
        return pl.BlockSpec(block, lambda i, s: index, pipeline_mode=once)

    where, *ins = ins
    moved = sum(v.size * v.dtype.itemsize for _, v in ins)
    return pl.pallas_call(
        without(kernel, 1 + len(ins), len(deps)),
        grid_spec=pltpu.PrefetchScalarGridSpec(
            num_scalar_prefetch=1,
            grid=(steps,),
            in_specs=[spec(kind, v.shape) for kind, v in ins] + [ANYWHERE] * len(deps),
            out_specs=[spec(kind, shape) for kind, shape, _ in outs],
            scratch_shapes=scratch,
        ),
        out_shape=[jax.ShapeDtypeStruct(shape, kind) for _, shape, kind in outs],
        compiler_params=pltpu.CompilerParams(
            dimension_semantics=("arbitrary",), vmem_limit_bytes=megabytes * 1024 * 1024
        ),
        cost_estimate=pl.CostEstimate(
            flops=int(microseconds * FLOPS), bytes_accessed=moved, transcendentals=0
        ),
        name=name,
    )(where, *[v for _, v in ins], *deps)


def piece(whole, a, b, low, count):
    sizes = (1, count, 1) + whole.shape[3:]
    return lax.dynamic_slice(whole, (a, low, b, 0, 0), sizes).reshape((count,) + whole.shape[3:])


def square_sends(over_dp, over_mid, to_mid, to_dp):
    half = to_mid.shape[0]
    send_mid = jnp.concatenate([over_mid[:half] + to_mid, over_mid[half:]], 0)
    send_dp = jnp.concatenate([over_dp[:half], over_dp[half:] + to_dp], 0)
    return send_dp, send_mid


def hi_swap(v, difference):
    return lax.ppermute(v, "hi", [(i, i ^ difference) for i in range(4)])


def sequence_weights(group_ids, loss_weights):
    group_count = loss_weights.shape[0]
    member = (group_ids[:, None] == jnp.arange(group_count, dtype=jnp.int32)[None, :]).astype(F32)
    counts = jnp.sum(member, axis=0)
    raw_weight = jnp.sum(member * loss_weights.astype(F32)[None, :], axis=1) / jnp.sum(
        member * counts[None, :], axis=1
    )
    return raw_weight * (group_ids.shape[0] / jnp.sum(raw_weight))


def shards(
    tokens,
    cotangent,
    group_ids,
    loss_weights,
    gain_one,
    w_query,
    w_key,
    w_value,
    w_gate,
    gate_bias,
    w_out,
    gain_two,
    w_gate_ff,
    w_up,
    w_down,
):
    count, width = tokens.shape
    both = 2 * count
    n_out, n_ff = w_out.shape[1] // 2, w_up.shape[1] // 2
    n_first = N_FRONT + n_out
    core, mid = lax.axis_index("core"), lax.axis_index("mid")
    dp, hi = lax.axis_index("dp"), lax.axis_index("hi")
    where = jnp.stack([core, dp, hi, mid]).astype(jnp.int32)
    small = small_slice()
    sequence = lax.axis_index(ALL) // SPAN
    square = (PAIRS, WIDE, WIDE)

    packed = pack(
        core, w_query, w_key, w_value, w_gate.T, gain_one[None], gain_two[None], w_out, w_gate_ff,
        w_up, w_down.T,
    )
    first = place(core, packed[0], swap(packed[2], "core"))
    rest = place(core, packed[1], swap(packed[3], "core"))
    w_rest = gather(rest)
    if small:
        pair = jnp.stack([first, hi_swap(first, 2)])
        own = jnp.concatenate([pair, hi_swap(pair, 1)], 0)
        over_dp, over_mid = swap(own, "dp"), swap(own, "mid")
        pieces = (own, over_dp, over_mid, swap(over_dp[:2], "mid"), swap(over_mid[2:], "dp"))
    else:
        pieces = (gather(first),)
    other_tokens, other_cotangent = swap(tokens, "core"), swap(cotangent, "core")

    block = 2 * mid + (core ^ jnp.arange(2))
    positions = (block[:, None] * count + jnp.arange(count)[None, :]).reshape(-1)
    frequency = ROPE_BASE ** (-jnp.arange(HEAD // 2, dtype=F32) / (HEAD // 2))
    angles = positions.astype(F32)[:, None] * frequency[None, :]
    cosine, sine_part = jnp.cos(angles), jnp.sin(angles)
    cosine = jnp.concatenate([cosine] * 4, 1)
    sine_part = jnp.concatenate([-sine_part, sine_part] * 2, 1)
    own_bias = lax.dynamic_slice_in_dim(gate_bias, core * HALF, HALF)
    own_bias = jnp.concatenate([own_bias, jnp.zeros((WIDE - HALF,), F32)])[None, :]
    w_front, w_half, normed_one, qkv, c, ct, z, gains, update, leaving = call(
        front_kernel,
        [where, ("all", tokens), ("all", other_tokens), ("all", own_bias)]
        + [("block", cosine), ("block", sine_part)]
        + [("all", v) for v in pieces],
        [("all", (width, N_FRONT), BF16), ("all", (width, n_out), BF16)]
        + [("block", (both, width), BF16), ("block", (both, 2 * N_Q), BF16)]
        + [("block", (both, WIDE), F32), ("entry", (2, HALF, count), F32)]
        + [("block", (both, WIDE), F32), ("all", (8, width), F32)]
        + [("all", square, F32), ("all", (PAIRS, HEAD, WIDE), BF16)],
        "front",
        14,
        24,
        2,
        [pltpu.VMEM(square, F32)],
    )
    state_0 = lax.ppermute(leaving, "mid", [(0, 1)])
    w_other = swap(w_half, "core")
    mixed_out, normed_own, normed_sent, state_1 = call(
        mix_kernel,
        [where, ("block", qkv), ("block", c), ("entry", ct), ("all", state_0), ("all", update)],
        [("block", (both, N_Q), F32)]
        + [("all", (count, N_Q), BF16)] * 2
        + [("all", square, F32)],
        "mix",
        11,
        16,
        2,
        [pltpu.VMEM(square, F32)],
    )
    normed_got = swap(normed_sent, "core")
    middle, normed_two_own = call(
        out_kernel,
        [where]
        + [("all", v) for v in (normed_own, normed_got, w_half, w_other, tokens, gains)],
        [("all", (count, width), F32), ("all", (count, width), BF16)],
        "out",
        4,
        16,
    )
    normed_two_other = swap(normed_two_own, "core")
    seq_weights = sequence_weights(group_ids, loss_weights)
    own_weight = jnp.sum(jnp.where(jnp.arange(group_ids.shape[0]) == sequence, seq_weights, 0.0))
    own_weight = own_weight.reshape(1)
    far = [("any", (width // 8, 2 * n_ff), BF16)] * 2 if small else []
    hidden, w_down_t, d_ff, d_down, part_kept, part_sent, *ff_sends = call(
        functools.partial(ff_kernel, small),
        [where, ("scalar", own_weight)]
        + [("all", v) for v in (normed_two_own, normed_two_other, cotangent, other_cotangent)]
        + [("any", w_rest)],
        [("any", (both, n_ff), BF16), ("any", (width, n_ff), BF16)]
        + [("any", (width, 2 * n_ff), BF16), ("any", (width, n_ff), BF16)]
        + [("all", (count, width), F32), ("all", (count, width), BF16)]
        + far,
        "ff",
        36,
        44,
        scratch=[pltpu.VMEM((width, 2 * n_ff), BF16), pltpu.VMEM((width, n_ff), BF16)]
        + [pltpu.VMEM((both, n_ff), BF16), pltpu.VMEM((both, 2 * n_ff), BF16)]
        + [pltpu.VMEM((both, width), BF16), pltpu.VMEM((width, 2 * n_ff), BF16)]
        + [pltpu.VMEM((width, n_ff), BF16)]
        + [pltpu.SemaphoreType.DMA((2,)), pltpu.SemaphoreType.DMA((8,))],
    )
    if small:
        d_ff = d_ff.reshape(2, 4, 2, -1, 2 * n_ff)
        ff_one = swap(ff_sends[0], "dp"), swap(ff_sends[1], "mid")
        down_hi = d_down.reshape(4, -1, n_ff)
        down_hi = lax.psum_scatter(down_hi, "hi", scatter_dimension=0, tiled=False)
        down_hi = down_hi.reshape(2, 1, 2, -1, n_ff)
    else:
        rest_sum = scatter(d_down)
        ff_one = []
    part_got = swap(part_sent, "core")
    down_rows = ((count, n_ff), (1, 0)), ((count, n_ff), (0, 0))
    (out_sent,) = call(
        down_kernel,
        [where, (down_rows[0], hidden), ("all", w_down_t)],
        [("all", (count, width), BF16)],
        "out_sent",
        5,
        16,
    )
    grad_middle, d_gain_two, grad_own, grad_sent, d_out_kept, d_out_sent = call(
        middle_kernel,
        [where, ("scalar", own_weight)]
        + [("all", v) for v in (part_kept, part_got, cotangent, middle, gains, w_half, w_other)]
        + [("all", v) for v in (normed_own, normed_got)],
        [("all", (count, width), F32), ("all", (8, width), F32)]
        + [("all", (count, N_Q), BF16)] * 2
        + [("all", (width, n_out), BF16)] * 2,
        "middle",
        8,
        24,
        deps=(out_sent,),
    )
    grad_got = swap(grad_sent, "core")
    d_out_got = swap(d_out_sent, "core")
    grad_mixed, through, entering = call(
        head_back_kernel,
        [where, ("all", grad_own), ("all", grad_got), ("block", mixed_out), ("queries", qkv)]
        + [("block", c)],
        [("block", (both, N_Q), BF16), ("all", square, F32), ("all", (PAIRS, HEAD, WIDE), BF16)],
        "head_back",
        8,
        16,
        2,
        [pltpu.VMEM(square, F32), pltpu.VMEM((PAIRS, 8, WIDE), F32)],
        deps=ff_one,
    )
    state_last = lax.ppermute(entering, "mid", [(1, 0)])
    (d_out,) = call(
        add_kernel,
        [where, ("all", d_out_kept), ("all", d_out_got)],
        [("all", (width, n_out), BF16)],
        "out_sum",
        2,
        16,
        deps=(entering,),
    )
    if small:
        d_out = d_out.reshape(2, 4, 2, -1, n_out)
        n_wide = 2 * n_ff + n_out
        out_sends = call(
            far_kernel,
            [where, ("far", d_out)],
            [("all", (width // 8, n_out), BF16)] * 2,
            "out_far",
            1.5,
            16,
        )
        out_one = swap(out_sends[0], "dp"), swap(out_sends[1], "mid")
    else:
        wide_sends = out_sends = [d_out]
        wide_sum = jnp.concatenate([scatter(d_ff), scatter(d_out)], 1)
    if small:
        wide_sends = call(
            sends_kernel,
            [where]
            + [("all", v) for pair in zip(ff_one, out_one) for v in pair]
            + [(kind, v) for kind in ("over_dp", "over_mid") for v in (d_ff, d_out)],
            [("all", (width // 4, n_wide), BF16)] * 2,
            "wide_sends",
            3.5,
            20,
            deps=(state_last,),
        )
        wide_got = swap(wide_sends[0], "dp"), swap(wide_sends[1], "mid")
    grad_front, d_bias = call(
        back_kernel,
        [where, ("block", qkv), ("block", c), ("entry", ct), ("block", z), ("block", grad_mixed)]
        + [("all", v) for v in (state_0, state_1, state_last, through)]
        + [("block", cosine), ("block", sine_part)],
        [("block", (both, N_FRONT), BF16), ("all", (8, WIDE), F32)],
        "back",
        20,
        16,
        2,
        [pltpu.VMEM(square, F32), pltpu.VMEM(square, F32)],
        deps=wide_sends,
        reverse=True,
    )
    if small:
        shapes = [(4, width // 16, N_FRONT)] * 3 + [(2, width // 16, N_FRONT)] * 2
    else:
        shapes = [(width, N_FRONT)]
    part_kept, part_sent, *d_first = call(
        front_back_kernel,
        [where]
        + [("all", v) for v in (normed_one, grad_front, w_front, tokens, other_tokens)]
        + [("all", v) for v in (d_gain_two, d_bias)],
        [("all", (count, width), F32), ("all", (count, width), BF16)]
        + [("all", shape, BF16) for shape in shapes],
        "front_back",
        12,
        20,
        scratch=[pltpu.VMEM((width, N_FRONT), BF16)],
    )
    part_got = swap(part_sent, "core")

    def add_input(deps):
        return call(
            input_kernel,
            [where]
            + [("all", v) for v in (part_kept, part_got, grad_middle, tokens, gains)],
            [("all", (count, width), BF16)],
            "grad_input",
            4.5,
            16,
            deps=deps,
        )

    out_got = swap(out_sent, "core")

    def add_output(deps):
        return call(
            output_kernel,
            [where, (down_rows[1], hidden), ("all", w_down_t)]
            + [("all", v) for v in (middle, out_got)],
            [("all", (count, width), BF16)],
            "output",
            5.5,
            16,
            deps=deps,
        )

    if small:
        own, over_dp, over_mid, far_0, far_1 = d_first
        one = swap(far_0, "dp"), swap(far_1, "mid")
        (wide_hi,) = call(
            own_kernel,
            [where] + [("all", v) for v in wide_got] + [("own", d_ff), ("own", d_out)],
            [("all", (4, width // 16, n_wide), BF16)],
            "wide_own",
            3.5,
            20,
            deps=(far_0,),
        )
        wide_sum = lax.psum_scatter(wide_hi, "hi", scatter_dimension=0, tiled=False)
        rest_sends = call(
            far_kernel,
            [where, ("far", down_hi)],
            [("all", (width // 32, n_ff), BF16)] * 2,
            "rest_far",
            1.5,
            16,
            deps=(wide_hi,),
        )
        rest_one = swap(rest_sends[0], "dp"), swap(rest_sends[1], "mid")
        sends = call(
            sends_kernel,
            [where] + [("all", v) for v in (*one, over_dp, over_mid)],
            [("all", (width // 4, N_FRONT), BF16)] * 2,
            "front_sends",
            2,
            16,
            deps=(wide_hi, *rest_sends),
        )
        front_got = swap(sends[0], "dp"), swap(sends[1], "mid")
        rest_sends = call(
            sends_kernel,
            [where]
            + [("all", v) for v in rest_one]
            + [("over_dp", down_hi), ("over_mid", down_hi)],
            [("all", (width // 16, n_ff), BF16)] * 2,
            "rest_sends",
            2,
            16,
            deps=(sends[0],),
        )
        rest_got = swap(rest_sends[0], "dp"), swap(rest_sends[1], "mid")
        (output,) = add_output((sends[0],))
        (grad_input,) = add_input((sends[0],))
        kept, sent = call(
            sum_kernel,
            [where] + [("all", v.reshape(own.shape)) for v in (own, *front_got)],
            [("all", (2,) + own.shape[1:], F32), ("all", (2,) + own.shape[1:], BF16)],
            "first_sum",
            2,
            16,
            deps=(grad_input, output, *rest_sends),
        )
        pair = kept + hi_swap(sent, 1).astype(F32)
        last, last_got = pair[0], hi_swap(pair[1].astype(BF16), 2)
        (rest_sum,) = call(
            own_kernel,
            [where] + [("all", v) for v in rest_got] + [("own", down_hi)],
            [("all", (width // 16, n_ff), BF16)],
            "rest_own",
            1.5,
            16,
            deps=(kept,),
        )
    else:
        last = scatter(d_first[0]).astype(F32)
        last_got = jnp.zeros_like(last, BF16)
        (output,), (grad_input,) = add_output(()), add_input(())

    def owned(rows):
        n = rows.shape[0] // 2
        mine = lax.dynamic_slice_in_dim(rows, core * n, n)
        return mine, swap(lax.dynamic_slice_in_dim(rows, (1 - core) * n, n), "core")

    outs = []
    for v in (rest_sum, wide_sum):
        mine, theirs = owned(v)
        outs.append((mine, theirs))
    n = last.shape[0] // 2
    mine, sent = call(
        last_kernel,
        [where, ("all", last), ("all", last_got)],
        [("all", (n, N_FRONT), BF16)] * 2,
        "last",
        1.5,
        16,
        deps=tuple(theirs for _, theirs in outs),
    )
    theirs = swap(sent, "core")
    ends = [(0, 0, n_ff), (1, 0, n_ff), (1, n_ff, 2 * n_ff), (1, 2 * n_ff, 2 * n_ff + n_out)]
    g_down, g_gate_ff, g_up, g_out = [
        beside(core, *[v[:, low:high] for v in outs[i]]) for i, low, high in ends
    ]
    g_query, g_key, g_value, g_gate, g_gains, g_bias = call(
        unpack_kernel,
        [where, ("all", mine), ("all", theirs)],
        [("all", (n, 2 * N_Q), F32)]
        + [("all", (n, 2 * N_K), F32)] * 2
        + [("all", (HEADS, n), F32), ("all", (8, n), F32), ("all", (HEADS, n), F32)],
        "unpack",
        1.5,
        16,
    )
    return (
        output,
        grad_input,
        g_gains[0],
        g_query,
        g_key,
        g_value,
        g_gate.T,
        g_bias[:, 0],
        g_out,
        g_gains[1],
        g_gate_ff,
        g_up,
        g_down.T,
    )


def solution(mesh):
    devices = mesh.devices
    fine = Mesh(
        devices.reshape(devices.shape[0], devices.shape[1] // SPAN, SPAN // 2, 2), ALL
    )
    rows, columns, split = P(ALL, None), P(None, ALL), P(ALL)
    in_specs = (rows, rows, P(), P(), split) + (rows,) * 4 + (P(), rows, split, rows, rows, columns)
    out_specs = (rows, rows, split) + (rows,) * 4 + (P(), rows, split, rows, rows, columns)
    return jax.shard_map(shards, mesh=fine, in_specs=in_specs, out_specs=out_specs, check_vma=False)
```

```python
import functools

import jax
import jax.numpy as jnp
from jax import lax
from jax.experimental import pallas as pl
from jax.experimental.pallas import tpu as pltpu
from jax.sharding import Mesh, PartitionSpec as P

HEADS = 16
HEAD = 64
KVH = 2
LATENT = 256
SPAN = 4

epsilon = 1e-05
head_floor = 0.25
ROPE_BASE = 10000.0
GATE_TEMP = 16.0

CHIPS = ("dp", "hi", "mid")
ALL = ("dp", "hi", "mid", "core")
F32 = jnp.float32
BF16 = jnp.bfloat16


def swap(v, axis):
    return lax.ppermute(v, axis, [(0, 1), (1, 0)])


def place(bit, mine, theirs):
    return jnp.where(
        bit == 0, jnp.concatenate([mine, theirs], 0), jnp.concatenate([theirs, mine], 0)
    )


def small_slice():
    return lax.axis_size("dp") == 2 and lax.axis_size("hi") == 4


def gather(part):
    return lax.all_gather(part, CHIPS, axis=0, tiled=True)


def add3(a, b, c):
    return a.astype(F32) + b.astype(F32) + c.astype(F32)


def scatter(whole):
    return lax.psum_scatter(whole, CHIPS, scatter_dimension=0, tiled=True)


def beside(core, mine, theirs):
    return jnp.where(
        core == 0, jnp.concatenate([mine, theirs], 1), jnp.concatenate([theirs, mine], 1)
    ).astype(F32)


HALF = HEADS // 2
PAIRS = HALF // 2
WIDE = 2 * HEAD
N_Q = HALF * HEAD
N_K = N_Q // 2
N_FRONT = N_Q + 2 * N_K + WIDE
FLOPS = 0.55e9


def dot(left, right):
    return jnp.dot(left, right, preferred_element_type=F32)


def dot_t(left, right):
    return lax.dot_general(left, right, (((1,), (1,)), ((), ())), preferred_element_type=F32)


def t_dot(left, right):
    return lax.dot_general(left, right, (((0,), (0,)), ((), ())), preferred_element_type=F32)


def thirds(v):
    high = v.astype(BF16)
    rest = v - high.astype(F32)
    middle = rest.astype(BF16)
    return high, middle, (rest - middle.astype(F32)).astype(BF16)


def halves(v):
    high = v.astype(BF16)
    return high, (v - high.astype(F32)).astype(BF16)


def iota(shape, axis):
    return lax.broadcasted_iota(jnp.int32, shape, axis)


def spread_pair(per_head, p):
    lane = iota((1, WIDE), 1)
    return jnp.where(
        lane < HEAD, per_head[:, 2 * p : 2 * p + 1], per_head[:, 2 * p + 1 : 2 * p + 2]
    )


def head_sums(v):
    ones = own_blocks().astype(BF16)
    high = v.astype(BF16)
    return dot(high, ones) + dot((v - high.astype(F32)).astype(BF16), ones)


def turn(v, cosine, sine_part):
    lane = iota((1, WIDE), 1)
    other = jnp.where(
        lane % HEAD < HEAD // 2,
        pltpu.roll(v, WIDE - HEAD // 2, 1),
        pltpu.roll(v, HEAD // 2, 1),
    )
    return v * cosine + other * sine_part


def own_blocks():
    return (iota((WIDE, WIDE), 0) < HEAD) == (iota((WIDE, WIDE), 1) < HEAD)


def folded(state):
    return (state[:HEAD] + state[HEAD:]).astype(BF16)


def unfolded(state):
    both = jnp.concatenate([state, state], 0).astype(F32)
    return jnp.where(own_blocks(), both, 0.0)


def q_cols(p):
    return slice(WIDE * p, WIDE * (p + 1))


def k_cols(p):
    return slice(N_Q + WIDE * (p % 2), N_Q + WIDE * (p % 2 + 1))


def v_cols(p):
    return slice(N_Q + N_K + WIDE * (p % 2), N_Q + N_K + WIDE * (p % 2 + 1))


def without(kernel, start, count):
    return lambda *refs: kernel(*refs[:start], *refs[start + count :])


ANYWHERE = pl.BlockSpec(memory_space=pl.ANY)
SCALARS = pl.BlockSpec(memory_space=pltpu.SMEM)


def inverse_rms(values, added=epsilon):
    return lax.rsqrt(jnp.mean(values * values, axis=-1, keepdims=True) + added)


def norm_back(grad_unit, unit_rows, scale_rows):
    return scale_rows * (
        grad_unit - unit_rows * jnp.mean(grad_unit * unit_rows, axis=-1, keepdims=True)
    )


def row_of(where, i, b, rows):
    hi = where[2] ^ (0, 2, 1, 3)[i]
    index = ((where[1] ^ b[0]) * 4 + hi) * 2 + (where[3] ^ b[1])
    return pl.multiple_of(index * rows, rows)


def pack_kernel(core_ref, q_ref, k_ref, v_ref, a_ref, g1_ref, g2_ref, o_ref, f_ref, u_ref, d_ref, *outs):
    def put(out, at, v):
        out[:, at : at + v.shape[1]] = v
        return at + v.shape[1]

    rows = q_ref.shape[0]
    lane = iota((1, WIDE), 1)
    gates = a_ref[...].astype(F32)
    gains = [g1_ref[...].astype(F32), g2_ref[...].astype(F32)]
    for i in range(2):
        front, rest = outs[2 * i : 2 * i + 2]
        mine = core_ref[0] if i == 0 else 1 - core_ref[0]

        def half(ref):
            n = ref.shape[1] // 2
            return jnp.where(mine == 0, ref[:, :n], ref[:, n:])

        at = put(front, 0, half(q_ref))
        at = put(front, at, half(k_ref))
        at = put(front, at, half(v_ref))
        some = jnp.where(mine == 0, gates[:HALF], gates[HALF:])
        small = jnp.concatenate([some, *gains, jnp.zeros((WIDE - HALF - 2, rows), F32)], 0)
        at = put(front, at, small.T.astype(BF16))
        put(front, at, half(o_ref))
        at = put(rest, 0, half(f_ref))
        at = put(rest, at, half(u_ref))
        put(rest, at, half(d_ref))


def pack(core, *weights):
    rows = weights[0].shape[0]
    n_out, n_ff = weights[6].shape[1] // 2, weights[7].shape[1] // 2
    return pl.pallas_call(
        pack_kernel,
        in_specs=[pl.BlockSpec(memory_space=pltpu.SMEM)]
        + [pl.BlockSpec(memory_space=pltpu.VMEM)] * len(weights),
        out_specs=[pl.BlockSpec(memory_space=pltpu.VMEM)] * 4,
        out_shape=[
            jax.ShapeDtypeStruct((rows, n), BF16) for n in (N_FRONT + n_out, 3 * n_ff)
        ]
        * 2,
        name="pack",
    )(core.reshape(1).astype(jnp.int32), *weights)


def front_kernel(
    core_ref, own_ref, other_ref, bias_ref, cos_ref, sin_ref, *refs
):
    *pieces, w_ref, out_ref = refs[:-9]
    normed_ref, qkv_ref, c_ref, ct_ref, z_ref, gains_ref, u_ref, leave_ref, first_u = refs[-9:]
    step = pl.program_id(0)
    slot = step ^ core_ref[0]

    @pl.when(step == 0)
    def _():
        if len(pieces) == 1:
            w_ref[...] = pieces[0][:, :N_FRONT]
            out_ref[...] = pieces[0][:, N_FRONT:]
        else:
            own, over_dp, over_mid, first, second = pieces
            rows = own.shape[1]
            for i in range(4):
                far = first[i] if i < 2 else second[i - 2]
                for v, b in ((own[i], (0, 0)), (over_dp[i], (1, 0)), (over_mid[i], (0, 1)), (far, (1, 1))):
                    to = pl.ds(row_of(core_ref, i, b, rows), rows)
                    w_ref[to, :] = v[:, :N_FRONT]
                    out_ref[to, :] = v[:, N_FRONT:]

    x = jnp.where(slot == 0, own_ref[...], other_ref[...]).astype(F32)
    gains = w_ref[:, N_FRONT - WIDE :].astype(F32).T[HALF : HALF + 8]
    gains_ref[...] = gains
    scale = lax.rsqrt(jnp.mean(x * x, axis=-1, keepdims=True) + epsilon)
    normed = (x * scale * gains[:1]).astype(BF16)
    normed_ref[...] = normed
    pre = dot(normed, w_ref[...])
    cosine, sine_part = cos_ref[...], sin_ref[...]
    for p in range(PAIRS):
        turned = turn(pre[:, q_cols(p)], cosine, sine_part)
        qkv_ref[:, q_cols(p)] = (turned * float(HEAD) ** (-0.5)).astype(BF16)
    for p in range(PAIRS // 2):
        qkv_ref[:, k_cols(p)] = turn(pre[:, k_cols(p)], cosine, sine_part).astype(BF16)
        qkv_ref[:, v_cols(p)] = pre[:, v_cols(p)].astype(BF16)
    z = pre[:, N_FRONT - WIDE :] + bias_ref[...]
    z_ref[...] = z
    small = jnp.exp(-jnp.abs(z))
    log_part = jnp.where(
        small < 0.01, small * (1.0 - small * (0.5 - small * (1.0 / 3.0))), jnp.log(1.0 + small)
    )
    softplus = jnp.maximum(z, 0.0) + log_part
    log_decay = jnp.where(iota((1, WIDE), 1) < HALF, -softplus / GATE_TEMP, 0.0)
    count = x.shape[0]
    lower = (iota((count, count), 0) >= iota((count, count), 1)).astype(BF16)
    c = sum(dot(lower, third) for third in thirds(log_decay))
    c_ref[...] = c
    ct_ref[...] = c.T[:HALF]
    last = c[count - 1 :]
    tail = jnp.exp(last - c)
    mask = own_blocks()
    for p in range(PAIRS):
        scaled = (qkv_ref[:, k_cols(p)].astype(F32) * spread_pair(tail, p)).astype(BF16)
        update = jnp.where(mask, t_dot(scaled, qkv_ref[:, v_cols(p)]), 0.0)

        @pl.when(step == 0)
        def _():
            u_ref[p] = update
            first_u[p] = update

        @pl.when(step == 1)
        def _():
            grown = spread_pair(jnp.exp(last), p) * first_u[p] + update
            leave_ref[p] = folded(grown)


def tile_of(qkv_ref, c, ct, r, rows, p, h):
    lane = iota((1, WIDE), 1)
    mine = (lane < HEAD) if h == 0 else (lane >= HEAD)
    span = slice(rows * r, rows * (r + 1))
    upto = rows * (r + 1)
    query = jnp.where(mine, qkv_ref[span, q_cols(p)], 0)
    scores = dot_t(query, qkv_ref[:upto, k_cols(p)])
    head = 2 * p + h
    differences = c[span, head : head + 1] - ct[head : head + 1, :upto]
    causal = iota((rows, upto), 0) + rows * r >= iota((rows, upto), 1)
    decays = jnp.exp(jnp.where(causal, differences, -1e30))
    return mine, span, upto, scores, decays


def mix_kernel(
    core_ref, qkv_ref, c_ref, ct_ref, s0_ref, u_ref,
    mixed_ref, own_ref, sent_ref, s1_ref, state,
):
    step = pl.program_id(0)
    slot = step ^ core_ref[0]
    count = c_ref.shape[0]
    rows = count // 2
    lane = iota((1, WIDE), 1)
    c, ct = c_ref[...], ct_ref[...]

    @pl.when(step == 0)
    def _():
        for p in range(PAIRS):
            state[p] = unfolded(s0_ref[p])

    growth = jnp.exp(c)
    for p in range(PAIRS):
        held = state[p]
        carried = spread_pair(growth, p) * dot(qkv_ref[:, q_cols(p)], held.astype(BF16))
        for r in range(2):
            parts = []
            for h in range(2):
                mine, span, upto, scores, decays = tile_of(qkv_ref, c, ct, r, rows, p, h)
                weighted = (scores * decays).astype(BF16)
                parts.append(dot(weighted, qkv_ref[:upto, v_cols(p)]))
            mixed = jnp.where(lane < HEAD, parts[0], parts[1]) + carried[span]
            mixed_ref[span, q_cols(p)] = mixed
            scale = lax.rsqrt(head_sums(mixed * mixed) * (1.0 / HEAD) + head_floor)
            normed = (mixed * scale).astype(BF16)

            @pl.when(slot == 0)
            def _():
                own_ref[span, q_cols(p)] = normed

            @pl.when(slot == 1)
            def _():
                sent_ref[span, q_cols(p)] = normed

        @pl.when(step == 0)
        def _():
            grown = spread_pair(growth[count - 1 :], p) * held + u_ref[p]
            s1_ref[p] = grown
            state[p] = grown


def out_kernel(
    core_ref, own_ref, got_ref, half_ref, other_ref, x_ref, gains_ref, middle_ref, normed_ref
):
    core = core_ref[0]
    n = own_ref.shape[1]
    mine = pl.ds(pl.multiple_of(core * n, n), n)
    theirs = pl.ds(pl.multiple_of((1 - core) * n, n), n)
    own, got = own_ref[...], got_ref[...]
    a = dot(own, half_ref[mine, :]) + dot(got, half_ref[theirs, :])
    b = dot(own, other_ref[mine, :]) + dot(got, other_ref[theirs, :])
    attention = jnp.where(core == 0, jnp.concatenate([a, b], 1), jnp.concatenate([b, a], 1))
    middle = x_ref[...].astype(F32) + attention
    middle_ref[...] = middle
    normed_ref[...] = (middle * inverse_rms(middle) * gains_ref[1:2]).astype(BF16)


def ff_kernel(
    small, where_ref, weight_ref, own_ref, other_ref, cot_ref, cot_other_ref, w_ref,
    hidden_out, down_out, d_ff_out, d_down_out, kept_ref, sent_ref, *refs,
):
    *far_outs, wide, down, hidden, grads, branch, d_ff, d_down, in_sems, out_sems = refs
    count = own_ref.shape[0]
    n = down.shape[1]
    loads = [
        pltpu.make_async_copy(w_ref.at[:, pl.ds(at, to.shape[1])], to, in_sems.at[i])
        for i, (to, at) in enumerate(((wide, 0), (down, 2 * n)))
    ]
    for load in loads:
        load.start()
    stores = []

    def store(piece, to):
        stores.append(pltpu.make_async_copy(piece, to, out_sems.at[len(stores)]))
        stores[-1].start()

    for i, ref in enumerate((cot_ref, cot_other_ref)):
        scaled = (ref[...].astype(F32) * weight_ref[0]).astype(BF16)
        branch[count * i : count * (i + 1), :] = scaled
    for i, ref in enumerate((own_ref, other_ref)):
        at = slice(count * i, count * (i + 1))
        if i == 0:
            loads[0].wait()
        pre = dot(ref[...], wide[...])
        g, u = pre[:, :n], pre[:, n:]
        sigmoid = 1.0 / (1.0 + jnp.exp(-g))
        silu = g * sigmoid
        slope = u * sigmoid * (1.0 + g * (1.0 - sigmoid))
        hidden[at, :] = (silu * u).astype(BF16)
        if i == 0:
            loads[1].wait()
        grad = dot(branch[at, :], down[...])
        grads[at, :n] = (grad * slope).astype(BF16)
        grads[at, n:] = (grad * silu).astype(BF16)

    store(hidden, hidden_out)
    store(down, down_out)

    def part(i):
        at = slice(count * i, count * (i + 1))
        return dot_t(grads[at, :], wide[...])

    width = own_ref.shape[1]
    block = 512

    @pl.loop(0, width // block)
    def _(j):
        at = pl.ds(pl.multiple_of(j * block, block), block)
        d = t_dot(own_ref[:, at], grads[:count, :]) + t_dot(other_ref[:, at], grads[count:, :])
        d_ff[at, :] = d.astype(BF16)

    store(d_ff, d_ff_out)
    if small:
        rows = width // 16
        for i in range(4):
            index = ((1 - where_ref[1]) * 4 + i) * 2 + 1 - where_ref[3]
            from_ = pl.ds(pl.multiple_of(index * rows, rows), rows)
            store(d_ff.at[from_, :], far_outs[i // 2].at[pl.ds(rows * (i % 2), rows), :])

    chunk = width // 8
    order = [4 * (j % 2) + j // 2 if small else j for j in range(8)]
    for j in range(0, 8, 4):
        columns = [branch[:, chunk * i : chunk * (i + 1)] for i in order[j : j + 4]]
        d = t_dot(jnp.concatenate(columns, 1), hidden[...])
        d_down[chunk * j : chunk * (j + 4), :] = d.astype(BF16)
    store(d_down, d_down_out)
    sent_ref[...] = part(1).astype(BF16)
    kept_ref[...] = part(0)
    for one in stores:
        one.wait()


def middle_kernel(
    core_ref, weight_ref, part_ref, got_ref, cot_ref, middle_ref, gains_ref, half_ref, other_ref,
    normed_ref, normed_got_ref, grad_middle_ref, gain_ref, own_ref, sent_ref, out_kept_ref,
    out_sent_ref,
):
    core = core_ref[0]
    part = part_ref[...] + got_ref[...].astype(F32)
    middle = middle_ref[...]
    scale = inverse_rms(middle)
    unit = middle * scale
    gain_ref[...] = jnp.broadcast_to(jnp.sum(part * unit, axis=0, keepdims=True), gain_ref.shape)
    grad_middle = cot_ref[...].astype(F32) * weight_ref[0]
    grad_middle = grad_middle + norm_back(part * gains_ref[1:2], unit, scale)
    grad_middle_ref[...] = grad_middle
    attention = grad_middle.astype(BF16)
    n = half_ref.shape[1]
    low, high = attention[:, :n], attention[:, n:]
    kept, rest = jnp.where(core == 0, low, high), jnp.where(core == 0, high, low)
    pairs = ((sent_ref, normed_got_ref, 1 - core), (own_ref, normed_ref, core))
    for ref, heads_ref, at in pairs:
        rows = pl.ds(pl.multiple_of(at * n, n), n)
        ref[...] = (dot_t(kept, half_ref[rows, :]) + dot_t(rest, other_ref[rows, :])).astype(BF16)
        heads = heads_ref[...]
        out_kept_ref[rows, :] = t_dot(heads, kept).astype(BF16)
        out_sent_ref[rows, :] = t_dot(heads, rest).astype(BF16)


def out_sum_kernel(core_ref, a_ref, b_ref, sum_ref, *far_refs):
    sum_ref[...] = (a_ref[...].astype(F32) + b_ref[...].astype(F32)).astype(BF16)
    rows = a_ref.shape[0] // 16
    for i in range(2 * len(far_refs)):
        index = ((1 - core_ref[1]) * 4 + i) * 2 + 1 - core_ref[3]
        from_ = pl.ds(pl.multiple_of(index * rows, rows), rows)
        far_refs[i // 2][rows * (i % 2) : rows * (i % 2 + 1), :] = sum_ref[from_, :]


def head_back_kernel(
    core_ref, own_ref, got_ref, mixed_ref, q_ref, c_ref,
    gm_ref, p1_ref, enter_ref, first_p, decay,
):
    step = pl.program_id(0)
    slot = step ^ core_ref[0]
    count = c_ref.shape[0]
    growth = jnp.exp(c_ref[...])
    mask = own_blocks()
    for p in range(PAIRS):
        mixed = mixed_ref[:, q_cols(p)]
        grad = jnp.where(slot == 0, own_ref[:, q_cols(p)], got_ref[:, q_cols(p)]).astype(F32)
        scale = lax.rsqrt(head_sums(mixed * mixed) * (1.0 / HEAD) + head_floor)
        unit = mixed * scale
        back = scale * (grad - unit * (head_sums(grad * unit) * (1.0 / HEAD)))
        gm = back.astype(BF16)
        gm_ref[:, q_cols(p)] = gm
        grown = (q_ref[:, q_cols(p)].astype(F32) * spread_pair(growth, p)).astype(BF16)
        through = jnp.where(mask, t_dot(grown, gm), 0.0)

        @pl.when(step == 0)
        def _():
            first_p[p] = through
            decay[p] = jnp.broadcast_to(spread_pair(growth[count - 1 :], p), (8, WIDE))

        @pl.when(step == 1)
        def _():
            p1_ref[p] = through
            enter_ref[p] = folded(first_p[p] + decay[p][:1] * through)


def back_kernel(
    core_ref, qkv_ref, c_ref, ct_ref, z_ref, gm_ref, s0_ref, s1_ref, e1_ref, p1_ref, cos_ref,
    sin_ref, front_ref, bias_ref, later, early,
):
    step = pl.program_id(0)
    count = c_ref.shape[0]
    rows = count // 2
    lane = iota((1, WIDE), 1)
    c, ct = c_ref[...], ct_ref[...]
    growth = jnp.exp(c)
    last = c[count - 1 :]
    tail = jnp.exp(last - c)
    last_row = iota((count, 1), 0) == count - 1
    per_head = jnp.zeros((count, WIDE), F32)
    key_sums, value_sums = [None, None], [None, None]
    cosine, sine_part = cos_ref[...], -sin_ref[...]

    @pl.when(step == 0)
    def _():
        for p in range(PAIRS):
            later[p] = unfolded(e1_ref[p])
        early[...] = s1_ref[...]

    @pl.when(step == 1)
    def _():
        for p in range(PAIRS):
            early[p] = unfolded(s0_ref[p])

    for p in range(PAIRS):
        held, ahead = early[p], later[p]
        query, key, value = qkv_ref[:, q_cols(p)], qkv_ref[:, k_cols(p)], qkv_ref[:, v_cols(p)]
        gm = gm_ref[:, q_cols(p)]
        query_t, gm_t = query.astype(F32).T.astype(BF16), gm.astype(F32).T.astype(BF16)
        d_query, d_key_t, d_value_t = [], [], []
        for h in range(2):
            by_rows, key_t, value_t = [], None, None
            for r in range(2):
                mine, span, upto, scores, decays = tile_of(qkv_ref, c, ct, r, rows, p, h)
                weighted = (scores * decays).astype(BF16)
                grad_weighted = dot_t(jnp.where(mine, gm[span], 0), value[:upto])
                grad_scores = (grad_weighted * decays).astype(BF16)
                by_rows.append(dot(grad_scores, key[:upto]))
                part = slice(HEAD * h, HEAD * (h + 1))
                one_key = dot(query_t[part, span], grad_scores)
                one_value = dot(gm_t[part, span], weighted)
                if r == 0:
                    key_t, value_t = one_key, one_value
                else:
                    key_t = jnp.concatenate([one_key[:, :rows] + key_t, one_key[:, rows:]], 1)
                    value_t = jnp.concatenate(
                        [one_value[:, :rows] + value_t, one_value[:, rows:]], 1
                    )
            d_query.append(jnp.concatenate(by_rows, 0))
            d_key_t.append(key_t)
            d_value_t.append(value_t)
        d_query = jnp.where(lane < HEAD, d_query[0], d_query[1])
        d_query = d_query + spread_pair(growth, p) * dot_t(gm, held.astype(BF16))
        ahead_low = ahead.astype(BF16)
        tails = spread_pair(tail, p)
        d_key_tail = tails * dot_t(value, ahead_low)
        d_key = jnp.concatenate(d_key_t, 0).T + d_key_tail
        d_value = jnp.concatenate(d_value_t, 0).T
        key_f = key.astype(F32)
        d_value = d_value + dot((key_f * tails).astype(BF16), ahead_low)
        total = spread_pair(jnp.exp(last), p)
        at_last = jnp.sum(key_f * d_key_tail, axis=0, keepdims=True)
        at_last = at_last + jnp.sum(ahead * held, axis=0, keepdims=True) * total
        grad_c = query.astype(F32) * d_query - key_f * d_key
        grad_c = grad_c + jnp.where(last_row, at_last, 0.0)
        to_head = iota((WIDE, WIDE), 1) == 2 * p + (iota((WIDE, WIDE), 0) >= HEAD)
        for some in halves(grad_c):
            per_head = per_head + dot(some, to_head.astype(BF16))
        turned = turn(d_query, cosine, sine_part) * float(HEAD) ** (-0.5)
        front_ref[:, q_cols(p)] = turned.astype(BF16)
        if p < 2:
            key_sums[p], value_sums[p] = d_key, d_value
        else:
            key_sums[p - 2] = key_sums[p - 2] + d_key
            value_sums[p - 2] = value_sums[p - 2] + d_value

        @pl.when(step == 0)
        def _():
            later[p] = p1_ref[p] + total * ahead

    for p in range(2):
        front_ref[:, k_cols(p)] = turn(key_sums[p], cosine, sine_part).astype(BF16)
        front_ref[:, v_cols(p)] = value_sums[p].astype(BF16)
    upper = (iota((count, count), 0) <= iota((count, count), 1)).astype(BF16)
    grad_log = sum(dot(upper, some) for some in halves(per_head))
    z = z_ref[...]
    grad_gate = jnp.where(lane < HALF, -grad_log / (GATE_TEMP * (1.0 + jnp.exp(-z))), 0.0)
    front_ref[:, N_FRONT - WIDE :] = grad_gate.astype(BF16)
    summed = jnp.broadcast_to(jnp.sum(grad_gate, axis=0, keepdims=True), (8, WIDE))

    @pl.when(step == 0)
    def _():
        bias_ref[...] = summed

    @pl.when(step == 1)
    def _():
        bias_ref[...] += summed


def front_back_kernel(
    core_ref, normed_ref, grad_ref, w_ref, own_ref, other_ref, gain_ref, bias_ref,
    part_ref, sent_ref, *refs,
):
    *outs, d_ref = refs
    grad = grad_ref[...]
    d = t_dot(normed_ref[...], grad)
    part = dot_t(grad, w_ref[...])
    count = own_ref.shape[0]
    part_ref[...] = part[:count]
    sent_ref[...] = part[count:].astype(BF16)
    d_gain = jnp.zeros((1, part.shape[1]), F32)
    for ref, rows in ((own_ref, part[:count]), (other_ref, part[count:])):
        x = ref[...].astype(F32)
        unit = x * lax.rsqrt(jnp.mean(x * x, axis=-1, keepdims=True) + epsilon)
        d_gain = d_gain + jnp.sum(rows * unit, axis=0, keepdims=True)
    main = N_FRONT - WIDE
    d_ref[:, :main] = d[:, :main].astype(BF16)
    rest = jnp.concatenate(
        [jnp.zeros((HALF, d_gain.shape[1]), F32), d_gain, gain_ref[:1]]
        + [jnp.zeros((WIDE - HALF - 2, d_gain.shape[1]), F32)],
        0,
    ).T
    d_ref[:, main:N_FRONT] = (d[:, main:] + rest + pltpu.roll(bias_ref[...], HALF + 2, 1)[:1]).astype(BF16)
    if len(outs) == 1:
        outs[0][...] = d_ref[...]
    else:
        own, over_dp, over_mid, first, second = outs
        rows = own.shape[1]
        for i in range(4):
            for ref, b in ((own, (0, 0)), (over_dp, (1, 0)), (over_mid, (0, 1))):
                ref[i] = d_ref[pl.ds(row_of(core_ref, i, b, rows), rows), :]
            far = first if i < 2 else second
            far[i % 2] = d_ref[pl.ds(row_of(core_ref, i, (1, 1), rows), rows), :]


def beside_each(refs):
    parts = [ref[...].reshape(-1, ref.shape[-1]) for ref in refs]
    return parts[0] if len(parts) == 1 else jnp.concatenate(parts, 1)


def far_kernel(core_ref, *refs):
    *far_refs, to_dp_ref, to_mid_ref = refs
    far = beside_each(far_refs)
    n = to_dp_ref.shape[0]
    to_dp_ref[...] = far[:n]
    to_mid_ref[...] = far[n:]


def sends_kernel(core_ref, *refs):
    *refs, over_dp_ref, over_mid_ref = refs
    n = len(refs) // 4
    to_mid, to_dp, over_dp, over_mid = [beside_each(refs[n * i : n * (i + 1)]) for i in range(4)]
    n = to_dp.shape[0]
    over_dp_ref[:n] = over_dp[:n]
    over_dp_ref[n:] = (over_dp[n:].astype(F32) + to_dp.astype(F32)).astype(BF16)
    over_mid_ref[:n] = (over_mid[:n].astype(F32) + to_mid.astype(F32)).astype(BF16)
    over_mid_ref[n:] = over_mid[n:]


def own_kernel(core_ref, dp_ref, mid_ref, *refs):
    *own_refs, sum_ref = refs
    whole = beside_each(own_refs).astype(F32) + beside_each([dp_ref]).astype(F32)
    whole = whole + beside_each([mid_ref]).astype(F32)
    sum_ref[...] = whole.astype(BF16).reshape(sum_ref.shape)


def sum_kernel(core_ref, own_ref, dp_ref, mid_ref, kept_ref, sent_ref):
    n = kept_ref.shape[0]
    whole = own_ref[...].astype(F32) + dp_ref[...].astype(F32) + mid_ref[...].astype(F32)
    kept_ref[...] = whole[:n]
    sent_ref[...] = whole[n:].astype(BF16)


def down_kernel(core_ref, hidden_ref, w_ref, out_ref):
    out_ref[...] = dot_t(hidden_ref[...], w_ref[...]).astype(BF16)


def output_kernel(core_ref, hidden_ref, w_ref, middle_ref, got_ref, out_ref):
    out = middle_ref[...] + dot_t(hidden_ref[...], w_ref[...])
    out_ref[...] = (out + got_ref[...].astype(F32)).astype(BF16)


def input_kernel(core_ref, part_ref, got_ref, middle_ref, x_ref, gains_ref, out_ref):
    x = x_ref[...].astype(F32)
    scale = inverse_rms(x)
    grad = (part_ref[...] + got_ref[...].astype(F32)) * gains_ref[:1]
    out_ref[...] = (middle_ref[...] + norm_back(grad, x * scale, scale)).astype(BF16)


def last_kernel(core_ref, pair_ref, got_ref, mine_ref, sent_ref):
    whole = (pair_ref[...] + got_ref[...].astype(F32)).astype(BF16)
    n = mine_ref.shape[0]
    low, high = whole[:n], whole[n:]
    mine_ref[...] = jnp.where(core_ref[0] == 0, low, high)
    sent_ref[...] = jnp.where(core_ref[0] == 0, high, low)


def unpack_kernel(
    core_ref, mine_ref, got_ref, q_ref, k_ref, v_ref, a_ref, gains_ref, bias_ref
):
    def both(ref, at):
        n = ref.shape[1] // 2
        a, b = mine_ref[:, at : at + n].astype(F32), got_ref[:, at : at + n].astype(F32)
        ref[:, :n] = jnp.where(core_ref[0] == 0, a, b)
        ref[:, n:] = jnp.where(core_ref[0] == 0, b, a)
        return at + n

    at = both(q_ref, 0)
    at = both(k_ref, at)
    at = both(v_ref, at)
    a = mine_ref[:, at:N_FRONT].astype(F32).T
    b = got_ref[:, at:N_FRONT].astype(F32).T
    low, high = jnp.where(core_ref[0] == 0, a, b), jnp.where(core_ref[0] == 0, b, a)
    a_ref[:HALF] = low[:HALF]
    a_ref[HALF:] = high[:HALF]
    gains_ref[...] = (a + b)[HALF : HALF + 8]
    bias_ref[:HALF] = low[HALF + 2 : 2 * HALF + 2]
    bias_ref[HALF:] = high[HALF + 2 : 2 * HALF + 2]


def call(kernel, ins, outs, name, microseconds, megabytes, steps=1, scratch=(), deps=(), reverse=False):
    once = pl.Buffered(1) if steps > 1 else None
    order = (lambda i, s: (1 - i) ^ s[0]) if reverse else (lambda i, s: i ^ s[0])

    def spec(kind, shape):
        zeros = (0,) * (len(shape) - 1)
        if kind == "all":
            return pl.BlockSpec(shape, lambda i, s: (0,) + zeros, pipeline_mode=once)
        if kind == "low":
            block = (shape[0] * 2 // steps,) + shape[1:]
            return pl.BlockSpec(block, lambda i, s: (jnp.minimum(i, steps // 2 - 1),) + zeros)
        if kind == "high":
            block = (shape[0] * 2 // steps,) + shape[1:]
            return pl.BlockSpec(block, lambda i, s: (jnp.maximum(i - steps // 2, 0),) + zeros)
        if kind in ("scalar", "any"):
            return SCALARS if kind == "scalar" else ANYWHERE
        if kind == "block":
            return pl.BlockSpec((shape[0] // 2,) + shape[1:], lambda i, s: (order(i, s),) + zeros)
        if kind == "rows":
            return pl.BlockSpec((shape[0] // steps,) + shape[1:], lambda i, s: (i,) + zeros)
        if kind == "entry":
            return pl.BlockSpec((None,) + shape[1:], lambda i, s: (order(i, s),) + zeros)
        if kind == "queries":
            return pl.BlockSpec((shape[0] // 2, N_Q), lambda i, s: (order(i, s), 0))
        if kind in ("own", "over_dp", "over_mid", "far"):
            a, b = int(kind in ("over_dp", "far")), int(kind in ("over_mid", "far"))
            block = (1, shape[1], 1) + shape[3:]
            return pl.BlockSpec(block, lambda i, s: (s[1] ^ a, 0, s[3] ^ b, 0, 0))
        block, index = kind
        return pl.BlockSpec(block, lambda i, s: index, pipeline_mode=once)

    where, *ins = ins
    moved = sum(v.size * v.dtype.itemsize for _, v in ins)
    return pl.pallas_call(
        without(kernel, 1 + len(ins), len(deps)),
        grid_spec=pltpu.PrefetchScalarGridSpec(
            num_scalar_prefetch=1,
            grid=(steps,),
            in_specs=[spec(kind, v.shape) for kind, v in ins] + [ANYWHERE] * len(deps),
            out_specs=[spec(kind, shape) for kind, shape, _ in outs],
            scratch_shapes=scratch,
        ),
        out_shape=[jax.ShapeDtypeStruct(shape, kind) for _, shape, kind in outs],
        compiler_params=pltpu.CompilerParams(
            dimension_semantics=("arbitrary",), vmem_limit_bytes=megabytes * 1024 * 1024
        ),
        cost_estimate=pl.CostEstimate(
            flops=int(microseconds * FLOPS), bytes_accessed=moved, transcendentals=0
        ),
        name=name,
    )(where, *[v for _, v in ins], *deps)


def piece(whole, a, b, low, count):
    sizes = (1, count, 1) + whole.shape[3:]
    return lax.dynamic_slice(whole, (a, low, b, 0, 0), sizes).reshape((count,) + whole.shape[3:])


def square_sends(over_dp, over_mid, to_mid, to_dp):
    half = to_mid.shape[0]
    send_mid = jnp.concatenate([over_mid[:half] + to_mid, over_mid[half:]], 0)
    send_dp = jnp.concatenate([over_dp[:half], over_dp[half:] + to_dp], 0)
    return send_dp, send_mid


def hi_swap(v, difference):
    return lax.ppermute(v, "hi", [(i, i ^ difference) for i in range(4)])


def sequence_weights(group_ids, loss_weights):
    group_count = loss_weights.shape[0]
    member = (group_ids[:, None] == jnp.arange(group_count, dtype=jnp.int32)[None, :]).astype(F32)
    counts = jnp.sum(member, axis=0)
    raw_weight = jnp.sum(member * loss_weights.astype(F32)[None, :], axis=1) / jnp.sum(
        member * counts[None, :], axis=1
    )
    return raw_weight * (group_ids.shape[0] / jnp.sum(raw_weight))


def shards(
    tokens,
    cotangent,
    group_ids,
    loss_weights,
    gain_one,
    w_query,
    w_key,
    w_value,
    w_gate,
    gate_bias,
    w_out,
    gain_two,
    w_gate_ff,
    w_up,
    w_down,
):
    count, width = tokens.shape
    both = 2 * count
    n_out, n_ff = w_out.shape[1] // 2, w_up.shape[1] // 2
    n_first = N_FRONT + n_out
    core, mid = lax.axis_index("core"), lax.axis_index("mid")
    dp, hi = lax.axis_index("dp"), lax.axis_index("hi")
    where = jnp.stack([core, dp, hi, mid]).astype(jnp.int32)
    small = small_slice()
    sequence = lax.axis_index(ALL) // SPAN
    square = (PAIRS, WIDE, WIDE)

    packed = pack(
        core, w_query, w_key, w_value, w_gate.T, gain_one[None], gain_two[None], w_out, w_gate_ff,
        w_up, w_down.T,
    )
    first = place(core, packed[0], swap(packed[2], "core"))
    rest = place(core, packed[1], swap(packed[3], "core"))
    w_rest = gather(rest)
    if small:
        pair = jnp.stack([first, hi_swap(first, 2)])
        own = jnp.concatenate([pair, hi_swap(pair, 1)], 0)
        over_dp, over_mid = swap(own, "dp"), swap(own, "mid")
        pieces = (own, over_dp, over_mid, swap(over_dp[:2], "mid"), swap(over_mid[2:], "dp"))
    else:
        pieces = (gather(first),)
    other_tokens, other_cotangent = swap(tokens, "core"), swap(cotangent, "core")

    block = 2 * mid + (core ^ jnp.arange(2))
    positions = (block[:, None] * count + jnp.arange(count)[None, :]).reshape(-1)
    frequency = ROPE_BASE ** (-jnp.arange(HEAD // 2, dtype=F32) / (HEAD // 2))
    angles = positions.astype(F32)[:, None] * frequency[None, :]
    cosine, sine_part = jnp.cos(angles), jnp.sin(angles)
    cosine = jnp.concatenate([cosine] * 4, 1)
    sine_part = jnp.concatenate([-sine_part, sine_part] * 2, 1)
    own_bias = lax.dynamic_slice_in_dim(gate_bias, core * HALF, HALF)
    own_bias = jnp.concatenate([own_bias, jnp.zeros((WIDE - HALF,), F32)])[None, :]
    w_front, w_half, normed_one, qkv, c, ct, z, gains, update, leaving = call(
        front_kernel,
        [where, ("all", tokens), ("all", other_tokens), ("all", own_bias)]
        + [("block", cosine), ("block", sine_part)]
        + [("all", v) for v in pieces],
        [("all", (width, N_FRONT), BF16), ("all", (width, n_out), BF16)]
        + [("block", (both, width), BF16), ("block", (both, 2 * N_Q), BF16)]
        + [("block", (both, WIDE), F32), ("entry", (2, HALF, count), F32)]
        + [("block", (both, WIDE), F32), ("all", (8, width), F32)]
        + [("all", square, F32), ("all", (PAIRS, HEAD, WIDE), BF16)],
        "front",
        14,
        24,
        2,
        [pltpu.VMEM(square, F32)],
    )
    state_0 = lax.ppermute(leaving, "mid", [(0, 1)])
    w_other = swap(w_half, "core")
    mixed_out, normed_own, normed_sent, state_1 = call(
        mix_kernel,
        [where, ("block", qkv), ("block", c), ("entry", ct), ("all", state_0), ("all", update)],
        [("block", (both, N_Q), F32)]
        + [("all", (count, N_Q), BF16)] * 2
        + [("all", square, F32)],
        "mix",
        11,
        16,
        2,
        [pltpu.VMEM(square, F32)],
    )
    normed_got = swap(normed_sent, "core")
    middle, normed_two_own = call(
        out_kernel,
        [where]
        + [("all", v) for v in (normed_own, normed_got, w_half, w_other, tokens, gains)],
        [("all", (count, width), F32), ("all", (count, width), BF16)],
        "out",
        4,
        16,
    )
    normed_two_other = swap(normed_two_own, "core")
    seq_weights = sequence_weights(group_ids, loss_weights)
    own_weight = jnp.sum(jnp.where(jnp.arange(group_ids.shape[0]) == sequence, seq_weights, 0.0))
    own_weight = own_weight.reshape(1)
    far = [("any", (width // 8, 2 * n_ff), BF16)] * 2 if small else []
    hidden, w_down_t, d_ff, d_down, part_kept, part_sent, *ff_sends = call(
        functools.partial(ff_kernel, small),
        [where, ("scalar", own_weight)]
        + [("all", v) for v in (normed_two_own, normed_two_other, cotangent, other_cotangent)]
        + [("any", w_rest)],
        [("any", (both, n_ff), BF16), ("any", (width, n_ff), BF16)]
        + [("any", (width, 2 * n_ff), BF16), ("any", (width, n_ff), BF16)]
        + [("all", (count, width), F32), ("all", (count, width), BF16)]
        + far,
        "ff",
        36,
        44,
        scratch=[pltpu.VMEM((width, 2 * n_ff), BF16), pltpu.VMEM((width, n_ff), BF16)]
        + [pltpu.VMEM((both, n_ff), BF16), pltpu.VMEM((both, 2 * n_ff), BF16)]
        + [pltpu.VMEM((both, width), BF16), pltpu.VMEM((width, 2 * n_ff), BF16)]
        + [pltpu.VMEM((width, n_ff), BF16)]
        + [pltpu.SemaphoreType.DMA((2,)), pltpu.SemaphoreType.DMA((8,))],
    )
    if small:
        d_ff = d_ff.reshape(2, 4, 2, -1, 2 * n_ff)
        ff_one = swap(ff_sends[0], "dp"), swap(ff_sends[1], "mid")
        down_hi = d_down.reshape(4, -1, n_ff)
        down_hi = lax.psum_scatter(down_hi, "hi", scatter_dimension=0, tiled=False)
        down_hi = down_hi.reshape(2, 1, 2, -1, n_ff)
    else:
        rest_sum = scatter(d_down)
        ff_one = []
    part_got = swap(part_sent, "core")
    down_rows = ((count, n_ff), (1, 0)), ((count, n_ff), (0, 0))
    (out_sent,) = call(
        down_kernel,
        [where, (down_rows[0], hidden), ("all", w_down_t)],
        [("all", (count, width), BF16)],
        "out_sent",
        5,
        16,
    )
    grad_middle, d_gain_two, grad_own, grad_sent, d_out_kept, d_out_sent = call(
        middle_kernel,
        [where, ("scalar", own_weight)]
        + [("all", v) for v in (part_kept, part_got, cotangent, middle, gains, w_half, w_other)]
        + [("all", v) for v in (normed_own, normed_got)],
        [("all", (count, width), F32), ("all", (8, width), F32)]
        + [("all", (count, N_Q), BF16)] * 2
        + [("all", (width, n_out), BF16)] * 2,
        "middle",
        8,
        24,
        deps=(out_sent,),
    )
    grad_got = swap(grad_sent, "core")
    d_out_got = swap(d_out_sent, "core")
    grad_mixed, through, entering = call(
        head_back_kernel,
        [where, ("all", grad_own), ("all", grad_got), ("block", mixed_out), ("queries", qkv)]
        + [("block", c)],
        [("block", (both, N_Q), BF16), ("all", square, F32), ("all", (PAIRS, HEAD, WIDE), BF16)],
        "head_back",
        8,
        16,
        2,
        [pltpu.VMEM(square, F32), pltpu.VMEM((PAIRS, 8, WIDE), F32)],
        deps=ff_one,
    )
    state_last = lax.ppermute(entering, "mid", [(1, 0)])
    d_out, *out_sends = call(
        out_sum_kernel,
        [where, ("all", d_out_kept), ("all", d_out_got)],
        [("all", (width, n_out), BF16)]
        + [("all", (width // 8, n_out), BF16)] * (2 if small else 0),
        "out_sum",
        2,
        16,
        deps=(entering,),
    )
    if small:
        d_out = d_out.reshape(2, 4, 2, -1, n_out)
        n_wide = 2 * n_ff + n_out
        out_one = swap(out_sends[0], "dp"), swap(out_sends[1], "mid")
    else:
        wide_sends = out_sends = [d_out]
        wide_sum = jnp.concatenate([scatter(d_ff), scatter(d_out)], 1)
    if small:
        wide_sends = call(
            sends_kernel,
            [where]
            + [("all", v) for pair in zip(ff_one, out_one) for v in pair]
            + [(kind, v) for kind in ("over_dp", "over_mid") for v in (d_ff, d_out)],
            [("all", (width // 4, n_wide), BF16)] * 2,
            "wide_sends",
            3.5,
            20,
            deps=(state_last,),
        )
        wide_got = swap(wide_sends[0], "dp"), swap(wide_sends[1], "mid")
    grad_front, d_bias = call(
        back_kernel,
        [where, ("block", qkv), ("block", c), ("entry", ct), ("block", z), ("block", grad_mixed)]
        + [("all", v) for v in (state_0, state_1, state_last, through)]
        + [("block", cosine), ("block", sine_part)],
        [("block", (both, N_FRONT), BF16), ("all", (8, WIDE), F32)],
        "back",
        20,
        16,
        2,
        [pltpu.VMEM(square, F32), pltpu.VMEM(square, F32)],
        deps=wide_sends,
        reverse=True,
    )
    if small:
        shapes = [(4, width // 16, N_FRONT)] * 3 + [(2, width // 16, N_FRONT)] * 2
    else:
        shapes = [(width, N_FRONT)]
    part_kept, part_sent, *d_first = call(
        front_back_kernel,
        [where]
        + [("all", v) for v in (normed_one, grad_front, w_front, tokens, other_tokens)]
        + [("all", v) for v in (d_gain_two, d_bias)],
        [("all", (count, width), F32), ("all", (count, width), BF16)]
        + [("all", shape, BF16) for shape in shapes],
        "front_back",
        12,
        20,
        scratch=[pltpu.VMEM((width, N_FRONT), BF16)],
    )
    part_got = swap(part_sent, "core")

    def add_input(deps):
        return call(
            input_kernel,
            [where]
            + [("all", v) for v in (part_kept, part_got, grad_middle, tokens, gains)],
            [("all", (count, width), BF16)],
            "grad_input",
            4.5,
            16,
            deps=deps,
        )

    out_got = swap(out_sent, "core")

    def add_output(deps):
        return call(
            output_kernel,
            [where, (down_rows[1], hidden), ("all", w_down_t)]
            + [("all", v) for v in (middle, out_got)],
            [("all", (count, width), BF16)],
            "output",
            5.5,
            16,
            deps=deps,
        )

    if small:
        own, over_dp, over_mid, far_0, far_1 = d_first
        one = swap(far_0, "dp"), swap(far_1, "mid")
        (wide_hi,) = call(
            own_kernel,
            [where] + [("all", v) for v in wide_got] + [("own", d_ff), ("own", d_out)],
            [("all", (4, width // 16, n_wide), BF16)],
            "wide_own",
            3.5,
            20,
            deps=(far_0,),
        )
        wide_sum = lax.psum_scatter(wide_hi, "hi", scatter_dimension=0, tiled=False)
        rest_sends = call(
            far_kernel,
            [where, ("far", down_hi)],
            [("all", (width // 32, n_ff), BF16)] * 2,
            "rest_far",
            1.5,
            16,
            deps=(wide_hi,),
        )
        rest_one = swap(rest_sends[0], "dp"), swap(rest_sends[1], "mid")
        sends = call(
            sends_kernel,
            [where] + [("all", v) for v in (*one, over_dp, over_mid)],
            [("all", (width // 4, N_FRONT), BF16)] * 2,
            "front_sends",
            2,
            16,
            deps=(wide_hi, *rest_sends),
        )
        front_got = swap(sends[0], "dp"), swap(sends[1], "mid")
        rest_sends = call(
            sends_kernel,
            [where]
            + [("all", v) for v in rest_one]
            + [("over_dp", down_hi), ("over_mid", down_hi)],
            [("all", (width // 16, n_ff), BF16)] * 2,
            "rest_sends",
            2,
            16,
            deps=(sends[0],),
        )
        rest_got = swap(rest_sends[0], "dp"), swap(rest_sends[1], "mid")
        (output,) = add_output((sends[0],))
        (grad_input,) = add_input((sends[0],))
        kept, sent = call(
            sum_kernel,
            [where] + [("all", v.reshape(own.shape)) for v in (own, *front_got)],
            [("all", (2,) + own.shape[1:], F32), ("all", (2,) + own.shape[1:], BF16)],
            "first_sum",
            2,
            16,
            deps=(grad_input, output, *rest_sends),
        )
        pair = kept + hi_swap(sent, 1).astype(F32)
        last, last_got = pair[0], hi_swap(pair[1].astype(BF16), 2)
        (rest_sum,) = call(
            own_kernel,
            [where] + [("all", v) for v in rest_got] + [("own", down_hi)],
            [("all", (width // 16, n_ff), BF16)],
            "rest_own",
            1.5,
            16,
            deps=(kept,),
        )
    else:
        last = scatter(d_first[0]).astype(F32)
        last_got = jnp.zeros_like(last, BF16)
        (output,), (grad_input,) = add_output(()), add_input(())

    def owned(rows):
        n = rows.shape[0] // 2
        mine = lax.dynamic_slice_in_dim(rows, core * n, n)
        return mine, swap(lax.dynamic_slice_in_dim(rows, (1 - core) * n, n), "core")

    outs = []
    for v in (rest_sum, wide_sum):
        mine, theirs = owned(v)
        outs.append((mine, theirs))
    n = last.shape[0] // 2
    mine, sent = call(
        last_kernel,
        [where, ("all", last), ("all", last_got)],
        [("all", (n, N_FRONT), BF16)] * 2,
        "last",
        1.5,
        16,
        deps=tuple(theirs for _, theirs in outs),
    )
    theirs = swap(sent, "core")
    ends = [(0, 0, n_ff), (1, 0, n_ff), (1, n_ff, 2 * n_ff), (1, 2 * n_ff, 2 * n_ff + n_out)]
    g_down, g_gate_ff, g_up, g_out = [
        beside(core, *[v[:, low:high] for v in outs[i]]) for i, low, high in ends
    ]
    g_query, g_key, g_value, g_gate, g_gains, g_bias = call(
        unpack_kernel,
        [where, ("all", mine), ("all", theirs)],
        [("all", (n, 2 * N_Q), F32)]
        + [("all", (n, 2 * N_K), F32)] * 2
        + [("all", (HEADS, n), F32), ("all", (8, n), F32), ("all", (HEADS, n), F32)],
        "unpack",
        1.5,
        16,
    )
    return (
        output,
        grad_input,
        g_gains[0],
        g_query,
        g_key,
        g_value,
        g_gate.T,
        g_bias[:, 0],
        g_out,
        g_gains[1],
        g_gate_ff,
        g_up,
        g_down.T,
    )


def solution(mesh):
    devices = mesh.devices
    fine = Mesh(
        devices.reshape(devices.shape[0], devices.shape[1] // SPAN, SPAN // 2, 2), ALL
    )
    rows, columns, split = P(ALL, None), P(None, ALL), P(ALL)
    in_specs = (rows, rows, P(), P(), split) + (rows,) * 4 + (P(), rows, split, rows, rows, columns)
    out_specs = (rows, rows, split) + (rows,) * 4 + (P(), rows, split, rows, rows, columns)
    return jax.shard_map(shards, mesh=fine, in_specs=in_specs, out_specs=out_specs, check_vma=False)
```
